32 devices in a mesh: row: 4 (over y, x), col: 8 (over z, core).
Axes of the slice: x: 2, y: 2, z: 4, core: 2. Of those that a mesh axis runs over, the one named last changes fastest.
Arguments:
- pixels: bfloat16 [384, 196, 768], P(('row', 'col')), may hold values from -6 to 6
- keep_idx: int32 [384, 49], P(('row', 'col')), may hold values from 0 to 195, as said below
- restore: int32 [384, 196], P(('row', 'col')), may hold values from 0 to 195
- enc_in: float32 [768, 7424], P('row', 'col'), may hold values from -0.21875 to 0.21875
- enc_fc2: float32 [3072, 768], P('row', 'col'), may hold values from -0.109375 to 0.109375
- dec_in: float32 [512, 4096], P('row', 'col'), may hold values from -0.25 to 0.25
- dec_fc2: float32 [2048, 512], P('row', 'col'), may hold values from -0.125 to 0.125
- head_w: float32 [512, 768], replicated, may hold values from -0.25 to 0.25
- small_vec: float32 [21248], replicated, as said below
- m_enc_in: float32 [768, 7424], P('row', 'col'), may hold values from -4.4703484e-08 to 4.4703484e-08
- m_enc_fc2: float32 [3072, 768], P('row', 'col'), may hold values from -4.4703484e-08 to 4.4703484e-08
- m_dec_in: float32 [512, 4096], P('row', 'col'), may hold values from -4.4703484e-08 to 4.4703484e-08
- m_dec_fc2: float32 [2048, 512], P('row', 'col'), may hold values from -4.4703484e-08 to 4.4703484e-08
- m_head: float32 [512, 768], replicated, may hold values from -4.4703484e-08 to 4.4703484e-08
- m_small: float32 [21248], replicated, may hold values from -4.4703484e-08 to 4.4703484e-08
- v_enc_in: float32 [768, 7424], P('row', 'col'), may hold values from 8.6050224e-19 to 3.442009e-18
- v_enc_fc2: float32 [3072, 768], P('row', 'col'), may hold values from 8.6050224e-19 to 3.442009e-18
- v_dec_in: float32 [512, 4096], P('row', 'col'), may hold values from 8.6050224e-19 to 3.442009e-18
- v_dec_fc2: float32 [2048, 512], P('row', 'col'), may hold values from 8.6050224e-19 to 3.442009e-18
- v_head: float32 [512, 768], replicated, may hold values from 8.6050224e-19 to 3.442009e-18
- v_small: float32 [21248], replicated, may hold values from 8.6050224e-19 to 3.442009e-18
Outputs:
- new_enc_in: float32 [768, 7424], P('row', 'col')
- new_enc_fc2: float32 [3072, 768], P('row', 'col')
- new_dec_in: float32 [512, 4096], P('row', 'col')
- new_dec_fc2: float32 [2048, 512], P('row', 'col')
- new_head: float32 [512, 768], replicated
- new_small: float32 [21248], replicated
- mo_enc_in: float32 [768, 7424], P('row', 'col')
- mo_enc_fc2: float32 [3072, 768], P('row', 'col')
- mo_dec_in: float32 [512, 4096], P('row', 'col')
- mo_dec_fc2: float32 [2048, 512], P('row', 'col')
- mo_head: float32 [512, 768], replicated
- mo_small: float32 [21248], replicated
- vo_enc_in: float32 [768, 7424], P('row', 'col')
- vo_enc_fc2: float32 [3072, 768], P('row', 'col')
- vo_dec_in: float32 [512, 4096], P('row', 'col')
- vo_dec_fc2: float32 [2048, 512], P('row', 'col')
- vo_head: float32 [512, 768], replicated
- vo_small: float32 [21248], replicated
- loss: float32 [], replicated
- grad_norm: float32 [], replicated
The draws below stay inside these ranges and needn't reach their ends.
Inputs may be any that keep to these rules, and one draw needn't show every extreme that they name: Each row of keep_idx holds 49 different patch numbers; restore is a permutation of each image's patches with restore[keep_idx[i]] = i, and restore >= 49 exactly on the patches that keep_idx leaves out. `small_vec`: gains near one and biases, class and mask tokens of order a third.
All inputs are finite; a program needn't handle non-finite values.
Results may differ from the reference program's by a relative error of at most 0.006.
Values may be sent and summed in bfloat16 or wider, within the bound.
A program may use at most 384 MiB of HBM per device.

```python
import math
import jax
import jax.numpy as jnp
from jax import lax

D = 768
HEADS = 12
FF = 3072
DD = 512
DHEADS = 16
DFF = 2048
PATCH_PIX = 768
GRID = 14
PATCHES = 196
KEEP = 49
IMG_MB = 6
STEP = 10
IMAGES = 384
SMALL = 21248
PARAMS = 11621120


def shuffle_rows(key):
    keys = jax.random.split(jax.random.fold_in(key, 7), IMAGES)
    return jax.vmap(lambda single: jax.random.permutation(single, PATCHES))(keys).astype(jnp.int32)


def draw_keep_idx(key, part):
    return shuffle_rows(key)[:, :KEEP]


def draw_restore(key, part):
    return jnp.argsort(shuffle_rows(key), axis=1, stable=True).astype(jnp.int32)


def draw_small_vec(key, part):
    lengths = [D, D, 2 * D, D, D, D, FF, D, D, D, D, D, DD, DD, DD, DD, 2 * DD, DD, DD, DD, DFF, DD, DD, DD, PATCH_PIX]
    gain_slots = [0, 4, 8, 14, 18, 22]
    flags = jnp.concatenate([jnp.full((piece_len,), 1.0 if place in gain_slots else 0.0, jnp.float32) for place, piece_len in enumerate(lengths)])
    noise = 0.3 * jax.random.normal(key, (SMALL,), jnp.float32)
    return flags + noise


def levels(key, dims, shards, smallest, largest):
    level = 1.0
    for axis_at, blocks in shards:
        steps = jax.random.uniform(jax.random.fold_in(jax.random.fold_in(key, 6), axis_at), (blocks,), jnp.float32, smallest / len(shards), largest / len(shards))
        level = level * jnp.repeat(jnp.exp(steps), dims[axis_at] // blocks).reshape((-1,) + (1,) * (len(dims) - 1 - axis_at))
    return level


def bell_draw(key, dims, spread, bound, cuts=(), dtype=jnp.bfloat16):
    drawn = jax.random.normal(key, dims, jnp.float32) * spread
    if len(cuts) > 0:
        drawn = levels(key, dims, cuts, -0.22, 0.18) * drawn
    return jnp.clip(drawn, min=-bound, max=bound).astype(dtype)


def setup_inputs(seed: int = 0) -> dict:
    seeds = jax.random.split(jax.random.key(seed), 22)
    pixels = bell_draw(seeds[0], (IMAGES, PATCHES, PATCH_PIX), 1.0, 6.0, ((0, 32),))
    keep_idx = draw_keep_idx(jax.random.fold_in(seeds[21], 71), 0)
    restore = draw_restore(jax.random.fold_in(seeds[21], 71), 0)
    enc_in = bell_draw(seeds[3], (D, 5 * D + FF + DD), D ** -0.5, 0.21875, ((0, 4), (1, 8)), jnp.float32)
    enc_fc2 = bell_draw(seeds[4], (FF, D), FF ** -0.5, 0.109375, ((0, 4), (1, 8)), jnp.float32)
    dec_in = bell_draw(seeds[5], (DD, 4 * DD + DFF), DD ** -0.5, 0.25, ((0, 4), (1, 8)), jnp.float32)
    dec_fc2 = bell_draw(seeds[6], (DFF, DD), DFF ** -0.5, 0.125, ((0, 4), (1, 8)), jnp.float32)
    head_w = bell_draw(seeds[7], (DD, PATCH_PIX), DD ** -0.5, 0.25, (), jnp.float32)
    small_vec = draw_small_vec(jax.random.fold_in(seeds[21], 71), 0)
    m_enc_in = bell_draw(seeds[9], (D, 5 * D + FF + DD), (0.111 * 0.0001 * PARAMS ** -0.5), 4.470348358154297e-08, ((0, 4), (1, 8)), jnp.float32)
    m_enc_fc2 = bell_draw(seeds[10], (FF, D), (0.111 * 0.0001 * PARAMS ** -0.5), 4.470348358154297e-08, ((0, 4), (1, 8)), jnp.float32)
    m_dec_in = bell_draw(seeds[11], (DD, 4 * DD + DFF), (0.111 * 0.0001 * PARAMS ** -0.5), 4.470348358154297e-08, ((0, 4), (1, 8)), jnp.float32)
    m_dec_fc2 = bell_draw(seeds[12], (DFF, DD), (0.111 * 0.0001 * PARAMS ** -0.5), 4.470348358154297e-08, ((0, 4), (1, 8)), jnp.float32)
    m_head = bell_draw(seeds[13], (DD, PATCH_PIX), (0.111 * 0.0001 * PARAMS ** -0.5), 4.470348358154297e-08, (), jnp.float32)
    m_small = bell_draw(seeds[14], (SMALL,), (0.111 * 0.0001 * PARAMS ** -0.5), 4.470348358154297e-08, (), jnp.float32)
    v_enc_in = jnp.clip(jnp.exp(math.log(3.442008957444924e-18) - 1.3862944 * jax.random.uniform(seeds[15], (D, 5 * D + FF + DD), jnp.float32) ** levels(seeds[15], (D, 5 * D + FF + DD), ((0, 4), (1, 8)), -0.2, 0.2)), 8.60502239361231e-19, 3.442008957444924e-18)
    v_enc_fc2 = jnp.clip(jnp.exp(math.log(3.442008957444924e-18) - 1.3862944 * jax.random.uniform(seeds[16], (FF, D), jnp.float32) ** levels(seeds[16], (FF, D), ((0, 4), (1, 8)), -0.2, 0.2)), 8.60502239361231e-19, 3.442008957444924e-18)
    v_dec_in = jnp.clip(jnp.exp(math.log(3.442008957444924e-18) - 1.3862944 * jax.random.uniform(seeds[17], (DD, 4 * DD + DFF), jnp.float32) ** levels(seeds[17], (DD, 4 * DD + DFF), ((0, 4), (1, 8)), -0.2, 0.2)), 8.60502239361231e-19, 3.442008957444924e-18)
    v_dec_fc2 = jnp.clip(jnp.exp(math.log(3.442008957444924e-18) - 1.3862944 * jax.random.uniform(seeds[18], (DFF, DD), jnp.float32) ** levels(seeds[18], (DFF, DD), ((0, 4), (1, 8)), -0.2, 0.2)), 8.60502239361231e-19, 3.442008957444924e-18)
    v_head = jnp.clip(jnp.exp(jax.random.uniform(seeds[19], (DD, PATCH_PIX), jnp.float32, math.log(8.60502239361231e-19), math.log(3.442008957444924e-18))), 8.60502239361231e-19, 3.442008957444924e-18)
    v_small = jnp.clip(jnp.exp(jax.random.uniform(seeds[20], (SMALL,), jnp.float32, math.log(8.60502239361231e-19), math.log(3.442008957444924e-18))), 8.60502239361231e-19, 3.442008957444924e-18)
    return {"pixels": pixels, "keep_idx": keep_idx, "restore": restore, "enc_in": enc_in, "enc_fc2": enc_fc2, "dec_in": dec_in, "dec_fc2": dec_fc2, "head_w": head_w, "small_vec": small_vec, "m_enc_in": m_enc_in, "m_enc_fc2": m_enc_fc2, "m_dec_in": m_dec_in, "m_dec_fc2": m_dec_fc2, "m_head": m_head, "m_small": m_small, "v_enc_in": v_enc_in, "v_enc_fc2": v_enc_fc2, "v_dec_in": v_dec_in, "v_dec_fc2": v_dec_fc2, "v_head": v_head, "v_small": v_small}


clip_limit = 0.0001
learn_rate = 0.08
beta_one = 0.9
beta_two = 0.999
adam_eps = 1e-08
decay_rate = 0.05

@jax.custom_vjp
def low(v):
    return lax.optimization_barrier(v.astype(jnp.bfloat16)).astype(jnp.float32)

@jax.custom_vjp
def low_back(v):
    return v

def low_keep(v):
    return (low(v), None)

def low_pass(kept, grad):
    return (grad,)

def back_keep(v):
    return (v, None)

def back_low(kept, grad):
    return (low(grad),)
low.defvjp(low_keep, low_pass)
low_back.defvjp(back_keep, back_low)

def small_parts(vector):
    lengths = [D, D, 2 * D, D, D, D, FF, D, D, D, D, D, DD, DD, DD, DD, 2 * DD, DD, DD, DD, DFF, DD, DD, DD, PATCH_PIX]
    pieces = []
    start = 0
    for piece_len in lengths:
        pieces.append(vector[start:start + piece_len])
        start += piece_len
    return pieces

def sincos_table(width):
    quarter = width // 4
    frequency = 1.0 / 10000.0 ** (jnp.arange(quarter).astype(jnp.float32) / quarter)
    positions = jnp.arange(GRID * GRID)
    col_part = (positions % GRID).astype(jnp.float32)[:, None] * frequency[None, :]
    row_part = (positions // GRID).astype(jnp.float32)[:, None] * frequency[None, :]
    return jnp.concatenate([jnp.sin(col_part), jnp.cos(col_part), jnp.sin(row_part), jnp.cos(row_part)], axis=1)

def layer_norm(values, gain, shift):
    centered = values - lax.optimization_barrier(jnp.mean(values, axis=-1, keepdims=True))
    scale = lax.rsqrt(lax.optimization_barrier(jnp.mean(centered * centered, axis=-1, keepdims=True)) + 1e-06)
    return centered * scale * gain + shift

def linear(values, weight, shift):
    product = jnp.einsum('...i,ij->...j', low(values), weight, precision=lax.Precision.HIGHEST)
    return low_back(product) + shift

def block(tokens, weights_in, weight_out, biases, heads):
    norm_one, shift_one, qv_bias, proj_bias, norm_two, shift_two, hidden_bias, out_bias = biases
    width = tokens.shape[-1]
    batch_n, seq_len = (tokens.shape[0], tokens.shape[1])
    normed = layer_norm(tokens, norm_one, shift_one)
    packed = jnp.einsum('nli,ij->nlj', low(normed), weights_in[:, :3 * width], precision=lax.Precision.HIGHEST)
    query = packed[..., :width] + qv_bias[:width]
    keyed = packed[..., width:2 * width]
    valued = packed[..., 2 * width:] + qv_bias[width:]

    def split_heads(part):
        return low_back(low(part)).reshape(batch_n, seq_len, heads, width // heads)
    raw = jnp.einsum('nqhd,nkhd->nhqk', split_heads(query), split_heads(keyed), precision=lax.Precision.HIGHEST)
    scores = low_back(raw) * (width // heads) ** (-0.5)
    probs = low_back(low(jax.nn.softmax(scores, axis=-1)))
    mixed = jnp.einsum('nhqk,nkhd->nqhd', probs, split_heads(valued), precision=lax.Precision.HIGHEST)
    mixed = low_back(mixed).reshape(batch_n, seq_len, width)
    tokens = tokens + linear(mixed, weights_in[:, 3 * width:4 * width], proj_bias)
    normed = layer_norm(tokens, norm_two, shift_two)
    hidden = jax.nn.gelu(linear(normed, weights_in[:, 4 * width:], hidden_bias), approximate=False)
    return tokens + linear(hidden, weight_out, out_bias)

def group_loss(enc_in, enc_fc2, dec_in, dec_fc2, head_w, small_vec, pixels, keep_idx, restore, denominator):
    enc_in, enc_fc2, dec_in, dec_fc2, head_w = (low(enc_in), low(enc_fc2), low(dec_in), low(dec_fc2), low(head_w))
    parts = small_parts(small_vec)
    images = pixels.astype(jnp.float32)
    batch_n = images.shape[0]
    kept = jnp.take_along_axis(images, keep_idx[:, :, None], axis=1)
    embed = linear(kept, enc_in[:, :D], parts[10]) + jnp.take(sincos_table(D), keep_idx, axis=0)
    cls_rows = jnp.broadcast_to(parts[11], (batch_n, 1, D))
    tokens = jnp.concatenate([cls_rows, embed], axis=1)
    tokens = block(tokens, enc_in[:, D:5 * D + FF], enc_fc2, parts[0:8], HEADS)
    tokens = layer_norm(tokens, parts[8], parts[9])
    decoded = linear(tokens, enc_in[:, 5 * D + FF:], parts[12])
    masked = restore >= KEEP
    picked = jnp.take_along_axis(decoded[:, 1:], jnp.minimum(restore, KEEP - 1)[:, :, None], axis=1)
    filled = jnp.where(masked[:, :, None], parts[13], picked) + sincos_table(DD)
    sequence = jnp.concatenate([decoded[:, :1], filled], axis=1)
    sequence = block(sequence, dec_in, dec_fc2, parts[14:22], DHEADS)
    sequence = layer_norm(sequence, parts[22], parts[23])
    predicted = linear(sequence[:, 1:], head_w, parts[24])
    centered = images - lax.optimization_barrier(jnp.mean(images, axis=-1, keepdims=True))
    target = centered * lax.rsqrt(lax.optimization_barrier(jnp.mean(centered * centered, axis=-1, keepdims=True)) + 1e-06)
    error = lax.optimization_barrier(jnp.mean((predicted - target) ** 2, axis=-1))
    return jnp.sum(jnp.where(masked, error, 0.0)) / denominator

def adamw(weight, first, second, grad):
    first = beta_one * first + (1.0 - beta_one) * grad
    second = beta_two * second + (1.0 - beta_two) * grad * grad
    first_hat = first / (1.0 - beta_one ** STEP)
    second_hat = second / (1.0 - beta_two ** STEP)
    weight = weight - learn_rate * (first_hat / (jnp.sqrt(second_hat) + adam_eps) + decay_rate * weight)
    return (weight, first, second)

def reference(pixels, keep_idx, restore, enc_in, enc_fc2, dec_in, dec_fc2, head_w, small_vec, m_enc_in, m_enc_fc2, m_dec_in, m_dec_fc2, m_head, m_small, v_enc_in, v_enc_fc2, v_dec_in, v_dec_fc2, v_head, v_small):
    weights = (enc_in, enc_fc2, dec_in, dec_fc2, head_w, small_vec)
    groups = IMAGES // IMG_MB
    denominator = 1.0 * IMAGES * (PATCHES - KEEP)

    def one_group(carry, batch):
        group_pix, group_keep, group_restore = batch

        def local_loss(*params):
            return group_loss(*params, group_pix, group_keep, group_restore, denominator)
        loss_value, pull = jax.vjp(local_loss, *weights)
        grads = pull(jnp.ones((), jnp.float32))
        return ((carry[0] + loss_value, tuple((a + b for a, b in zip(carry[1], grads)))), None)
    start = (jnp.zeros((), jnp.float32), tuple((jnp.zeros_like(weight) for weight in weights)))
    batches = (pixels.reshape(groups, IMG_MB, PATCHES, PATCH_PIX), keep_idx.reshape(groups, IMG_MB, KEEP), restore.reshape(groups, IMG_MB, PATCHES))
    (loss, grads), _ = lax.scan(one_group, start, batches)
    grad_norm = jnp.sqrt(sum((jnp.sum(grad * grad) for grad in grads)))
    factor = clip_limit / jnp.maximum(grad_norm, clip_limit)
    firsts = (m_enc_in, m_enc_fc2, m_dec_in, m_dec_fc2, m_head, m_small)
    seconds = (v_enc_in, v_enc_fc2, v_dec_in, v_dec_fc2, v_head, v_small)
    results = [adamw(w, m, v, g * factor) for w, m, v, g in zip(weights, firsts, seconds, grads)]
    return (results[0][0], results[1][0], results[2][0], results[3][0], results[4][0], results[5][0], results[0][1], results[1][1], results[2][1], results[3][1], results[4][1], results[5][1], results[0][2], results[1][2], results[2][2], results[3][2], results[4][2], results[5][2], loss, grad_norm)
```

```python
import functools
import math

import jax
import jax.numpy as jnp
import ml_dtypes
import numpy as np
from jax import lax
from jax.experimental import pallas as pl
from jax.experimental.pallas import tpu as pltpu
from jax.sharding import PartitionSpec as P

D = 768
HEADS = 12
FF = 3072
DD = 512
DHEADS = 16
DFF = 2048
PIX = 768
GRID = 14
PATCHES = 196
KEEP = 49
STEP = 10
SMALL = 21248
ES = 56
DS = 208
SEL = 80
NOROW = 255
f32 = jnp.float32
bf = jnp.bfloat16

LENS = [
    D, D, 2 * D, D, D, D, FF, D, D, D, D, D,
    DD, DD, DD, DD, 2 * DD, DD, DD, DD, DFF, DD, DD, DD, PIX,
]
OFF = [0]
for piece in LENS:
    OFF.append(OFF[-1] + piece)


def part(ref, i):
    return ref[:, OFF[i] : OFF[i + 1]]


def dg(a, b, ca, cb):
    return lax.dot_general(a, b, (((ca,), (cb,)), ((), ())), preferred_element_type=f32)


def nn(a, b):
    return dg(a, b, 1, 0)


def nt(a, b):
    return dg(a, b, 1, 1)


def rows(total, size, fn):
    @pl.loop(0, total // size)
    def _(i):
        fn(pl.ds(pl.multiple_of(i * size, size), size))


def cols(total, size, fn):
    @pl.loop(0, total // size)
    def _(i):
        fn(pl.multiple_of(i * size, size))


def pieces(x):
    hi = x.astype(bf)
    rest = x - hi.astype(f32)
    mid = rest.astype(bf)
    low = (rest - mid.astype(f32)).astype(bf)
    return hi, mid, low


def gelu_pair(x):
    ax = jnp.abs(x)
    d = 1.0 + (0.3275911 * 0.7071067811865476) * ax
    r = pl.reciprocal(d, approx=True)
    t = r * (2.0 - d * r)
    e = jnp.exp(-0.5 * (x * x))
    poly = ((((0.5 * 1.061405429 * t - 0.5 * 1.453152027) * t + 0.5 * 1.421413741) * t
             - 0.5 * 0.284496736) * t + 0.5 * 0.254829592) * t
    q = poly * e
    phi = jnp.where(x >= 0.0, 1.0 - q, q)
    return x * phi, phi + x * (e * 0.3989422804014327)


def norm_rows(x, gain, shift):
    c = x - jnp.mean(x, axis=1, keepdims=True)
    rs = lax.rsqrt(jnp.mean(c * c, axis=1, keepdims=True) + 1e-06)
    xh = c * rs
    return xh, rs, xh * gain + shift


def norm_back(da, xh, rs, gain):
    g = da * gain
    m1 = jnp.mean(g, axis=1, keepdims=True)
    m2 = jnp.mean(g * xh, axis=1, keepdims=True)
    return rs * (g - m1 - xh * m2)


def rsum(x):
    return jnp.sum(x, axis=0, keepdims=True)


def lanes_of(x, h, hd):
    lane = lax.broadcasted_iota(jnp.int32, (1, 128), 1)
    return jnp.where((lane >= h * hd) & (lane < (h + 1) * hd), x, jnp.zeros_like(x))


def att_fwd(qkv, o, p, bias, rsl, width, g, slot, hd):
    c0 = pl.multiple_of(g * 128, 128)
    q = qkv[rsl, pl.ds(c0, 128)]
    k = qkv[rsl, pl.ds(pl.multiple_of(c0 + width, 128), 128)]
    v = qkv[rsl, pl.ds(pl.multiple_of(c0 + 2 * width, 128), 128)]
    acc = None
    for h in range(128 // hd):
        s = nt(lanes_of(k, h, hd), q) * (hd ** -0.5) + bias
        e = jnp.exp(s - jnp.max(s, axis=0, keepdims=True))
        pr = (e * (1.0 / jnp.sum(e, axis=0, keepdims=True))).astype(bf)
        p[slot + h] = pr
        t = dg(pr, lanes_of(v, h, hd), 0, 0)
        acc = t if acc is None else acc + t
    o[rsl, pl.ds(c0, 128)] = acc.astype(bf)


def att_bwd(qkv, do, p, dqkv, rsl, width, g, slot, hd):
    c0 = pl.multiple_of(g * 128, 128)
    c1 = pl.multiple_of(c0 + width, 128)
    c2 = pl.multiple_of(c0 + 2 * width, 128)
    q = qkv[rsl, pl.ds(c0, 128)]
    k = qkv[rsl, pl.ds(c1, 128)]
    v = qkv[rsl, pl.ds(c2, 128)]
    d = do[rsl, pl.ds(c0, 128)]
    aq = ak = av = None
    for h in range(128 // hd):
        pr = p[slot + h]
        dp = nt(lanes_of(v, h, hd), d).astype(bf).astype(f32)
        pf = pr.astype(f32)
        t = pf * dp
        ds = ((t - pf * jnp.sum(t, axis=0, keepdims=True)) * (hd ** -0.5)).astype(bf)
        tv = nn(pr, lanes_of(d, h, hd))
        tk = nn(ds, lanes_of(q, h, hd))
        tq = dg(ds, lanes_of(k, h, hd), 0, 0)
        if h == 0:
            aq, ak, av = tq, tk, tv
        else:
            aq, ak, av = aq + tq, ak + tk, av + tv
    dqkv[rsl, pl.ds(c0, 128)] = aq.astype(bf)
    dqkv[rsl, pl.ds(c1, 128)] = ak.astype(bf)
    dqkv[rsl, pl.ds(c2, 128)] = av.astype(bf)


def dec_kernel(scale, nb, y, codec, coder, pix, pos, sv, win, wout, hw,
               dy, dwin, dwout, dhw, dsm, loss,
               x, t, xh1, xh2, xhf, rs1, rs2, rsf, tm, tr, a1, a2, u, o, qkv, p, hid, gp, dpr, d16, lacc):
    M = nb * DS
    R = 32
    W = DD

    @pl.when(pl.program_id(0) == 0)
    def _():
        dsm[...] = jnp.zeros_like(dsm)
        loss[...] = jnp.zeros_like(loss)
        lacc[...] = jnp.zeros_like(lacc)
        for ref in (dwin, dwout, dhw):
            rows(ref.shape[0], 16, lambda r: ref.__setitem__((r, slice(None)), jnp.zeros((16, ref.shape[1]), f32)))

    def gsum(i, v, lo=0, n=None):
        a = OFF[i] + lo
        n = LENS[i] if n is None else n
        dsm[:, pl.ds(a, n)] += rsum(v)

    for b in range(nb):
        pick = (codec[b] == lax.broadcasted_iota(jnp.int32, (DS, SEL), 1)).astype(f32).astype(bf)
        tok = jnp.where(lax.broadcasted_iota(jnp.int32, (8, W), 0) == 0, part(sv, 13), 0.0)
        table = jnp.concatenate([y[b], jnp.zeros((8, W), f32), tok, jnp.zeros((8, W), f32)], axis=0)
        z = pos[...]
        for piece in pieces(table):
            z = z + nn(pick, piece)
        x[b * DS : (b + 1) * DS, :] = z

    def ln1(r):
        xh, rs, a = norm_rows(x[r, :], part(sv, 14), part(sv, 15))
        xh1[r, :] = xh
        rs1[r, :] = rs
        a1[r, :] = a.astype(bf)
    rows(M, R, ln1)

    qkv[:, 0:W] = (nn(a1[...], win[:, 0:W]) + sv[:, OFF[16] : OFF[16] + W]).astype(bf)
    qkv[:, W : 2 * W] = nn(a1[...], win[:, W : 2 * W]).astype(bf)
    qkv[:, 2 * W :] = (nn(a1[...], win[:, 2 * W : 3 * W]) + sv[:, OFF[16] + W : OFF[17]]).astype(bf)

    bias = jnp.where(lax.broadcasted_iota(jnp.int32, (DS, 1), 0) <= PATCHES, 0.0, -1e30).astype(f32)

    @pl.loop(0, nb * 4)
    def _(i):
        rsl = pl.ds(pl.multiple_of((i // 4) * DS, 16), DS)
        att_fwd(qkv, o, p, bias, rsl, W, i % 4, i * 4, 32)

    x[...] += nn(o[...], win[:, 3 * W : 4 * W]) + part(sv, 17)

    def ln2(r):
        xh, rs, a = norm_rows(x[r, :], part(sv, 18), part(sv, 19))
        xh2[r, :] = xh
        rs2[r, :] = rs
        a2[r, :] = a.astype(bf)
    rows(M, R, ln2)

    def fc1(c):
        h = nn(a2[...], win[:, pl.ds(pl.multiple_of(4 * W + c, 256), 256)])
        g, dg_ = gelu_pair(h + sv[:, pl.ds(pl.multiple_of(OFF[20] + c, 128), 256)])
        hid[:, pl.ds(c, 256)] = g.astype(bf)
        gp[:, pl.ds(c, 256)] = dg_.astype(bf)
    cols(DFF, 256, fc1)

    x[...] += nt(hid[...], wout[...]) + part(sv, 21)

    def lnf(r):
        xh, rs, a = norm_rows(x[r, :], part(sv, 22), part(sv, 23))
        xhf[r, :] = xh
        rsf[r, :] = rs
        u[r, :] = a.astype(bf)
    rows(M, R, lnf)

    for b in range(nb):
        def tstat(r):
            v = pix[b, r, :].astype(f32)
            m = jnp.mean(v, axis=1, keepdims=True)
            c = v - m
            q = pl.ds(pl.multiple_of(b * DS + r.start, 16), 16)
            tm[q, :] = m
            tr[q, :] = lax.rsqrt(jnp.mean(c * c, axis=1, keepdims=True) + 1e-06)
        rows(DS, 16, tstat)

    def headc(c):
        hwc = hw[:, pl.ds(c, 256)].astype(bf)
        pr = nn(u[...], hwc) + sv[:, pl.ds(pl.multiple_of(OFF[24] + c, 128), 256)]
        for b in range(nb):
            sl = slice(b * DS, (b + 1) * DS)
            tgt = (pix[b, :, pl.ds(c, 256)].astype(f32) - tm[sl, :]) * tr[sl, :]
            diff = jnp.where(codec[b] == 64, pr[sl] - tgt, 0.0)
            lacc[:, 0:256] += rsum(diff * diff)
            dp = diff * (2.0 * scale / PIX)
            dsm[:, pl.ds(pl.multiple_of(OFF[24] + c, 128), 256)] += rsum(dp)
            dpr[sl, pl.ds(c, 256)] = dp.astype(bf)
    cols(PIX, 256, headc)

    def hgrad(c):
        dhw[:, pl.ds(c, 256)] += dg(u[...], dpr[:, pl.ds(c, 256)], 0, 0)
    cols(PIX, 256, hgrad)
    t[...] = nt(dpr[...], hw[...].astype(bf))

    def lnfb(r):
        da = t[r, :]
        xh = xhf[r, :]
        gsum(22, da * xh)
        gsum(23, da)
        dx = norm_back(da, xh, rsf[r, :], part(sv, 22))
        gsum(21, dx)
        x[r, :] = dx
        d16[r, :] = dx.astype(bf)
    rows(M, R, lnfb)

    def fc1b(c):
        cs = pl.ds(c, 256)
        dwout[:, cs] += dg(d16[...], hid[:, cs], 0, 0)
        dh = nn(d16[...], wout[:, cs]) * gp[:, cs].astype(f32)
        dsm[:, pl.ds(pl.multiple_of(OFF[20] + c, 128), 256)] += rsum(dh)
        dh16 = dh.astype(bf)
        gp[:, cs] = dh16
        wc = pl.ds(pl.multiple_of(4 * W + c, 256), 256)
        dwin[:, wc] += dg(a2[...], dh16, 0, 0)
    cols(DFF, 256, fc1b)
    t[...] = nt(gp[...], win[:, 4 * W :])

    def ln2b(r):
        da = t[r, :]
        xh = xh2[r, :]
        gsum(18, da * xh)
        gsum(19, da)
        dx = x[r, :] + norm_back(da, xh, rs2[r, :], part(sv, 18))
        gsum(17, dx)
        x[r, :] = dx
        d16[r, :] = dx.astype(bf)
    rows(M, R, ln2b)

    dwin[:, 3 * W : 4 * W] += dg(o[...], d16[...], 0, 0)
    o[...] = nt(d16[...], win[:, 3 * W : 4 * W]).astype(bf)
    dqkv = gp

    @pl.loop(0, nb * 4)
    def _(i):
        rsl = pl.ds(pl.multiple_of((i // 4) * DS, 16), DS)
        att_bwd(qkv, o, p, dqkv, rsl, W, i % 4, i * 4, 32)

    def wq(c):
        cs = pl.ds(c, 256)
        dwin[:, cs] += dg(a1[...], dqkv[:, cs], 0, 0)
    cols(3 * W, 256, wq)
    def qb(r):
        dsm[:, OFF[16] : OFF[16] + W] += rsum(dqkv[r, 0:W].astype(f32))
        dsm[:, OFF[16] + W : OFF[17]] += rsum(dqkv[r, 2 * W : 3 * W].astype(f32))
    rows(M, R, qb)
    t[...] = nt(dqkv[:, 0 : 3 * W], win[:, 0 : 3 * W])

    def ln1b(r):
        da = t[r, :]
        xh = xh1[r, :]
        gsum(14, da * xh)
        gsum(15, da)
        x[r, :] = x[r, :] + norm_back(da, xh, rs1[r, :], part(sv, 14))
    rows(M, R, ln1b)

    for b in range(nb):
        pick = (coder[b] == lax.broadcasted_iota(jnp.int32, (SEL, DS), 0)).astype(f32).astype(bf)
        out = None
        for piece in pieces(x[b * DS : (b + 1) * DS, :]):
            v = nn(pick, piece)
            out = v if out is None else out + v
        dy[b] = out[0:ES]
        dsm[:, OFF[13] : OFF[14]] += out[64:65]

    @pl.when(pl.program_id(0) == pl.num_programs(0) - 1)
    def _():
        loss[...] = jnp.broadcast_to(jnp.sum(lacc[...], axis=1, keepdims=True) * (scale / PIX), (1, 128))


def decoder(y, codec, coder, pix, pos, sv, win, wout, hw, scale, nb=2):
    n = y.shape[0]
    M = nb * DS
    whole = lambda a: pl.BlockSpec(a.shape, lambda i: (0,) * a.ndim, pipeline_mode=pl.Buffered(1))
    fixed = lambda s: pl.BlockSpec(s, lambda i: (0,) * len(s), pipeline_mode=pl.Buffered(1))
    blk = lambda s: pl.BlockSpec((nb,) + s, lambda i: (i, 0, 0))
    V = pltpu.VMEM
    return pl.pallas_call(
        functools.partial(dec_kernel, scale, nb),
        grid=(n // nb,),
        in_specs=[blk((ES, DD)), blk((DS, 1)), blk((1, DS)), blk((DS, PIX)), whole(pos), whole(sv), whole(win), whole(wout), whole(hw)],
        out_specs=[blk((ES, DD)), fixed(win.shape), fixed(wout.shape), fixed(hw.shape), fixed((1, SMALL)), fixed((1, 128))],
        out_shape=[
            jax.ShapeDtypeStruct((n, ES, DD), f32), jax.ShapeDtypeStruct(win.shape, f32),
            jax.ShapeDtypeStruct(wout.shape, f32), jax.ShapeDtypeStruct(hw.shape, f32),
            jax.ShapeDtypeStruct((1, SMALL), f32), jax.ShapeDtypeStruct((1, 128), f32)],
        scratch_shapes=[
            V((M, DD), f32), V((M, DD), f32), V((M, DD), f32), V((M, DD), f32), V((M, DD), f32),
            V((M, 1), f32), V((M, 1), f32), V((M, 1), f32), V((M, 1), f32), V((M, 1), f32),
            V((M, DD), bf), V((M, DD), bf), V((M, DD), bf), V((M, DD), bf), V((M, 3 * DD), bf),
            V((nb * DHEADS, DS, DS), bf), V((M, DFF), bf), V((M, DFF), bf), V((M, PIX), bf), V((M, DD), bf),
            V((1, 256), f32)],
        compiler_params=pltpu.CompilerParams(vmem_limit_bytes=60 << 20),
        name="decoder",
    )(y, codec, coder, pix, pos, sv, win, wout, hw)


EG = 4 * ES
O_Q, O_P, O_F, O_E = D, 4 * D, 5 * D, 5 * D + FF


def enc_fwd_kernel(pix, keepc, pos3, sv, win, wout,
                   y, kept, xh1, xh2, xhf, rs1, rs2, rsf, a1, a2, e16, o, qkv, p, hid, gp, x, bias):
    n = pix.shape[0]
    M = n * ES
    R = 32
    W = D
    for i in range(0, n, 2):
        two = []
        for b in (i, i + 1):
            kc = keepc[b * ES : (b + 1) * ES, :]
            pick = (kc == lax.broadcasted_iota(jnp.int32, (ES, DS), 1)).astype(f32).astype(bf)
            two.append(nn(pick, pix[b]))
        kept[i * ES : (i + 2) * ES, :] = jnp.concatenate(two, axis=0).astype(bf)
    for lo in range(0, M, EG):
        sl = slice(lo, lo + EG)
        kc = keepc[sl, :]
        pick = (kc == lax.broadcasted_iota(jnp.int32, (EG, DS), 1)).astype(f32).astype(bf)
        v = nn(kept[sl, :], win[:, 0:W]) + part(sv, 10)
        v = v + nn(pick, pos3[0:DS, :]) + nn(pick, pos3[DS : 2 * DS, :]) + nn(pick, pos3[2 * DS :, :])
        x[sl, :] = jnp.where(kc < PATCHES, v, jnp.where(kc == NOROW - 1, part(sv, 11), 0.0))

    def ln1(r):
        xh, rs, a = norm_rows(x[r, :], part(sv, 0), part(sv, 1))
        xh1[r, :] = xh
        rs1[r, :] = rs
        a1[r, :] = a.astype(bf)
    rows(M, R, ln1)
    qkv[:, 0:W] = (nn(a1[...], win[:, O_Q : O_Q + W]) + sv[:, OFF[2] : OFF[2] + W]).astype(bf)
    qkv[:, W : 2 * W] = nn(a1[...], win[:, O_Q + W : O_Q + 2 * W]).astype(bf)
    qkv[:, 2 * W :] = (nn(a1[...], win[:, O_Q + 2 * W : O_P]) + sv[:, OFF[2] + W : OFF[3]]).astype(bf)

    ki = lax.broadcasted_iota(jnp.int32, (EG, EG), 0)
    qi = lax.broadcasted_iota(jnp.int32, (EG, EG), 1)
    same = jnp.zeros((EG, EG), jnp.bool_)
    for j in range(4):
        same = same | ((ki >= j * ES) & (ki < j * ES + KEEP + 1) & (qi >= j * ES) & (qi < (j + 1) * ES))
    bias[...] = jnp.where(same, 0.0, -1e30).astype(f32)

    @pl.loop(0, (n // 4) * 6)
    def _(i):
        rsl = pl.ds(pl.multiple_of((i // 6) * EG, 16), EG)
        att_fwd(qkv, o, p, bias[...], rsl, W, i % 6, i * 2, 64)

    x[...] += nn(o[...], win[:, O_P : O_P + W]) + part(sv, 3)

    def ln2(r):
        xh, rs, a = norm_rows(x[r, :], part(sv, 4), part(sv, 5))
        xh2[r, :] = xh
        rs2[r, :] = rs
        a2[r, :] = a.astype(bf)
    rows(M, R, ln2)

    def fc1(c):
        h = nn(a2[...], win[:, pl.ds(pl.multiple_of(O_F + c, 256), 256)])
        g, dg_ = gelu_pair(h + sv[:, pl.ds(pl.multiple_of(OFF[6] + c, 128), 256)])
        hid[:, pl.ds(c, 256)] = g.astype(bf)
        gp[:, pl.ds(c, 256)] = dg_.astype(bf)
    cols(FF, 256, fc1)
    x[...] += nt(hid[...], wout[...]) + part(sv, 7)

    def lnf(r):
        xh, rs, a = norm_rows(x[r, :], part(sv, 8), part(sv, 9))
        xhf[r, :] = xh
        rsf[r, :] = rs
        e16[r, :] = a.astype(bf)
    rows(M, R, lnf)
    y[...] = nn(e16[...], win[:, O_E:]) + part(sv, 12)


def vspec(k):
    return [pl.BlockSpec(memory_space=pltpu.VMEM)] * k


def encoder_fwd(pix, keepc, pos3, sv, win, wout):
    n = pix.shape[0]
    M = n * ES
    S = jax.ShapeDtypeStruct
    V = pltpu.VMEM
    outs = [S((M, DD), f32), S((M, D), bf), S((M, D), f32), S((M, D), f32), S((M, D), f32),
            S((M, 1), f32), S((M, 1), f32), S((M, 1), f32), S((M, D), bf), S((M, D), bf), S((M, D), bf), S((M, D), bf),
            S((M, 3 * D), bf), S((n // 4 * HEADS, EG, EG), bf), S((M, FF), bf), S((M, FF), bf)]
    return pl.pallas_call(
        enc_fwd_kernel,
        in_specs=vspec(6), out_specs=vspec(len(outs)), out_shape=outs,
        scratch_shapes=[V((M, D), f32), V((EG, EG), f32)],
        compiler_params=pltpu.CompilerParams(vmem_limit_bytes=60 << 20),
        name="encoder_fwd",
    )(pix, keepc, pos3, sv, win, wout)


def enc_bwd_kernel(dy, keepc, sv, win, wout, kept, xh1, xh2, xhf, rs1, rs2, rsf, a1, a2, e16, o, qkv, p, hid, gp,
                   dwin, dwout, dsm, x, t, d16, dqkv, stage, sem):
    M = dy.shape[0]
    R = 32
    W = D
    CW = 256
    dsm[...] = jnp.zeros_like(dsm)

    def gsum(i, v, lo=0, n=None):
        a = OFF[i] + lo
        n = LENS[i] if n is None else n
        dsm[:, pl.ds(a, n)] += rsum(v)

    def put(out, count, base, value):
        def copy(i, slot):
            return pltpu.make_async_copy(stage.at[slot], out.at[:, pl.ds(pl.multiple_of(base + i * CW, 128), CW)], sem.at[slot])

        @pl.loop(0, count)
        def _(i):
            slot = lax.rem(i, 2)

            @pl.when(i >= 2)
            def _():
                copy(i - 2, slot).wait()
            stage[slot] = value(pl.multiple_of(i * CW, CW)).astype(bf)
            copy(i, slot).start()
        for i in range(max(count - 2, 0), count):
            copy(i, i % 2).wait()

    def emb(r):
        v = dy[r, :]
        gsum(12, v)
        d16[r, 0:DD] = v.astype(bf)
    rows(M, R, emb)
    put(dwin, DD // CW, O_E, lambda c: dg(e16[...], d16[:, pl.ds(c, CW)], 0, 0))
    t[...] = nt(d16[:, 0:DD], win[:, O_E:])

    def lnfb(r):
        da = t[r, :]
        xh = xhf[r, :]
        gsum(8, da * xh)
        gsum(9, da)
        dx = norm_back(da, xh, rsf[r, :], part(sv, 8))
        gsum(7, dx)
        x[r, :] = dx
        d16[r, :] = dx.astype(bf)
    rows(M, R, lnfb)
    put(dwout, FF // CW, 0, lambda c: dg(d16[...], hid[:, pl.ds(c, CW)], 0, 0))

    def fc1b(c):
        cs = pl.ds(c, CW)
        dh = nn(d16[...], wout[:, cs]) * gp[:, cs].astype(f32)
        dsm[:, pl.ds(pl.multiple_of(OFF[6] + c, 128), CW)] += rsum(dh)
        gp[:, cs] = dh.astype(bf)
        return dg(a2[...], gp[:, cs], 0, 0)
    put(dwin, FF // CW, O_F, fc1b)
    t[...] = nt(gp[...], win[:, O_F:O_E])

    def ln2b(r):
        da = t[r, :]
        xh = xh2[r, :]
        gsum(4, da * xh)
        gsum(5, da)
        dx = x[r, :] + norm_back(da, xh, rs2[r, :], part(sv, 4))
        gsum(3, dx)
        x[r, :] = dx
        d16[r, :] = dx.astype(bf)
    rows(M, R, ln2b)
    put(dwin, D // CW, O_P, lambda c: dg(o[...], d16[:, pl.ds(c, CW)], 0, 0))
    d16[...] = nt(d16[...], win[:, O_P:O_F]).astype(bf)

    @pl.loop(0, (M // EG) * 6)
    def _(i):
        rsl = pl.ds(pl.multiple_of((i // 6) * EG, 16), EG)
        att_bwd(qkv, d16, p, dqkv, rsl, W, i % 6, i * 2, 64)

    put(dwin, 3 * D // CW, O_Q, lambda c: dg(a1[...], dqkv[:, pl.ds(c, CW)], 0, 0))
    def qb(r):
        dsm[:, OFF[2] : OFF[2] + W] += rsum(dqkv[r, 0:W].astype(f32))
        dsm[:, OFF[2] + W : OFF[3]] += rsum(dqkv[r, 2 * W : 3 * W].astype(f32))
    rows(M, R, qb)
    t[...] = nt(dqkv[...], win[:, O_Q:O_P])

    def ln1b(r):
        da = t[r, :]
        xh = xh1[r, :]
        gsum(0, da * xh)
        gsum(1, da)
        dx = x[r, :] + norm_back(da, xh, rs1[r, :], part(sv, 0))
        kc = keepc[r, :]
        gsum(11, jnp.where(kc == NOROW - 1, dx, 0.0))
        dx = jnp.where(kc < PATCHES, dx, 0.0)
        gsum(10, dx)
        d16[r, :] = dx.astype(bf)
    rows(M, R, ln1b)
    put(dwin, D // CW, 0, lambda c: dg(kept[...], d16[:, pl.ds(c, CW)], 0, 0))


def encoder_bwd(dy, keepc, sv, win, wout, saved):
    M = dy.shape[0]
    S = jax.ShapeDtypeStruct
    V = pltpu.VMEM
    anyspec = pl.BlockSpec(memory_space=pl.ANY)
    return pl.pallas_call(
        enc_bwd_kernel,
        in_specs=vspec(5 + len(saved)),
        out_specs=[anyspec, anyspec, pl.BlockSpec(memory_space=pltpu.VMEM)],
        out_shape=[S(win.shape, bf), S(wout.shape, bf), S((1, SMALL), f32)],
        scratch_shapes=[V((M, D), f32), V((M, D), f32), V((M, D), bf), V((M, 3 * D), bf), V((2, D, 256), bf),
                        pltpu.SemaphoreType.DMA((2,))],
        compiler_params=pltpu.CompilerParams(vmem_limit_bytes=62 << 20),
        name="encoder_bwd",
    )(dy, keepc, sv, win, wout, *saved)


def sincos_np(width):
    quarter = width // 4
    freq = (1.0 / np.float32(10000.0) ** (np.arange(quarter, dtype=np.float32) / np.float32(quarter))).astype(np.float32)
    pos = np.arange(GRID * GRID)
    cp = (pos % GRID).astype(np.float32)[:, None] * freq[None, :]
    rp = (pos // GRID).astype(np.float32)[:, None] * freq[None, :]
    return np.concatenate([np.sin(cp), np.cos(cp), np.sin(rp), np.cos(rp)], axis=1).astype(np.float32)


def tables():
    dec = np.zeros((DS, DD), np.float32)
    dec[:PATCHES] = sincos_np(DD)
    enc = np.zeros((DS, D), np.float32)
    enc[:PATCHES] = sincos_np(D)
    b = ml_dtypes.bfloat16
    hi = enc.astype(b)
    mid = (enc - hi.astype(np.float32)).astype(b)
    lo = (enc - hi.astype(np.float32) - mid.astype(np.float32)).astype(b)
    return dec, np.concatenate([hi, mid, lo], axis=0)


def step(pixels, keep, restore, A, BT, C, DT, hw, small, denom):
    n = pixels.shape[0]
    dec_pos, enc_pos = tables()
    pix = jnp.pad(pixels, ((0, 0), (0, DS - PATCHES), (0, 0)))
    keepc = jnp.concatenate([keep, jnp.full((n, 1), NOROW - 1, jnp.int32), jnp.full((n, ES - KEEP - 1), NOROW, jnp.int32)], axis=1).reshape(n * ES, 1)
    code = jnp.concatenate([jnp.where(restore < KEEP, restore, 64), jnp.full((n, 1), KEEP, jnp.int32), jnp.full((n, DS - PATCHES - 1), NOROW, jnp.int32)], axis=1)
    sv = small.reshape(1, SMALL)
    fw = encoder_fwd(pix, keepc, jnp.asarray(enc_pos), sv, A, BT)
    y, saved = fw[0], fw[1:]
    dy, dC, dDT, dhw, dsm_d, loss = decoder(y.reshape(n, ES, DD), code.reshape(n, DS, 1), code.reshape(n, 1, DS), pix, jnp.asarray(dec_pos), sv, C, DT, hw, 1.0 / denom)
    dA, dBT, dsm_e = encoder_bwd(dy.reshape(n * ES, DD), keepc, sv, A, BT, saved)
    return dA, dBT, dC, dDT, dhw, (dsm_d + dsm_e).reshape(SMALL), loss[0, 0]


def adamw(weight, first, second, grad):
    first = 0.9 * first + (1.0 - 0.9) * grad
    second = 0.999 * second + (1.0 - 0.999) * grad * grad
    first_hat = first / (1.0 - 0.9**STEP)
    second_hat = second / (1.0 - 0.999**STEP)
    weight = weight - 0.08 * (first_hat / (jnp.sqrt(second_hat) + 1e-08) + 0.05 * weight)
    return (weight, first, second)


def local(pixels, keep_idx, restore, *state):
    weights, firsts, seconds = state[0:6], state[6:12], state[12:18]
    devices = lax.axis_size("row") * lax.axis_size("col")
    denom = 1.0 * pixels.shape[0] * devices * (PATCHES - KEEP)

    def gather(v, flip):
        v = v.astype(bf)
        v = lax.all_gather(v, "row", axis=0, tiled=True)
        v = lax.all_gather(v, "col", axis=1, tiled=True)
        return v.T if flip else v

    A, BT, C, DT = (gather(w, f) for w, f in zip(weights[0:4], (False, True, False, True)))
    dA, dBT, dC, dDT, dhw, dsm, loss = step(pixels, keep_idx, restore, A, BT, C, DT, weights[4], weights[5], denom)

    def scatter(v, flip):
        v = v.astype(bf)
        v = v.T if flip else v
        v = lax.psum_scatter(v, "col", scatter_dimension=1, tiled=True)
        return lax.psum_scatter(v, "row", scatter_dimension=0, tiled=True).astype(f32)

    grads = [scatter(g, f) for g, f in zip((dA, dBT, dC, dDT), (False, True, False, True))]
    squares = sum(jnp.sum(g * g) for g in grads)
    dhw, dsm, loss, squares = lax.psum((dhw, dsm, loss, squares), ("row", "col"))
    grads += [dhw, dsm]
    norm = jnp.sqrt(squares + jnp.sum(dhw * dhw) + jnp.sum(dsm * dsm))
    factor = 0.0001 / jnp.maximum(norm, 0.0001)
    done = [adamw(w, m, v, g * factor) for w, m, v, g in zip(weights, firsts, seconds, grads)]
    return tuple(d[0] for d in done) + tuple(d[1] for d in done) + tuple(d[2] for d in done) + (loss, norm)


def solution(mesh):
    both = P(("row", "col"))
    big = [P("row", "col")] * 4 + [P()] * 2
    return jax.shard_map(
        local,
        mesh=mesh,
        in_specs=(both, both, both, *big, *big, *big),
        out_specs=(*big, *big, *big, P(), P()),
        check_vma=False,
    )
```

```python
import functools
import math

import jax
import jax.numpy as jnp
import ml_dtypes
import numpy as np
from jax import lax
from jax.experimental import pallas as pl
from jax.experimental.pallas import tpu as pltpu
from jax.sharding import PartitionSpec as P

D = 768
HEADS = 12
FF = 3072
DD = 512
DHEADS = 16
DFF = 2048
PIX = 768
GRID = 14
PATCHES = 196
KEEP = 49
STEP = 10
SMALL = 21248
ES = 56
DS = 208
SEL = 80
NOROW = 255
f32 = jnp.float32
bf = jnp.bfloat16

LENS = [
    D, D, 2 * D, D, D, D, FF, D, D, D, D, D,
    DD, DD, DD, DD, 2 * DD, DD, DD, DD, DFF, DD, DD, DD, PIX,
]
OFF = [0]
for piece in LENS:
    OFF.append(OFF[-1] + piece)


def part(ref, i):
    return ref[:, OFF[i] : OFF[i + 1]]


def dg(a, b, ca, cb):
    return lax.dot_general(a, b, (((ca,), (cb,)), ((), ())), preferred_element_type=f32)


def nn(a, b):
    return dg(a, b, 1, 0)


def nt(a, b):
    return dg(a, b, 1, 1)


def rows(total, size, fn):
    @pl.loop(0, total // size)
    def _(i):
        fn(pl.ds(pl.multiple_of(i * size, size), size))


def cols(total, size, fn):
    @pl.loop(0, total // size)
    def _(i):
        fn(pl.multiple_of(i * size, size))


def pieces(x):
    hi = x.astype(bf)
    rest = x - hi.astype(f32)
    mid = rest.astype(bf)
    low = (rest - mid.astype(f32)).astype(bf)
    return hi, mid, low


def gelu_pair(x):
    ax = jnp.abs(x)
    d = 1.0 + (0.3275911 * 0.7071067811865476) * ax
    r = pl.reciprocal(d, approx=True)
    t = r * (2.0 - d * r)
    e = jnp.exp(-0.5 * (x * x))
    poly = ((((0.5 * 1.061405429 * t - 0.5 * 1.453152027) * t + 0.5 * 1.421413741) * t
             - 0.5 * 0.284496736) * t + 0.5 * 0.254829592) * t
    q = poly * e
    phi = jnp.where(x >= 0.0, 1.0 - q, q)
    return x * phi, phi + x * (e * 0.3989422804014327)


def norm_rows(x, gain, shift):
    c = x - jnp.mean(x, axis=1, keepdims=True)
    rs = lax.rsqrt(jnp.mean(c * c, axis=1, keepdims=True) + 1e-06)
    xh = c * rs
    return xh, rs, xh * gain + shift


def norm_back(da, xh, rs, gain):
    g = da * gain
    m1 = jnp.mean(g, axis=1, keepdims=True)
    m2 = jnp.mean(g * xh, axis=1, keepdims=True)
    return rs * (g - m1 - xh * m2)


def rsum(x):
    return jnp.sum(x, axis=0, keepdims=True)


def lanes_of(x, h, hd):
    lane = lax.broadcasted_iota(jnp.int32, (1, 128), 1)
    return jnp.where((lane >= h * hd) & (lane < (h + 1) * hd), x, jnp.zeros_like(x))


def att_fwd(qkv, o, p, bias, rsl, width, g, slot, hd):
    c0 = pl.multiple_of(g * 128, 128)
    q = qkv[rsl, pl.ds(c0, 128)]
    k = qkv[rsl, pl.ds(pl.multiple_of(c0 + width, 128), 128)]
    v = qkv[rsl, pl.ds(pl.multiple_of(c0 + 2 * width, 128), 128)]
    acc = None
    for h in range(128 // hd):
        s = nt(lanes_of(k, h, hd), q) * (hd ** -0.5) + bias
        e = jnp.exp(s - jnp.max(s, axis=0, keepdims=True))
        pr = (e * (1.0 / jnp.sum(e, axis=0, keepdims=True))).astype(bf)
        p[slot + h] = pr
        t = dg(pr, lanes_of(v, h, hd), 0, 0)
        acc = t if acc is None else acc + t
    o[rsl, pl.ds(c0, 128)] = acc.astype(bf)


def att_bwd(qkv, do, p, dqkv, rsl, width, g, slot, hd):
    c0 = pl.multiple_of(g * 128, 128)
    c1 = pl.multiple_of(c0 + width, 128)
    c2 = pl.multiple_of(c0 + 2 * width, 128)
    q = qkv[rsl, pl.ds(c0, 128)]
    k = qkv[rsl, pl.ds(c1, 128)]
    v = qkv[rsl, pl.ds(c2, 128)]
    d = do[rsl, pl.ds(c0, 128)]
    aq = ak = av = None
    for h in range(128 // hd):
        pr = p[slot + h]
        dp = nt(lanes_of(v, h, hd), d).astype(bf).astype(f32)
        pf = pr.astype(f32)
        t = pf * dp
        ds = ((t - pf * jnp.sum(t, axis=0, keepdims=True)) * (hd ** -0.5)).astype(bf)
        tv = nn(pr, lanes_of(d, h, hd))
        tk = nn(ds, lanes_of(q, h, hd))
        tq = dg(ds, lanes_of(k, h, hd), 0, 0)
        if h == 0:
            aq, ak, av = tq, tk, tv
        else:
            aq, ak, av = aq + tq, ak + tk, av + tv
    dqkv[rsl, pl.ds(c0, 128)] = aq.astype(bf)
    dqkv[rsl, pl.ds(c1, 128)] = ak.astype(bf)
    dqkv[rsl, pl.ds(c2, 128)] = av.astype(bf)


def dec_kernel(scale, nb, y, codec, coder, pix, pos, sv, win, wout, hw,
               dy, win_out, wout_out, dhw, dsm, loss,
               dwin, dwout, x, t, xh1, xh2, xhf, rs1, rs2, rsf, tm, tr, a1, a2, u, o, qkv, p, hid, gp, dpr, d16, lacc):
    M = nb * DS
    R = 32
    W = DD

    @pl.when(pl.program_id(0) == 0)
    def _():
        dsm[...] = jnp.zeros_like(dsm)
        loss[...] = jnp.zeros_like(loss)
        lacc[...] = jnp.zeros_like(lacc)
        for ref in (dwin, dwout, dhw):
            rows(ref.shape[0], 16, lambda r: ref.__setitem__((r, slice(None)), jnp.zeros((16, ref.shape[1]), f32)))

    def gsum(i, v, lo=0, n=None):
        a = OFF[i] + lo
        n = LENS[i] if n is None else n
        dsm[:, pl.ds(a, n)] += rsum(v)

    for b in range(nb):
        pick = (codec[b] == lax.broadcasted_iota(jnp.int32, (DS, SEL), 1)).astype(f32).astype(bf)
        tok = jnp.where(lax.broadcasted_iota(jnp.int32, (8, W), 0) == 0, part(sv, 13), 0.0)
        table = jnp.concatenate([y[b], jnp.zeros((8, W), f32), tok, jnp.zeros((8, W), f32)], axis=0)
        z = pos[...]
        for piece in pieces(table):
            z = z + nn(pick, piece)
        x[b * DS : (b + 1) * DS, :] = z

    def ln1(r):
        xh, rs, a = norm_rows(x[r, :], part(sv, 14), part(sv, 15))
        xh1[r, :] = xh
        rs1[r, :] = rs
        a1[r, :] = a.astype(bf)
    rows(M, R, ln1)

    qkv[:, 0:W] = (nn(a1[...], win[:, 0:W]) + sv[:, OFF[16] : OFF[16] + W]).astype(bf)
    qkv[:, W : 2 * W] = nn(a1[...], win[:, W : 2 * W]).astype(bf)
    qkv[:, 2 * W :] = (nn(a1[...], win[:, 2 * W : 3 * W]) + sv[:, OFF[16] + W : OFF[17]]).astype(bf)

    bias = jnp.where(lax.broadcasted_iota(jnp.int32, (DS, 1), 0) <= PATCHES, 0.0, -1e30).astype(f32)

    @pl.loop(0, nb * 4)
    def _(i):
        rsl = pl.ds(pl.multiple_of((i // 4) * DS, 16), DS)
        att_fwd(qkv, o, p, bias, rsl, W, i % 4, i * 4, 32)

    x[...] += nn(o[...], win[:, 3 * W : 4 * W]) + part(sv, 17)

    def ln2(r):
        xh, rs, a = norm_rows(x[r, :], part(sv, 18), part(sv, 19))
        xh2[r, :] = xh
        rs2[r, :] = rs
        a2[r, :] = a.astype(bf)
    rows(M, R, ln2)

    def fc1(c):
        h = nn(a2[...], win[:, pl.ds(pl.multiple_of(4 * W + c, 256), 256)])
        g, dg_ = gelu_pair(h + sv[:, pl.ds(pl.multiple_of(OFF[20] + c, 128), 256)])
        hid[:, pl.ds(c, 256)] = g.astype(bf)
        gp[:, pl.ds(c, 256)] = dg_.astype(bf)
    cols(DFF, 256, fc1)

    x[...] += nt(hid[...], wout[...]) + part(sv, 21)

    def lnf(r):
        xh, rs, a = norm_rows(x[r, :], part(sv, 22), part(sv, 23))
        xhf[r, :] = xh
        rsf[r, :] = rs
        u[r, :] = a.astype(bf)
    rows(M, R, lnf)

    for b in range(nb):
        def tstat(r):
            v = pix[b, r, :].astype(f32)
            m = jnp.mean(v, axis=1, keepdims=True)
            c = v - m
            q = pl.ds(pl.multiple_of(b * DS + r.start, 16), 16)
            tm[q, :] = m
            tr[q, :] = lax.rsqrt(jnp.mean(c * c, axis=1, keepdims=True) + 1e-06)
        rows(DS, 16, tstat)

    def headc(c):
        hwc = hw[:, pl.ds(c, 256)].astype(bf)
        pr = nn(u[...], hwc) + sv[:, pl.ds(pl.multiple_of(OFF[24] + c, 128), 256)]
        for b in range(nb):
            sl = slice(b * DS, (b + 1) * DS)
            tgt = (pix[b, :, pl.ds(c, 256)].astype(f32) - tm[sl, :]) * tr[sl, :]
            diff = jnp.where(codec[b] == 64, pr[sl] - tgt, 0.0)
            lacc[:, 0:256] += rsum(diff * diff)
            dp = diff * (2.0 * scale / PIX)
            dsm[:, pl.ds(pl.multiple_of(OFF[24] + c, 128), 256)] += rsum(dp)
            dpr[sl, pl.ds(c, 256)] = dp.astype(bf)
    cols(PIX, 256, headc)

    def hgrad(c):
        dhw[:, pl.ds(c, 256)] += dg(u[...], dpr[:, pl.ds(c, 256)], 0, 0)
    cols(PIX, 256, hgrad)
    t[...] = nt(dpr[...], hw[...].astype(bf))

    def lnfb(r):
        da = t[r, :]
        xh = xhf[r, :]
        gsum(22, da * xh)
        gsum(23, da)
        dx = norm_back(da, xh, rsf[r, :], part(sv, 22))
        gsum(21, dx)
        x[r, :] = dx
        d16[r, :] = dx.astype(bf)
    rows(M, R, lnfb)

    def fc1b(c):
        cs = pl.ds(c, 256)
        dwout[:, cs] += dg(d16[...], hid[:, cs], 0, 0)
        dh = nn(d16[...], wout[:, cs]) * gp[:, cs].astype(f32)
        dsm[:, pl.ds(pl.multiple_of(OFF[20] + c, 128), 256)] += rsum(dh)
        dh16 = dh.astype(bf)
        gp[:, cs] = dh16
        wc = pl.ds(pl.multiple_of(4 * W + c, 256), 256)
        dwin[:, wc] += dg(a2[...], dh16, 0, 0)
    cols(DFF, 256, fc1b)
    t[...] = nt(gp[...], win[:, 4 * W :])

    def ln2b(r):
        da = t[r, :]
        xh = xh2[r, :]
        gsum(18, da * xh)
        gsum(19, da)
        dx = x[r, :] + norm_back(da, xh, rs2[r, :], part(sv, 18))
        gsum(17, dx)
        x[r, :] = dx
        d16[r, :] = dx.astype(bf)
    rows(M, R, ln2b)

    dwin[:, 3 * W : 4 * W] += dg(o[...], d16[...], 0, 0)
    o[...] = nt(d16[...], win[:, 3 * W : 4 * W]).astype(bf)
    dqkv = gp

    @pl.loop(0, nb * 4)
    def _(i):
        rsl = pl.ds(pl.multiple_of((i // 4) * DS, 16), DS)
        att_bwd(qkv, o, p, dqkv, rsl, W, i % 4, i * 4, 32)

    def wq(c):
        cs = pl.ds(c, 256)
        dwin[:, cs] += dg(a1[...], dqkv[:, cs], 0, 0)
    cols(3 * W, 256, wq)
    def qb(r):
        dsm[:, OFF[16] : OFF[16] + W] += rsum(dqkv[r, 0:W].astype(f32))
        dsm[:, OFF[16] + W : OFF[17]] += rsum(dqkv[r, 2 * W : 3 * W].astype(f32))
    rows(M, R, qb)
    t[...] = nt(dqkv[:, 0 : 3 * W], win[:, 0 : 3 * W])

    def ln1b(r):
        da = t[r, :]
        xh = xh1[r, :]
        gsum(14, da * xh)
        gsum(15, da)
        x[r, :] = x[r, :] + norm_back(da, xh, rs1[r, :], part(sv, 14))
    rows(M, R, ln1b)

    for b in range(nb):
        pick = (coder[b] == lax.broadcasted_iota(jnp.int32, (SEL, DS), 0)).astype(f32).astype(bf)
        out = None
        for piece in pieces(x[b * DS : (b + 1) * DS, :]):
            v = nn(pick, piece)
            out = v if out is None else out + v
        dy[b] = out[0:ES]
        dsm[:, OFF[13] : OFF[14]] += out[64:65]

    @pl.when(pl.program_id(0) == pl.num_programs(0) - 1)
    def _():
        loss[...] = jnp.broadcast_to(jnp.sum(lacc[...], axis=1, keepdims=True) * (scale / PIX), (1, 128))
        for src, dst in ((dwin, win_out), (dwout, wout_out)):
            rows(DD, 16, lambda r: dst.__setitem__((r, slice(None)), src[r, :].astype(bf)))


def decoder(y, codec, coder, pix, pos, sv, win, wout, hw, scale, nb=2):
    n = y.shape[0]
    M = nb * DS
    whole = lambda a: pl.BlockSpec(a.shape, lambda i: (0,) * a.ndim, pipeline_mode=pl.Buffered(1))
    fixed = lambda s: pl.BlockSpec(s, lambda i: (0,) * len(s), pipeline_mode=pl.Buffered(1))
    blk = lambda s: pl.BlockSpec((nb,) + s, lambda i: (i, 0, 0))
    V = pltpu.VMEM
    return pl.pallas_call(
        functools.partial(dec_kernel, scale, nb),
        grid=(n // nb,),
        in_specs=[blk((ES, DD)), blk((DS, 1)), blk((1, DS)), blk((DS, PIX)), whole(pos), whole(sv), whole(win), whole(wout), whole(hw)],
        out_specs=[blk((ES, DD)), fixed(win.shape), fixed(wout.shape), fixed(hw.shape), fixed((1, SMALL)), fixed((1, 128))],
        out_shape=[
            jax.ShapeDtypeStruct((n, ES, DD), f32), jax.ShapeDtypeStruct(win.shape, bf),
            jax.ShapeDtypeStruct(wout.shape, bf), jax.ShapeDtypeStruct(hw.shape, f32),
            jax.ShapeDtypeStruct((1, SMALL), f32), jax.ShapeDtypeStruct((1, 128), f32)],
        scratch_shapes=[
            V(win.shape, f32), V(wout.shape, f32),
            V((M, DD), f32), V((M, DD), f32), V((M, DD), f32), V((M, DD), f32), V((M, DD), f32),
            V((M, 1), f32), V((M, 1), f32), V((M, 1), f32), V((M, 1), f32), V((M, 1), f32),
            V((M, DD), bf), V((M, DD), bf), V((M, DD), bf), V((M, DD), bf), V((M, 3 * DD), bf),
            V((nb * DHEADS, DS, DS), bf), V((M, DFF), bf), V((M, DFF), bf), V((M, PIX), bf), V((M, DD), bf),
            V((1, 256), f32)],
        compiler_params=pltpu.CompilerParams(vmem_limit_bytes=60 << 20),
        name="decoder",
    )(y, codec, coder, pix, pos, sv, win, wout, hw)


class Place:
    def __init__(self, nrow, ncol):
        side = math.isqrt(nrow)
        self.nrow, self.ncol = nrow, ncol
        self.n = {"x": side, "y": nrow // side, "z": ncol // 2}
        row, col = lax.axis_index("row"), lax.axis_index("col")
        self.at = {"x": row % side, "y": row // side, "z": col // 2, "core": col % 2}

    def moved(self, **by):
        at = {}
        for k, v in self.at.items():
            step = by.get(k, 0)
            size = 2 if k == "core" else self.n[k]
            at[k] = v if step == 0 else lax.rem(v + (step % size), size)
        return at["y"] * self.n["x"] + at["x"], at["z"] * 2 + at["core"]

    def greet(self):
        sem = pltpu.get_barrier_semaphore()
        count = 0
        for axis in ("x", "y", "z", "core"):
            size = 2 if axis == "core" else self.n[axis]
            for step in sorted({1 % size, (size - 1) % size} - {0}):
                pl.semaphore_signal(sem, inc=1, device_id=self.moved(**{axis: step}), device_id_type=pl.DeviceIdType.MESH)
                count += 1
        pl.semaphore_wait(sem, count)


class Shapes:
    def __init__(self, nrow, ncol):
        self.nrow, self.ncol = nrow, ncol
        self.awide, self.bwide = (5 * D + FF + DD) // ncol, FF // nrow
        self.alanes, self.blanes = self.window(self.awide, ncol), self.window(self.bwide, nrow)
        self.arows, self.brows = D // nrow, D // ncol
        self.crows, self.clanes = DD // nrow, 4 * DD // ncol + DFF // ncol
        self.drows, self.dlanes = DD // ncol, DFF // nrow
        self.erows = -(-(DD * PIX + SMALL) // (nrow * ncol * 256 * 8)) * 8
        self.blocks = {"A": (self.arows, self.alanes), "B": (self.brows, self.blanes), "C": (self.crows, self.clanes), "D": (self.drows, self.dlanes)}

    @staticmethod
    def window(wide, count):
        return max(-(-((wide * c) % 128 + wide) // 128) * 128 for c in range(count))

    def start(self, which, index):
        wide, lanes, total = (self.awide, self.alanes, 5 * D + FF + DD) if which == "A" else (self.bwide, self.blanes, FF)
        first = (wide * index) // 128
        last = (total - lanes) // 128
        if isinstance(index, int):
            return min(first, last) * 128
        return jnp.minimum(first, last) * 128


STREAMS = (("A",), ("B", "C", "D"))
ORDER = (("x", "y"), ("y", "x"))


def gather_kernel(nrow, ncol, ain, bin_, cin, din, aout, bout, cout, dout, send, recv, csend, crecv, lsem):
    place = Place(nrow, ncol)
    sh = Shapes(nrow, ncol)
    ins = {"A": ain, "B": bin_, "C": cin, "D": din}
    mats = "ABCD"

    def spot(m, row, col):
        if m == "A":
            return aout.at[col, pl.ds(pl.multiple_of(row * sh.arows, 16), sh.arows), :]
        if m == "B":
            return bout.at[row, pl.ds(pl.multiple_of(col * sh.brows, 16), sh.brows), :]
        if m == "C":
            return cout.at[pl.ds(pl.multiple_of(row * sh.crows, 16), sh.crows), pl.ds(pl.multiple_of(col * sh.clanes, 128), sh.clanes)]
        return dout.at[pl.ds(pl.multiple_of(col * sh.drows, 16), sh.drows), pl.ds(pl.multiple_of(row * sh.dlanes, 128), sh.dlanes)]

    nz = place.n["z"]
    place.greet()
    me = place.moved()
    locals_ = [pltpu.make_async_copy(ins[m], spot(m, *me), lsem.at[i]) for i, m in enumerate(mats)]
    for c in locals_:
        c.start()
    steps = []
    for s in (0, 1):
        p, q = ORDER[s]
        for i in range(place.n[q]):
            for j in range(place.n[p]):
                for k in range(nz):
                    steps.append((i + j + k, k, s, i, j, k))
    steps.sort()
    sent = []
    late = []
    for _, _, s, i, j, k in steps:
        p, q = ORDER[s]
        npp, nq = place.n[p], place.n[q]
        slot = (i * npp + j) * nz + k
        own = i == j == k == 0
        for m in STREAMS[s]:
            mi = mats.index(m)
            dst = spot(m, *place.moved(**{q: -i, p: -j, "z": -k}))
            src = ins[m] if own else dst
            if not own:
                pltpu.make_async_remote_copy(dst, dst, send.at[mi, slot], recv.at[mi, slot], device_id=place.moved(core=1), device_id_type=pl.DeviceIdType.MESH).wait_recv()
            plan = []
            if i == j == 0 and k < nz - 1:
                plan.append(({"z": 1}, slot + 1))
            if i == 0 and j < npp - 1:
                plan.append(({p: 1}, slot + nz))
            if i < nq - 1:
                plan.append(({q: 1}, slot + nz * npp))
            for by, there in plan:
                c = pltpu.make_async_remote_copy(src, dst, send.at[mi, there], recv.at[mi, there], device_id=place.moved(**by), device_id_type=pl.DeviceIdType.MESH)
                c.start()
                sent.append(c)
            c = pltpu.make_async_remote_copy(src, dst, csend.at[mi, slot], crecv.at[mi, slot], device_id=place.moved(core=1), device_id_type=pl.DeviceIdType.MESH)
            c.start()
            sent.append(c)
            other = spot(m, *place.moved(**{q: -i, p: -j, "z": -k, "core": 1}))
            late.append(pltpu.make_async_remote_copy(other, other, csend.at[mi, slot], crecv.at[mi, slot], device_id=place.moved(core=1), device_id_type=pl.DeviceIdType.MESH))
    for c in late:
        c.wait_recv()
    for c in sent:
        c.wait_send()
    for c in locals_:
        c.wait()


def gather_weights(nrow, ncol, ain, bin_, cin, din):
    sh = Shapes(nrow, ncol)
    half = nrow * ncol // 2
    S = jax.ShapeDtypeStruct
    anyspec = pl.BlockSpec(memory_space=pl.ANY)
    sem = pltpu.SemaphoreType.DMA
    return pl.pallas_call(
        functools.partial(gather_kernel, nrow, ncol),
        in_specs=[anyspec] * 4, out_specs=[anyspec] * 4,
        out_shape=[S((ncol, D, sh.alanes), bf), S((nrow, D, sh.blanes), bf), S((DD, 4 * DD + DFF), bf), S((DD, DFF), bf)],
        scratch_shapes=[sem((4, half)), sem((4, half)), sem((4, half)), sem((4, half)), sem((4,))],
        compiler_params=pltpu.CompilerParams(collective_id=0, has_side_effects=True),
        name="gather_weights",
    )(ain, bin_, cin, din)


RSTREAMS = (("A",), ("B", "C", "D", "E"))


def reduce_kernel(nrow, ncol, da, db, dc, dd, de, loss,
                  ga, gb, gc, gd, eall, *scratch):
    mats = "ABCDE"
    acc, sib, rq, rp, rz = (dict(zip(mats, scratch[5 * t : 5 * t + 5])) for t in range(5))
    ge, lsem, csend, crecv, send, qrecv, prec, zrecv, esend, erecv, ecs, ecr = scratch[25:]
    place = Place(nrow, ncol)
    sh = Shapes(nrow, ncol)
    nz = place.n["z"]
    ins = {"A": da, "B": db, "C": dc, "D": dd, "E": de}
    outs = {"A": ga, "B": gb, "C": gc, "D": gd}

    def spot(m, row, col):
        if m == "A":
            return da.at[pl.ds(pl.multiple_of(row * sh.arows, 16), sh.arows), pl.ds(pl.multiple_of(sh.start("A", col), 128), sh.alanes)]
        if m == "B":
            return db.at[pl.ds(pl.multiple_of(col * sh.brows, 16), sh.brows), pl.ds(pl.multiple_of(sh.start("B", row), 128), sh.blanes)]
        if m == "C":
            return dc.at[pl.ds(pl.multiple_of(row * sh.crows, 16), sh.crows), pl.ds(pl.multiple_of(col * sh.clanes, 128), sh.clanes)]
        if m == "D":
            return dd.at[pl.ds(pl.multiple_of(col * sh.drows, 16), sh.drows), pl.ds(pl.multiple_of(row * sh.dlanes, 128), sh.dlanes)]
        return de.at[row * ncol + col]

    place.greet()

    def remote(src, dst, ssem, rsem, **by):
        return pltpu.make_async_remote_copy(src, dst, ssem, rsem, device_id=place.moved(**by), device_id_type=pl.DeviceIdType.MESH)

    steps = []
    for s in (0, 1):
        p, q = ORDER[s]
        for i in range(place.n[q]):
            for j in range(place.n[p]):
                for k in range(nz):
                    steps.append(((place.n[q] - 1 - i) + (place.n[p] - 1 - j) + (nz - 1 - k), s, i, j, k))
    steps.sort()
    sent = []
    loads = {}
    for _, s, i, j, k in steps:
        p, q = ORDER[s]
        slot = (i * place.n[p] + j) * nz + k
        for m in RSTREAMS[s]:
            mi = mats.index(m)
            c = remote(spot(m, *place.moved(**{q: -i, p: -j, "z": -k, "core": 1})), sib[m].at[slot], csend.at[mi, slot], crecv.at[mi, slot], core=1)
            c.start()
            sent.append(c)
            loads[m, slot] = pltpu.make_async_copy(spot(m, *place.moved(**{q: -i, p: -j, "z": -k})), acc[m].at[slot], lsem.at[mi, slot])
            loads[m, slot].start()
    for _, s, i, j, k in steps:
        p, q = ORDER[s]
        npp, nq = place.n[p], place.n[q]
        slot = (i * npp + j) * nz + k
        for m in RSTREAMS[s]:
            mi = mats.index(m)
            loads[m, slot].wait()
            remote(sib[m].at[slot], sib[m].at[slot], csend.at[mi, slot], crecv.at[mi, slot], core=1).wait_recv()
            terms = [(acc[m], slot), (sib[m], slot)]
            if i < nq - 1:
                remote(rq[m].at[slot], rq[m].at[slot], send.at[mi, slot], qrecv.at[mi, slot], core=1).wait_recv()
                terms.append((rq[m], slot))
            if i == 0 and j < npp - 1:
                remote(rp[m].at[slot], rp[m].at[slot], send.at[mi, slot], prec.at[mi, slot], core=1).wait_recv()
                terms.append((rp[m], slot))
            if i == j == 0 and k < nz - 1:
                remote(rz[m].at[slot], rz[m].at[slot], send.at[mi, slot], zrecv.at[mi, slot], core=1).wait_recv()
                terms.append((rz[m], slot))
            last = i == j == k == 0
            total = acc[m].shape[1]
            size = 8 if m == "E" else 16

            def add(r, m=m, terms=terms, last=last, slot=slot):
                v = terms[0][0][slot, r, :].astype(f32)
                for ref, at in terms[1:]:
                    v = v + ref[at, r, :].astype(f32)
                if not last:
                    acc[m][slot, r, :] = v.astype(acc[m].dtype)
                elif m == "E":
                    ge[pl.ds(0, total), :] = v
                else:
                    outs[m][r, :] = v
            if m == "E":
                add(slice(None))
            else:
                rows(total, size, add)
            if last:
                continue
            if i > 0:
                c = remote(acc[m].at[slot], rq[m].at[slot - npp * nz], send.at[mi, slot], qrecv.at[mi, slot - npp * nz], **{q: -1})
            elif j > 0:
                c = remote(acc[m].at[slot], rp[m].at[slot - nz], send.at[mi, slot], prec.at[mi, slot - nz], **{p: -1})
            else:
                c = remote(acc[m].at[slot], rz[m].at[slot - 1], send.at[mi, slot], zrecv.at[mi, slot - 1], z=-1)
            c.start()
            sent.append(c)


    row, col = place.moved()
    la = lax.broadcasted_iota(jnp.int32, (1, sh.alanes), 1) + (sh.start("A", col) - col * sh.awide)
    lb = lax.broadcasted_iota(jnp.int32, (1, sh.blanes), 1) + (sh.start("B", row) - row * sh.bwide)
    va = jnp.where((la >= 0) & (la < sh.awide), ga[...], 0.0)
    vb = jnp.where((lb >= 0) & (lb < sh.bwide), gb[...], 0.0)
    er = sh.erows
    sq = jnp.zeros((1, 128), f32)
    for v in (va, vb, gc[...], gd[...], ge[0:er, :]):
        w = rsum(v * v)
        for c0 in range(0, w.shape[1], 128):
            sq = sq + w[:, c0 : c0 + 128]
    ge[er : er + 8, :] = jnp.concatenate([jnp.broadcast_to(sq, (8, 128)), jnp.broadcast_to(loss[...], (8, 128))], axis=1)

    def espot(**by):
        r, c = place.moved(**by)
        return eall.at[r * ncol + c]

    eall[row * ncol + col] = ge[...]
    npp, nq = place.n["x"], place.n["y"]
    esteps = sorted((i + j + k, k, i, j) for i in range(nq) for j in range(npp) for k in range(nz))
    late = []
    for _, k, i, j in esteps:
        slot = (i * npp + j) * nz + k
        own = i == j == k == 0
        dst = espot(y=-i, x=-j, z=-k)
        src = ge if own else dst
        if not own:
            remote(dst, dst, esend.at[slot], erecv.at[slot], core=1).wait_recv()
        plan = []
        if i == j == 0 and k < nz - 1:
            plan.append(({"z": 1}, slot + 1))
        if i == 0 and j < npp - 1:
            plan.append(({"x": 1}, slot + nz))
        if i < nq - 1:
            plan.append(({"y": 1}, slot + nz * npp))
        for by, there in plan:
            c = remote(src, dst, esend.at[there], erecv.at[there], **by)
            c.start()
            sent.append(c)
        c = remote(src, dst, ecs.at[slot], ecr.at[slot], core=1)
        c.start()
        sent.append(c)
        other = espot(y=-i, x=-j, z=-k, core=1)
        late.append(remote(other, other, ecs.at[slot], ecr.at[slot], core=1))
    for c in late:
        c.wait_recv()
    for c in sent:
        c.wait_send()


def reduce_grads(nrow, ncol, da, db, dc, dd, de, loss):
    sh = Shapes(nrow, ncol)
    half = nrow * ncol // 2
    side = math.isqrt(nrow)
    n = {"x": side, "y": nrow // side, "z": ncol // 2}
    S = jax.ShapeDtypeStruct
    V = pltpu.VMEM
    anyspec = pl.BlockSpec(memory_space=pl.ANY)
    vm = pl.BlockSpec(memory_space=pltpu.VMEM)
    sem = pltpu.SemaphoreType.DMA
    kinds = [sh.blocks[m] + (bf,) for m in "ABCD"] + [(sh.erows, 256, f32)]
    order = [ORDER[s] for s in (0, 1, 1, 1, 1)]
    nz = n["z"]
    scratch = []
    for count in (
        lambda p, q: half, lambda p, q: half, lambda p, q: (n[q] - 1) * n[p] * nz,
        lambda p, q: (n[p] - 1) * nz, lambda p, q: nz - 1,
    ):
        scratch += [V((count(p, q), r, l), t) for (r, l, t), (p, q) in zip(kinds, order)]
    scratch += [V((sh.erows + 8, 256), f32)]
    big = n["x"] * n["y"] * nz - min(n["x"], n["y"]) * nz
    scratch += [sem((5, half))] * 4 + [sem((5, big)), sem((5, max(n["x"], n["y"]) * nz)), sem((5, nz))] + [sem((half,))] * 4
    return pl.pallas_call(
        functools.partial(reduce_kernel, nrow, ncol),
        in_specs=[anyspec] * 5 + [vm], out_specs=[vm] * 5,
        out_shape=[S(sh.blocks[m], f32) for m in "ABCD"] + [S((nrow * ncol, sh.erows + 8, 256), f32)],
        scratch_shapes=scratch,
        compiler_params=pltpu.CompilerParams(collective_id=1, has_side_effects=True, vmem_limit_bytes=60 << 20),
        name="reduce_grads",
    )(da, db, dc, dd, de, loss)


def windows(nrow, ncol, weights):
    sh = Shapes(nrow, ncol)
    row, col = lax.axis_index("row"), lax.axis_index("col")

    def put(v, which, index, wide, lanes):
        if wide == lanes:
            return v
        shift = index * wide - sh.start(which, index)
        return lax.dynamic_update_slice(jnp.zeros((v.shape[0], lanes), v.dtype), v, (0, shift))
    a, b, c, d = (w.astype(bf) for w in weights)
    return put(a, "A", col, sh.awide, sh.alanes), put(b.T, "B", row, sh.bwide, sh.blanes), c, d.T


def unwindow(nrow, ncol, ga, gb, gc, gd):
    sh = Shapes(nrow, ncol)
    row, col = lax.axis_index("row"), lax.axis_index("col")

    def take(v, which, index, wide, lanes):
        if wide == lanes:
            return v
        return lax.dynamic_slice(v, (0, index * wide - sh.start(which, index)), (v.shape[0], wide))
    return take(ga, "A", col, sh.awide, sh.alanes), take(gb, "B", row, sh.bwide, sh.blanes).T, gc, gd.T


def tile_plan(sh, which):
    wide, count = (sh.awide, sh.ncol) if which == "A" else (sh.bwide, sh.nrow)
    alone, shared = [], []
    for c in range(count):
        first, end = wide * c // 128, -(-(wide * (c + 1)) // 128)
        base = sh.start(which, c) // 128
        lo = first + 1 if (wide * c) % 128 else first
        hi = end - 1 if (wide * (c + 1)) % 128 else end
        alone.append((c, lo, hi, base))
        if hi < end:
            shared.append((c, hi, base, sh.start(which, c + 1) // 128))
    return alone, shared


def joiner(sh, which, src, dst, tmp, sem, base=0):
    alone, shared = tile_plan(sh, which)
    copies = []
    for c, lo, hi, at in alone:
        copies.append((src.at[c, :, pl.ds((lo - at) * 128, (hi - lo) * 128)], dst.at[:, pl.ds(lo * 128, (hi - lo) * 128)]))
    for u, (c, t, at, nxt) in enumerate(shared):
        copies.append((src.at[c, :, pl.ds((t - at) * 128, 128)], dst.at[:, pl.ds(t * 128, 128)]))
        copies.append((src.at[c + 1, :, pl.ds((t - nxt) * 128, 128)], tmp.at[u]))
    made = [pltpu.make_async_copy(a, b, sem.at[base + i]) for i, (a, b) in enumerate(copies)]
    for m in made:
        m.start()

    def end():
        for m in made:
            m.wait()
        for u, (c, t, at, nxt) in enumerate(shared):
            dst[:, t * 128 : (t + 1) * 128] += tmp[u]
    return end


def joiner_scratch(sh):
    V = pltpu.VMEM
    counts = [(len(a), len(s)) for a, s in (tile_plan(sh, "A"), tile_plan(sh, "B"))]
    return [V((D, 5 * D + FF + DD), bf), V((D, FF), bf)] + [V((max(s, 1), D, 128), bf) for _, s in counts] + [
        pltpu.SemaphoreType.DMA((a + 2 * s,)) for a, s in counts]


EG = 4 * ES
O_Q, O_P, O_F, O_E = D, 4 * D, 5 * D, 5 * D + FF


def enc_fwd_kernel(sh, pix, keepc, pos3, sv, awin, bwin,
                   y, kept, xh1, xh2, xhf, rs1, rs2, rsf, a1, a2, e16, o, qkv, p, hid, gp, x, bias, win, wout, atmp, btmp, asem, bsem):
    enda = joiner(sh, "A", awin, win, atmp, asem)
    endb = joiner(sh, "B", bwin, wout, btmp, bsem)
    n = pix.shape[0]
    M = n * ES
    R = 32
    W = D
    for i in range(0, n, 2):
        two = []
        for b in (i, i + 1):
            kc = keepc[b * ES : (b + 1) * ES, :]
            pick = (kc == lax.broadcasted_iota(jnp.int32, (ES, DS), 1)).astype(f32).astype(bf)
            two.append(nn(pick, pix[b]))
        kept[i * ES : (i + 2) * ES, :] = jnp.concatenate(two, axis=0).astype(bf)
    enda()
    for lo in range(0, M, EG):
        sl = slice(lo, lo + EG)
        kc = keepc[sl, :]
        pick = (kc == lax.broadcasted_iota(jnp.int32, (EG, DS), 1)).astype(f32).astype(bf)
        v = nn(kept[sl, :], win[:, 0:W]) + part(sv, 10)
        v = v + nn(pick, pos3[0:DS, :]) + nn(pick, pos3[DS : 2 * DS, :]) + nn(pick, pos3[2 * DS :, :])
        x[sl, :] = jnp.where(kc < PATCHES, v, jnp.where(kc == NOROW - 1, part(sv, 11), 0.0))

    def ln1(r):
        xh, rs, a = norm_rows(x[r, :], part(sv, 0), part(sv, 1))
        xh1[r, :] = xh
        rs1[r, :] = rs
        a1[r, :] = a.astype(bf)
    rows(M, R, ln1)
    qkv[:, 0:W] = (nn(a1[...], win[:, O_Q : O_Q + W]) + sv[:, OFF[2] : OFF[2] + W]).astype(bf)
    qkv[:, W : 2 * W] = nn(a1[...], win[:, O_Q + W : O_Q + 2 * W]).astype(bf)
    qkv[:, 2 * W :] = (nn(a1[...], win[:, O_Q + 2 * W : O_P]) + sv[:, OFF[2] + W : OFF[3]]).astype(bf)

    ki = lax.broadcasted_iota(jnp.int32, (EG, EG), 0)
    qi = lax.broadcasted_iota(jnp.int32, (EG, EG), 1)
    same = jnp.zeros((EG, EG), jnp.bool_)
    for j in range(4):
        same = same | ((ki >= j * ES) & (ki < j * ES + KEEP + 1) & (qi >= j * ES) & (qi < (j + 1) * ES))
    bias[...] = jnp.where(same, 0.0, -1e30).astype(f32)

    @pl.loop(0, (n // 4) * 6)
    def _(i):
        rsl = pl.ds(pl.multiple_of((i // 6) * EG, 16), EG)
        att_fwd(qkv, o, p, bias[...], rsl, W, i % 6, i * 2, 64)

    x[...] += nn(o[...], win[:, O_P : O_P + W]) + part(sv, 3)

    def ln2(r):
        xh, rs, a = norm_rows(x[r, :], part(sv, 4), part(sv, 5))
        xh2[r, :] = xh
        rs2[r, :] = rs
        a2[r, :] = a.astype(bf)
    rows(M, R, ln2)

    def fc1(c):
        h = nn(a2[...], win[:, pl.ds(pl.multiple_of(O_F + c, 256), 256)])
        g, dg_ = gelu_pair(h + sv[:, pl.ds(pl.multiple_of(OFF[6] + c, 128), 256)])
        hid[:, pl.ds(c, 256)] = g.astype(bf)
        gp[:, pl.ds(c, 256)] = dg_.astype(bf)
    cols(FF, 256, fc1)
    endb()
    x[...] += nt(hid[...], wout[...]) + part(sv, 7)

    def lnf(r):
        xh, rs, a = norm_rows(x[r, :], part(sv, 8), part(sv, 9))
        xhf[r, :] = xh
        rsf[r, :] = rs
        e16[r, :] = a.astype(bf)
    rows(M, R, lnf)
    y[...] = nn(e16[...], win[:, O_E:]) + part(sv, 12)


def vspec(k):
    return [pl.BlockSpec(memory_space=pltpu.VMEM)] * k


def encoder_fwd(sh, pix, keepc, pos3, sv, awin, bwin):
    n = pix.shape[0]
    M = n * ES
    S = jax.ShapeDtypeStruct
    V = pltpu.VMEM
    outs = [S((M, DD), f32), S((M, D), bf), S((M, D), f32), S((M, D), f32), S((M, D), f32),
            S((M, 1), f32), S((M, 1), f32), S((M, 1), f32), S((M, D), bf), S((M, D), bf), S((M, D), bf), S((M, D), bf),
            S((M, 3 * D), bf), S((n // 4 * HEADS, EG, EG), bf), S((M, FF), bf), S((M, FF), bf)]
    return pl.pallas_call(
        functools.partial(enc_fwd_kernel, sh),
        in_specs=vspec(4) + [pl.BlockSpec(memory_space=pl.ANY)] * 2, out_specs=vspec(len(outs)), out_shape=outs,
        scratch_shapes=[V((M, D), f32), V((EG, EG), f32)] + joiner_scratch(sh),
        compiler_params=pltpu.CompilerParams(vmem_limit_bytes=60 << 20),
        name="encoder_fwd",
    )(pix, keepc, pos3, sv, awin, bwin)


def enc_bwd_kernel(sh, dy, keepc, sv, awin, bwin, kept, xh1, xh2, xhf, rs1, rs2, rsf, a1, a2, e16, o, qkv, p, hid, gp,
                   dwin, dwout, dsm, x, t, d16, dqkv, stage, sem, win, wout, atmp, btmp, asem, bsem):
    enda = joiner(sh, "A", awin, win, atmp, asem)
    endb = joiner(sh, "B", bwin, wout, btmp, bsem)
    M = dy.shape[0]
    R = 32
    W = D
    CW = 256
    dsm[...] = jnp.zeros_like(dsm)

    def gsum(i, v, lo=0, n=None):
        a = OFF[i] + lo
        n = LENS[i] if n is None else n
        dsm[:, pl.ds(a, n)] += rsum(v)

    def put(out, count, base, value):
        def copy(i, slot):
            return pltpu.make_async_copy(stage.at[slot], out.at[:, pl.ds(pl.multiple_of(base + i * CW, 128), CW)], sem.at[slot])

        @pl.loop(0, count)
        def _(i):
            slot = lax.rem(i, 2)

            @pl.when(i >= 2)
            def _():
                copy(i - 2, slot).wait()
            stage[slot] = value(pl.multiple_of(i * CW, CW)).astype(bf)
            copy(i, slot).start()
        for i in range(max(count - 2, 0), count):
            copy(i, i % 2).wait()

    def emb(r):
        v = dy[r, :]
        gsum(12, v)
        d16[r, 0:DD] = v.astype(bf)
    rows(M, R, emb)
    put(dwin, DD // CW, O_E, lambda c: dg(e16[...], d16[:, pl.ds(c, CW)], 0, 0))
    enda()
    endb()
    t[...] = nt(d16[:, 0:DD], win[:, O_E:])

    def lnfb(r):
        da = t[r, :]
        xh = xhf[r, :]
        gsum(8, da * xh)
        gsum(9, da)
        dx = norm_back(da, xh, rsf[r, :], part(sv, 8))
        gsum(7, dx)
        x[r, :] = dx
        d16[r, :] = dx.astype(bf)
    rows(M, R, lnfb)
    put(dwout, FF // CW, 0, lambda c: dg(d16[...], hid[:, pl.ds(c, CW)], 0, 0))

    def fc1b(c):
        cs = pl.ds(c, CW)
        dh = nn(d16[...], wout[:, cs]) * gp[:, cs].astype(f32)
        dsm[:, pl.ds(pl.multiple_of(OFF[6] + c, 128), CW)] += rsum(dh)
        gp[:, cs] = dh.astype(bf)
        return dg(a2[...], gp[:, cs], 0, 0)
    put(dwin, FF // CW, O_F, fc1b)
    t[...] = nt(gp[...], win[:, O_F:O_E])

    def ln2b(r):
        da = t[r, :]
        xh = xh2[r, :]
        gsum(4, da * xh)
        gsum(5, da)
        dx = x[r, :] + norm_back(da, xh, rs2[r, :], part(sv, 4))
        gsum(3, dx)
        x[r, :] = dx
        d16[r, :] = dx.astype(bf)
    rows(M, R, ln2b)
    put(dwin, D // CW, O_P, lambda c: dg(o[...], d16[:, pl.ds(c, CW)], 0, 0))
    d16[...] = nt(d16[...], win[:, O_P:O_F]).astype(bf)

    @pl.loop(0, (M // EG) * 6)
    def _(i):
        rsl = pl.ds(pl.multiple_of((i // 6) * EG, 16), EG)
        att_bwd(qkv, d16, p, dqkv, rsl, W, i % 6, i * 2, 64)

    put(dwin, 3 * D // CW, O_Q, lambda c: dg(a1[...], dqkv[:, pl.ds(c, CW)], 0, 0))
    def qb(r):
        dsm[:, OFF[2] : OFF[2] + W] += rsum(dqkv[r, 0:W].astype(f32))
        dsm[:, OFF[2] + W : OFF[3]] += rsum(dqkv[r, 2 * W : 3 * W].astype(f32))
    rows(M, R, qb)
    t[...] = nt(dqkv[...], win[:, O_Q:O_P])

    def ln1b(r):
        da = t[r, :]
        xh = xh1[r, :]
        gsum(0, da * xh)
        gsum(1, da)
        dx = x[r, :] + norm_back(da, xh, rs1[r, :], part(sv, 0))
        kc = keepc[r, :]
        gsum(11, jnp.where(kc == NOROW - 1, dx, 0.0))
        dx = jnp.where(kc < PATCHES, dx, 0.0)
        gsum(10, dx)
        d16[r, :] = dx.astype(bf)
    rows(M, R, ln1b)
    put(dwin, D // CW, 0, lambda c: dg(kept[...], d16[:, pl.ds(c, CW)], 0, 0))


def encoder_bwd(sh, dy, keepc, sv, awin, bwin, saved):
    M = dy.shape[0]
    S = jax.ShapeDtypeStruct
    V = pltpu.VMEM
    anyspec = pl.BlockSpec(memory_space=pl.ANY)
    return pl.pallas_call(
        functools.partial(enc_bwd_kernel, sh),
        in_specs=vspec(3) + [pl.BlockSpec(memory_space=pl.ANY)] * 2 + vspec(len(saved)),
        out_specs=[anyspec, anyspec, pl.BlockSpec(memory_space=pltpu.VMEM)],
        out_shape=[S((D, 5 * D + FF + DD), bf), S((D, FF), bf), S((1, SMALL), f32)],
        scratch_shapes=[V((M, D), f32), V((M, D), f32), V((M, D), bf), V((M, 3 * D), bf), V((2, D, 256), bf),
                        pltpu.SemaphoreType.DMA((2,))] + joiner_scratch(sh),
        compiler_params=pltpu.CompilerParams(vmem_limit_bytes=62 << 20),
        name="encoder_bwd",
    )(dy, keepc, sv, awin, bwin, *saved)


def sincos_np(width):
    quarter = width // 4
    freq = (1.0 / np.float32(10000.0) ** (np.arange(quarter, dtype=np.float32) / np.float32(quarter))).astype(np.float32)
    pos = np.arange(GRID * GRID)
    cp = (pos % GRID).astype(np.float32)[:, None] * freq[None, :]
    rp = (pos // GRID).astype(np.float32)[:, None] * freq[None, :]
    return np.concatenate([np.sin(cp), np.cos(cp), np.sin(rp), np.cos(rp)], axis=1).astype(np.float32)


def tables():
    dec = np.zeros((DS, DD), np.float32)
    dec[:PATCHES] = sincos_np(DD)
    enc = np.zeros((DS, D), np.float32)
    enc[:PATCHES] = sincos_np(D)
    b = ml_dtypes.bfloat16
    hi = enc.astype(b)
    mid = (enc - hi.astype(np.float32)).astype(b)
    lo = (enc - hi.astype(np.float32) - mid.astype(np.float32)).astype(b)
    return dec, np.concatenate([hi, mid, lo], axis=0)


def adamw(weight, first, second, grad):
    first = 0.9 * first + (1.0 - 0.9) * grad
    second = 0.999 * second + (1.0 - 0.999) * grad * grad
    first_hat = first / (1.0 - 0.9**STEP)
    second_hat = second / (1.0 - 0.999**STEP)
    weight = weight - 0.08 * (first_hat / (jnp.sqrt(second_hat) + 1e-08) + 0.05 * weight)
    return (weight, first, second)


def local(pixels, keep_idx, restore, *state):
    weights, firsts, seconds = state[0:6], state[6:12], state[12:18]
    nrow, ncol = lax.axis_size("row"), lax.axis_size("col")
    sh = Shapes(nrow, ncol)
    n = pixels.shape[0]
    denom = 1.0 * n * nrow * ncol * (PATCHES - KEEP)

    dec_pos, enc_pos = tables()
    pix = jnp.pad(pixels, ((0, 0), (0, DS - PATCHES), (0, 0)))
    fill = lambda count, value: jnp.full((n, count), value, jnp.int32)
    keepc = jnp.concatenate([keep_idx, fill(1, NOROW - 1), fill(ES - KEEP - 1, NOROW)], axis=1).reshape(n * ES, 1)
    code = jnp.concatenate([jnp.where(restore < KEEP, restore, 64), fill(1, KEEP), fill(DS - PATCHES - 1, NOROW)], axis=1)
    head, sv = weights[4], weights[5].reshape(1, SMALL)

    aw, bw, c, dt = gather_weights(nrow, ncol, *windows(nrow, ncol, weights[0:4]))
    y, *saved = encoder_fwd(sh, pix, keepc, jnp.asarray(enc_pos), sv, aw, bw)
    dy, dc, ddt, dhead, dsm_d, loss = decoder(
        y.reshape(n, ES, DD), code.reshape(n, DS, 1), code.reshape(n, 1, DS), pix, jnp.asarray(dec_pos), sv, c, dt, head, 1.0 / denom)
    da, dbt, dsm_e = encoder_bwd(sh, dy.reshape(n * ES, DD), keepc, sv, aw, bw, saved)

    count = nrow * ncol * sh.erows * 256
    flat = jnp.concatenate([dhead.reshape(-1), (dsm_d + dsm_e).reshape(-1), jnp.zeros((count - DD * PIX - SMALL,), f32)])
    ga, gb, gc, gd, ge = reduce_grads(nrow, ncol, da, dbt, dc, ddt, flat.reshape(nrow * ncol, sh.erows, 256), loss)
    flat = ge[:, : sh.erows].reshape(-1)
    grads = [*unwindow(nrow, ncol, ga, gb, gc, gd), flat[: DD * PIX].reshape(DD, PIX), flat[DD * PIX : DD * PIX + SMALL]]
    aux = jnp.sum(ge[:, sh.erows], axis=0)
    norm = jnp.sqrt(jnp.sum(aux[:128]))
    loss = aux[128]
    factor = 0.0001 / jnp.maximum(norm, 0.0001)
    done = [adamw(w, m, v, g * factor) for w, m, v, g in zip(weights, firsts, seconds, grads)]
    return tuple(d[0] for d in done) + tuple(d[1] for d in done) + tuple(d[2] for d in done) + (loss, norm)


def solution(mesh):
    both = P(("row", "col"))
    big = [P("row", "col")] * 4 + [P()] * 2
    return jax.shard_map(
        local,
        mesh=mesh,
        in_specs=(both, both, both, *big, *big, *big),
        out_specs=(*big, *big, *big, P(), P()),
        check_vma=False,
    )
```

```python
import functools
import math

import jax
import jax.numpy as jnp
import ml_dtypes
import numpy as np
from jax import lax
from jax.experimental import pallas as pl
from jax.experimental.pallas import tpu as pltpu
from jax.sharding import PartitionSpec as P

D = 768
HEADS = 12
FF = 3072
DD = 512
DHEADS = 16
DFF = 2048
PIX = 768
GRID = 14
PATCHES = 196
KEEP = 49
STEP = 10
SMALL = 21248
ES = 56
DS = 208
SEL = 80
NOROW = 255
f32 = jnp.float32
bf = jnp.bfloat16

LENS = [
    D, D, 2 * D, D, D, D, FF, D, D, D, D, D,
    DD, DD, DD, DD, 2 * DD, DD, DD, DD, DFF, DD, DD, DD, PIX,
]
OFF = [0]
for piece in LENS:
    OFF.append(OFF[-1] + piece)


def part(ref, i):
    return ref[:, OFF[i] : OFF[i + 1]]


def dg(a, b, ca, cb):
    return lax.dot_general(a, b, (((ca,), (cb,)), ((), ())), preferred_element_type=f32)


def nn(a, b):
    return dg(a, b, 1, 0)


def nt(a, b):
    return dg(a, b, 1, 1)


def rows(total, size, fn):
    @pl.loop(0, total // size)
    def _(i):
        fn(pl.ds(pl.multiple_of(i * size, size), size))


def rows_sum(total, size, widths, fn):
    def body(i, carry):
        parts = fn(pl.ds(pl.multiple_of(i * size, size), size))
        return tuple(c + jnp.sum(v.reshape(size // 8, 8, v.shape[1]), axis=0) for c, v in zip(carry, parts))
    carry = lax.fori_loop(0, total // size, body, tuple(jnp.zeros((8, w), f32) for w in widths))
    return [rsum(c) for c in carry]


def pieces(x):
    hi = x.astype(bf)
    rest = x - hi.astype(f32)
    mid = rest.astype(bf)
    low = (rest - mid.astype(f32)).astype(bf)
    return hi, mid, low


def gelu_pair(x):
    ax = jnp.abs(x)
    d = 1.0 + (0.3275911 * 0.7071067811865476) * ax
    r = pl.reciprocal(d, approx=True)
    t = r * (2.0 - d * r)
    e = jnp.exp(-0.5 * (x * x))
    poly = ((((0.5 * 1.061405429 * t - 0.5 * 1.453152027) * t + 0.5 * 1.421413741) * t
             - 0.5 * 0.284496736) * t + 0.5 * 0.254829592) * t
    q = poly * e
    phi = jnp.where(x >= 0.0, 1.0 - q, q)
    return x * phi, phi + x * (e * 0.3989422804014327)


def norm_rows(x, gain, shift):
    c = x - jnp.mean(x, axis=1, keepdims=True)
    rs = lax.rsqrt(jnp.mean(c * c, axis=1, keepdims=True) + 1e-06)
    xh = c * rs
    return xh, rs, xh * gain + shift


def norm_back(da, xh, rs, gain):
    g = da * gain
    m1 = jnp.mean(g, axis=1, keepdims=True)
    m2 = jnp.mean(g * xh, axis=1, keepdims=True)
    return rs * (g - m1 - xh * m2)


def rsum(x):
    return jnp.sum(x, axis=0, keepdims=True)


def lanes_of(x, h, hd):
    lane = lax.broadcasted_iota(jnp.int32, (1, 128), 1)
    return jnp.where((lane >= h * hd) & (lane < (h + 1) * hd), x, jnp.zeros_like(x))


def stack(x, hd):
    return jnp.concatenate([lanes_of(x, h, hd) for h in range(128 // hd)], axis=0)


def unstack(x, hd):
    n = x.shape[0] * hd // 128
    out = None
    for h in range(128 // hd):
        t = lanes_of(x[h * n : (h + 1) * n], h, hd)
        out = t if out is None else out + t
    return out


def att_fwd(qkv, o, p, bias, rsl, width, g, slot, hd):
    c0 = g * 128
    q = qkv[rsl, c0 : c0 + 128]
    k = qkv[rsl, c0 + width : c0 + width + 128]
    v = qkv[rsl, c0 + 2 * width : c0 + 2 * width + 128]
    n = q.shape[0]
    every = nt(stack(k, hd), q)
    probs = []
    for h in range(128 // hd):
        s = every[h * n : (h + 1) * n] * (hd ** -0.5 * 1.4426950408889634) + bias
        e = jnp.exp2(s - jnp.max(s, axis=0, keepdims=True))
        pr = (e * (1.0 / jnp.sum(e, axis=0, keepdims=True))).astype(bf)
        p[slot + h] = pr
        probs.append(pr)
    o[rsl, c0 : c0 + 128] = dg(jnp.concatenate(probs, axis=0), stack(v, hd), 0, 0).astype(bf)


def att_bwd(qkv, do, p, dqkv, rsl, width, g, slot, hd):
    c0 = g * 128
    c1, c2 = c0 + width, c0 + 2 * width
    q = qkv[rsl, c0 : c0 + 128]
    k = qkv[rsl, c1 : c1 + 128]
    v = qkv[rsl, c2 : c2 + 128]
    d = do[rsl, c0 : c0 + 128]
    n = q.shape[0]
    probs = jnp.concatenate([p[slot + h] for h in range(128 // hd)], axis=0)
    every = nt(stack(v, hd), d)
    back = []
    for h in range(128 // hd):
        pf = probs[h * n : (h + 1) * n].astype(f32)
        t = pf * every[h * n : (h + 1) * n].astype(bf).astype(f32)
        back.append(((t - pf * jnp.sum(t, axis=0, keepdims=True)) * (hd ** -0.5)).astype(bf))
    back = jnp.concatenate(back, axis=0)
    dqkv[rsl, c0 : c0 + 128] = dg(back, stack(k, hd), 0, 0).astype(bf)
    dqkv[rsl, c1 : c1 + 128] = unstack(nn(back, q), hd).astype(bf)
    dqkv[rsl, c2 : c2 + 128] = unstack(nn(probs, d), hd).astype(bf)


def dec_kernel(scale, nb, y, codec, coder, pix, pos, sv, win, wout, hw,
               dy, win_out, wout_out, dhw, dsm, loss,
               dwin, dwout, x, t, xh1, xh2, xhf, rs1, rs2, rsf, tm, tr, a1, a2, u, o, qkv, p, hid, gp, dpr, d16, lacc):
    M = nb * DS
    R = M
    W = DD

    @pl.when(pl.program_id(0) == 0)
    def _():
        dsm[...] = jnp.zeros_like(dsm)
        loss[...] = jnp.zeros_like(loss)
        lacc[...] = jnp.zeros_like(lacc)
        for ref in (dwin, dwout, dhw):
            rows(ref.shape[0], 16, lambda r: ref.__setitem__((r, slice(None)), jnp.zeros((16, ref.shape[1]), f32)))

    def put(where, sums):
        for (i, lo), v in zip(where, sums):
            dsm[:, OFF[i] + lo : OFF[i] + lo + v.shape[1]] += v

    for b in range(nb):
        pick = (codec[b] == lax.broadcasted_iota(jnp.int32, (DS, SEL), 1)).astype(f32).astype(bf)
        tok = jnp.where(lax.broadcasted_iota(jnp.int32, (8, W), 0) == 0, part(sv, 13), 0.0)
        table = jnp.concatenate([y[b], jnp.zeros((8, W), f32), tok, jnp.zeros((8, W), f32)], axis=0)
        z = pos[...]
        for piece in pieces(table):
            z = z + nn(pick, piece)
        x[b * DS : (b + 1) * DS, :] = z

    def ln1(r):
        xh, rs, a = norm_rows(x[r, :], part(sv, 14), part(sv, 15))
        xh1[r, :] = xh
        rs1[r, :] = rs
        a1[r, :] = a.astype(bf)
    rows(M, R, ln1)

    qkv[:, 0:W] = (nn(a1[...], win[:, 0:W]) + sv[:, OFF[16] : OFF[16] + W]).astype(bf)
    qkv[:, W : 2 * W] = nn(a1[...], win[:, W : 2 * W]).astype(bf)
    qkv[:, 2 * W :] = (nn(a1[...], win[:, 2 * W : 3 * W]) + sv[:, OFF[16] + W : OFF[17]]).astype(bf)

    bias = jnp.where(lax.broadcasted_iota(jnp.int32, (DS, 1), 0) <= PATCHES, 0.0, -1e30).astype(f32)

    @pl.loop(0, nb)
    def _(i):
        rsl = pl.ds(pl.multiple_of(i * DS, 16), DS)
        for g in range(4):
            att_fwd(qkv, o, p, bias, rsl, W, g, i * 16 + g * 4, 32)

    x[...] += nn(o[...], win[:, 3 * W : 4 * W]) + part(sv, 17)

    def ln2(r):
        xh, rs, a = norm_rows(x[r, :], part(sv, 18), part(sv, 19))
        xh2[r, :] = xh
        rs2[r, :] = rs
        a2[r, :] = a.astype(bf)
    rows(M, R, ln2)

    CW = 512
    for c in range(0, DFF, CW):
        h = nn(a2[...], win[:, 4 * W + c : 4 * W + c + CW])
        g, dg_ = gelu_pair(h + sv[:, OFF[20] + c : OFF[20] + c + CW])
        hid[:, c : c + CW] = g.astype(bf)
        gp[:, c : c + CW] = dg_.astype(bf)

    x[...] += nt(hid[...], wout[...]) + part(sv, 21)

    def lnf(r):
        xh, rs, a = norm_rows(x[r, :], part(sv, 22), part(sv, 23))
        xhf[r, :] = xh
        rsf[r, :] = rs
        u[r, :] = a.astype(bf)
    rows(M, R, lnf)

    for b in range(nb):
        v = pix[b].astype(f32)
        m = jnp.mean(v, axis=1, keepdims=True)
        c = v - m
        tm[b * DS : (b + 1) * DS, :] = m
        tr[b * DS : (b + 1) * DS, :] = lax.rsqrt(jnp.mean(c * c, axis=1, keepdims=True) + 1e-06)

    for c in range(0, PIX, 256):
        pr = nn(u[...], hw[:, c : c + 256].astype(bf)) + sv[:, OFF[24] + c : OFF[24] + c + 256]
        for b in range(nb):
            sl = slice(b * DS, (b + 1) * DS)
            tgt = (pix[b, :, c : c + 256].astype(f32) - tm[sl, :]) * tr[sl, :]
            diff = jnp.where(codec[b] == 64, pr[sl] - tgt, 0.0)
            lacc[...] += rsum(diff * diff)
            dp = diff * (2.0 * scale / PIX)
            dsm[:, OFF[24] + c : OFF[24] + c + 256] += rsum(dp)
            dpr[sl, c : c + 256] = dp.astype(bf)

    dhw[...] += dg(u[...], dpr[...], 0, 0)
    t[...] = nt(dpr[...], hw[...].astype(bf))

    def lnfb(r):
        da = t[r, :]
        xh = xhf[r, :]
        dx = norm_back(da, xh, rsf[r, :], part(sv, 22))
        x[r, :] = dx
        d16[r, :] = dx.astype(bf)
        return da * xh, da, dx
    put([(22, 0), (23, 0), (21, 0)], rows_sum(M, R, [W] * 3, lnfb))

    dwout[...] += dg(d16[...], hid[...], 0, 0)
    for c in range(0, DFF, CW):
        dh = nn(d16[...], wout[:, c : c + CW]) * gp[:, c : c + CW].astype(f32)
        dsm[:, OFF[20] + c : OFF[20] + c + CW] += rsum(dh)
        gp[:, c : c + CW] = dh.astype(bf)
    dwin[:, 4 * W :] += dg(a2[...], gp[...], 0, 0)
    t[...] = nt(gp[...], win[:, 4 * W :])

    def ln2b(r):
        da = t[r, :]
        xh = xh2[r, :]
        dx = x[r, :] + norm_back(da, xh, rs2[r, :], part(sv, 18))
        x[r, :] = dx
        d16[r, :] = dx.astype(bf)
        return da * xh, da, dx
    put([(18, 0), (19, 0), (17, 0)], rows_sum(M, R, [W] * 3, ln2b))

    dwin[:, 3 * W : 4 * W] += dg(o[...], d16[...], 0, 0)
    o[...] = nt(d16[...], win[:, 3 * W : 4 * W]).astype(bf)
    dqkv = gp

    @pl.loop(0, nb)
    def _(i):
        rsl = pl.ds(pl.multiple_of(i * DS, 16), DS)
        for g in range(4):
            att_bwd(qkv, o, p, dqkv, rsl, W, g, i * 16 + g * 4, 32)

    dwin[:, 0 : 3 * W] += dg(a1[...], dqkv[:, 0 : 3 * W], 0, 0)
    put([(16, 0), (16, W)], rows_sum(M, R, [W, W], lambda r: [dqkv[r, 0:W].astype(f32), dqkv[r, 2 * W : 3 * W].astype(f32)]))
    t[...] = nt(dqkv[:, 0 : 3 * W], win[:, 0 : 3 * W])

    def ln1b(r):
        da = t[r, :]
        xh = xh1[r, :]
        x[r, :] = x[r, :] + norm_back(da, xh, rs1[r, :], part(sv, 14))
        return da * xh, da
    put([(14, 0), (15, 0)], rows_sum(M, R, [W] * 2, ln1b))

    for b in range(nb):
        pick = (coder[b] == lax.broadcasted_iota(jnp.int32, (SEL, DS), 0)).astype(f32).astype(bf)
        out = None
        for piece in pieces(x[b * DS : (b + 1) * DS, :]):
            v = nn(pick, piece)
            out = v if out is None else out + v
        dy[b] = out[0:ES]
        dsm[:, OFF[13] : OFF[14]] += out[64:65]

    @pl.when(pl.program_id(0) == pl.num_programs(0) - 1)
    def _():
        loss[...] = jnp.broadcast_to(jnp.sum(lacc[...], axis=1, keepdims=True) * (scale / PIX), (1, 128))
        for src, dst in ((dwin, win_out), (dwout, wout_out)):
            rows(DD, 16, lambda r: dst.__setitem__((r, slice(None)), src[r, :].astype(bf)))


def decoder(y, codec, coder, pix, pos, sv, win, wout, hw, scale, nb=2):
    n = y.shape[0]
    M = nb * DS
    whole = lambda a: pl.BlockSpec(a.shape, lambda i: (0,) * a.ndim, pipeline_mode=pl.Buffered(1))
    fixed = lambda s: pl.BlockSpec(s, lambda i: (0,) * len(s), pipeline_mode=pl.Buffered(1))
    blk = lambda s: pl.BlockSpec((nb,) + s, lambda i: (i, 0, 0))
    V = pltpu.VMEM
    return pl.pallas_call(
        functools.partial(dec_kernel, scale, nb),
        grid=(n // nb,),
        in_specs=[blk((ES, DD)), blk((DS, 1)), blk((1, DS)), blk((DS, PIX)), whole(pos), whole(sv), whole(win), whole(wout), whole(hw)],
        out_specs=[blk((ES, DD)), fixed(win.shape), fixed(wout.shape), fixed(hw.shape), fixed((1, SMALL)), fixed((1, 128))],
        out_shape=[
            jax.ShapeDtypeStruct((n, ES, DD), f32), jax.ShapeDtypeStruct(win.shape, bf),
            jax.ShapeDtypeStruct(wout.shape, bf), jax.ShapeDtypeStruct(hw.shape, f32),
            jax.ShapeDtypeStruct((1, SMALL), f32), jax.ShapeDtypeStruct((1, 128), f32)],
        scratch_shapes=[
            V(win.shape, f32), V(wout.shape, f32),
            V((M, DD), f32), V((M, DD), f32), V((M, DD), f32), V((M, DD), f32), V((M, DD), f32),
            V((M, 1), f32), V((M, 1), f32), V((M, 1), f32), V((M, 1), f32), V((M, 1), f32),
            V((M, DD), bf), V((M, DD), bf), V((M, DD), bf), V((M, DD), bf), V((M, 3 * DD), bf),
            V((nb * DHEADS, DS, DS), bf), V((M, DFF), bf), V((M, DFF), bf), V((M, PIX), bf), V((M, DD), bf),
            V((1, 256), f32)],
        compiler_params=pltpu.CompilerParams(vmem_limit_bytes=60 << 20),
        name="decoder",
    )(y, codec, coder, pix, pos, sv, win, wout, hw)


class Place:
    def __init__(self, nrow, ncol):
        side = math.isqrt(nrow)
        self.nrow, self.ncol = nrow, ncol
        self.n = {"x": side, "y": nrow // side, "z": ncol // 2}
        row, col = lax.axis_index("row"), lax.axis_index("col")
        self.at = {"x": row % side, "y": row // side, "z": col // 2, "core": col % 2}

    def moved(self, **by):
        at = {}
        for k, v in self.at.items():
            step = by.get(k, 0)
            size = 2 if k == "core" else self.n[k]
            at[k] = v if step == 0 else lax.rem(v + (step % size), size)
        return at["y"] * self.n["x"] + at["x"], at["z"] * 2 + at["core"]

    def greet(self):
        sem = pltpu.get_barrier_semaphore()
        count = 0
        for axis in ("x", "y", "z", "core"):
            size = 2 if axis == "core" else self.n[axis]
            for step in sorted({1 % size, (size - 1) % size} - {0}):
                pl.semaphore_signal(sem, inc=1, device_id=self.moved(**{axis: step}), device_id_type=pl.DeviceIdType.MESH)
                count += 1
        pl.semaphore_wait(sem, count)


class Shapes:
    def __init__(self, nrow, ncol):
        self.nrow, self.ncol = nrow, ncol
        self.awide, self.bwide = (5 * D + FF + DD) // ncol, FF // nrow
        self.alanes, self.blanes = self.window(self.awide, ncol), self.window(self.bwide, nrow)
        self.arows, self.brows = D // nrow, D // ncol
        self.crows, self.clanes = DD // nrow, 4 * DD // ncol + DFF // ncol
        self.drows, self.dlanes = DD // ncol, DFF // nrow
        self.erows = -(-(DD * PIX + SMALL) // (nrow * ncol * 256 * 8)) * 8
        self.blocks = {"A": (self.arows, self.alanes), "B": (self.brows, self.blanes), "C": (self.crows, self.clanes), "D": (self.drows, self.dlanes)}

    @staticmethod
    def window(wide, count):
        return max(-(-((wide * c) % 128 + wide) // 128) * 128 for c in range(count))

    def start(self, which, index):
        wide, lanes, total = (self.awide, self.alanes, 5 * D + FF + DD) if which == "A" else (self.bwide, self.blanes, FF)
        first = (wide * index) // 128
        last = (total - lanes) // 128
        if isinstance(index, int):
            return min(first, last) * 128
        return jnp.minimum(first, last) * 128


STREAMS = (("A",), ("B", "C", "D"))
ORDER = (("x", "y"), ("y", "x"))


def gather_kernel(nrow, ncol, ain, bin_, cin, din, aout, bout, cout, dout, send, recv, csend, crecv, lsem):
    place = Place(nrow, ncol)
    sh = Shapes(nrow, ncol)
    ins = {"A": ain, "B": bin_, "C": cin, "D": din}
    mats = "ABCD"

    def spot(m, row, col):
        if m == "A":
            return aout.at[col, pl.ds(pl.multiple_of(row * sh.arows, 16), sh.arows), :]
        if m == "B":
            return bout.at[row, pl.ds(pl.multiple_of(col * sh.brows, 16), sh.brows), :]
        if m == "C":
            return cout.at[pl.ds(pl.multiple_of(row * sh.crows, 16), sh.crows), pl.ds(pl.multiple_of(col * sh.clanes, 128), sh.clanes)]
        return dout.at[pl.ds(pl.multiple_of(col * sh.drows, 16), sh.drows), pl.ds(pl.multiple_of(row * sh.dlanes, 128), sh.dlanes)]

    nz = place.n["z"]
    place.greet()
    me = place.moved()
    locals_ = [pltpu.make_async_copy(ins[m], spot(m, *me), lsem.at[i]) for i, m in enumerate(mats)]
    for c in locals_:
        c.start()
    steps = []
    for s in (0, 1):
        p, q = ORDER[s]
        for i in range(place.n[q]):
            for j in range(place.n[p]):
                for k in range(nz):
                    steps.append((i + j + k, k, s, i, j, k))
    steps.sort()
    sent = []
    late = []
    for _, _, s, i, j, k in steps:
        p, q = ORDER[s]
        npp, nq = place.n[p], place.n[q]
        slot = (i * npp + j) * nz + k
        own = i == j == k == 0
        for m in STREAMS[s]:
            mi = mats.index(m)
            dst = spot(m, *place.moved(**{q: -i, p: -j, "z": -k}))
            src = ins[m] if own else dst
            if not own:
                pltpu.make_async_remote_copy(dst, dst, send.at[mi, slot], recv.at[mi, slot], device_id=place.moved(core=1), device_id_type=pl.DeviceIdType.MESH).wait_recv()
            plan = []
            if i == j == 0 and k < nz - 1:
                plan.append(({"z": 1}, slot + 1))
            if i == 0 and j < npp - 1:
                plan.append(({p: 1}, slot + nz))
            if i < nq - 1:
                plan.append(({q: 1}, slot + nz * npp))
            for by, there in plan:
                c = pltpu.make_async_remote_copy(src, dst, send.at[mi, there], recv.at[mi, there], device_id=place.moved(**by), device_id_type=pl.DeviceIdType.MESH)
                c.start()
                sent.append(c)
            c = pltpu.make_async_remote_copy(src, dst, csend.at[mi, slot], crecv.at[mi, slot], device_id=place.moved(core=1), device_id_type=pl.DeviceIdType.MESH)
            c.start()
            sent.append(c)
            other = spot(m, *place.moved(**{q: -i, p: -j, "z": -k, "core": 1}))
            late.append(pltpu.make_async_remote_copy(other, other, csend.at[mi, slot], crecv.at[mi, slot], device_id=place.moved(core=1), device_id_type=pl.DeviceIdType.MESH))
    for c in late:
        c.wait_recv()
    for c in sent:
        c.wait_send()
    for c in locals_:
        c.wait()


def gather_weights(nrow, ncol, ain, bin_, cin, din):
    sh = Shapes(nrow, ncol)
    half = nrow * ncol // 2
    S = jax.ShapeDtypeStruct
    anyspec = pl.BlockSpec(memory_space=pl.ANY)
    sem = pltpu.SemaphoreType.DMA
    return pl.pallas_call(
        functools.partial(gather_kernel, nrow, ncol),
        in_specs=[anyspec] * 4, out_specs=[anyspec] * 4,
        out_shape=[S((ncol, D, sh.alanes), bf), S((nrow, D, sh.blanes), bf), S((DD, 4 * DD + DFF), bf), S((DD, DFF), bf)],
        scratch_shapes=[sem((4, half)), sem((4, half)), sem((4, half)), sem((4, half)), sem((4,))],
        compiler_params=pltpu.CompilerParams(collective_id=0, has_side_effects=True),
        name="gather_weights",
    )(ain, bin_, cin, din)


RSTREAMS = (("A",), ("B", "C", "D", "E"))


def reduce_kernel(nrow, ncol, da, db, dc, dd, de, loss,
                  ga, gb, gc, gd, eall, *scratch):
    mats = "ABCDE"
    acc, sib, rq, rp, rz = (dict(zip(mats, scratch[5 * t : 5 * t + 5])) for t in range(5))
    ge, lsem, csend, crecv, send, qrecv, prec, zrecv, esend, erecv, ecs, ecr = scratch[25:]
    place = Place(nrow, ncol)
    sh = Shapes(nrow, ncol)
    nz = place.n["z"]
    ins = {"A": da, "B": db, "C": dc, "D": dd, "E": de}
    outs = {"A": ga, "B": gb, "C": gc, "D": gd}

    def spot(m, row, col):
        if m == "A":
            return da.at[pl.ds(pl.multiple_of(row * sh.arows, 16), sh.arows), pl.ds(pl.multiple_of(sh.start("A", col), 128), sh.alanes)]
        if m == "B":
            return db.at[pl.ds(pl.multiple_of(col * sh.brows, 16), sh.brows), pl.ds(pl.multiple_of(sh.start("B", row), 128), sh.blanes)]
        if m == "C":
            return dc.at[pl.ds(pl.multiple_of(row * sh.crows, 16), sh.crows), pl.ds(pl.multiple_of(col * sh.clanes, 128), sh.clanes)]
        if m == "D":
            return dd.at[pl.ds(pl.multiple_of(col * sh.drows, 16), sh.drows), pl.ds(pl.multiple_of(row * sh.dlanes, 128), sh.dlanes)]
        return de.at[row * ncol + col]

    place.greet()

    def remote(src, dst, ssem, rsem, **by):
        return pltpu.make_async_remote_copy(src, dst, ssem, rsem, device_id=place.moved(**by), device_id_type=pl.DeviceIdType.MESH)

    steps = []
    for s in (0, 1):
        p, q = ORDER[s]
        for i in range(place.n[q]):
            for j in range(place.n[p]):
                for k in range(nz):
                    steps.append(((place.n[q] - 1 - i) + (place.n[p] - 1 - j) + (nz - 1 - k), s, i, j, k))
    steps.sort()
    sent = []
    loads = {}
    for _, s, i, j, k in steps:
        p, q = ORDER[s]
        slot = (i * place.n[p] + j) * nz + k
        for m in RSTREAMS[s]:
            mi = mats.index(m)
            c = remote(spot(m, *place.moved(**{q: -i, p: -j, "z": -k, "core": 1})), sib[m].at[slot], csend.at[mi, slot], crecv.at[mi, slot], core=1)
            c.start()
            sent.append(c)
            loads[m, slot] = pltpu.make_async_copy(spot(m, *place.moved(**{q: -i, p: -j, "z": -k})), acc[m].at[slot], lsem.at[mi, slot])
            loads[m, slot].start()
    for _, s, i, j, k in steps:
        p, q = ORDER[s]
        npp, nq = place.n[p], place.n[q]
        slot = (i * npp + j) * nz + k
        for m in RSTREAMS[s]:
            mi = mats.index(m)
            loads[m, slot].wait()
            remote(sib[m].at[slot], sib[m].at[slot], csend.at[mi, slot], crecv.at[mi, slot], core=1).wait_recv()
            terms = [(acc[m], slot), (sib[m], slot)]
            if i < nq - 1:
                remote(rq[m].at[slot], rq[m].at[slot], send.at[mi, slot], qrecv.at[mi, slot], core=1).wait_recv()
                terms.append((rq[m], slot))
            if i == 0 and j < npp - 1:
                remote(rp[m].at[slot], rp[m].at[slot], send.at[mi, slot], prec.at[mi, slot], core=1).wait_recv()
                terms.append((rp[m], slot))
            if i == j == 0 and k < nz - 1:
                remote(rz[m].at[slot], rz[m].at[slot], send.at[mi, slot], zrecv.at[mi, slot], core=1).wait_recv()
                terms.append((rz[m], slot))
            last = i == j == k == 0
            total = acc[m].shape[1]
            size = 8 if m == "E" else 16

            def add(r, m=m, terms=terms, last=last, slot=slot):
                v = terms[0][0][slot, r, :].astype(f32)
                for ref, at in terms[1:]:
                    v = v + ref[at, r, :].astype(f32)
                if not last:
                    acc[m][slot, r, :] = v.astype(acc[m].dtype)
                elif m == "E":
                    ge[pl.ds(0, total), :] = v
                else:
                    outs[m][r, :] = v
            if m == "E":
                add(slice(None))
            else:
                rows(total, size, add)
            if last:
                continue
            if i > 0:
                c = remote(acc[m].at[slot], rq[m].at[slot - npp * nz], send.at[mi, slot], qrecv.at[mi, slot - npp * nz], **{q: -1})
            elif j > 0:
                c = remote(acc[m].at[slot], rp[m].at[slot - nz], send.at[mi, slot], prec.at[mi, slot - nz], **{p: -1})
            else:
                c = remote(acc[m].at[slot], rz[m].at[slot - 1], send.at[mi, slot], zrecv.at[mi, slot - 1], z=-1)
            c.start()
            sent.append(c)


    row, col = place.moved()
    la = lax.broadcasted_iota(jnp.int32, (1, sh.alanes), 1) + (sh.start("A", col) - col * sh.awide)
    lb = lax.broadcasted_iota(jnp.int32, (1, sh.blanes), 1) + (sh.start("B", row) - row * sh.bwide)
    va = jnp.where((la >= 0) & (la < sh.awide), ga[...], 0.0)
    vb = jnp.where((lb >= 0) & (lb < sh.bwide), gb[...], 0.0)
    er = sh.erows
    sq = jnp.zeros((1, 128), f32)
    for v in (va, vb, gc[...], gd[...], ge[0:er, :]):
        w = rsum(v * v)
        for c0 in range(0, w.shape[1], 128):
            sq = sq + w[:, c0 : c0 + 128]
    ge[er : er + 8, :] = jnp.concatenate([jnp.broadcast_to(sq, (8, 128)), jnp.broadcast_to(loss[...], (8, 128))], axis=1)

    def espot(**by):
        r, c = place.moved(**by)
        return eall.at[r * ncol + c]

    eall[row * ncol + col] = ge[...]
    npp, nq = place.n["x"], place.n["y"]
    esteps = sorted((i + j + k, k, i, j) for i in range(nq) for j in range(npp) for k in range(nz))
    late = []
    for _, k, i, j in esteps:
        slot = (i * npp + j) * nz + k
        own = i == j == k == 0
        dst = espot(y=-i, x=-j, z=-k)
        src = ge if own else dst
        if not own:
            remote(dst, dst, esend.at[slot], erecv.at[slot], core=1).wait_recv()
        plan = []
        if i == j == 0 and k < nz - 1:
            plan.append(({"z": 1}, slot + 1))
        if i == 0 and j < npp - 1:
            plan.append(({"x": 1}, slot + nz))
        if i < nq - 1:
            plan.append(({"y": 1}, slot + nz * npp))
        for by, there in plan:
            c = remote(src, dst, esend.at[there], erecv.at[there], **by)
            c.start()
            sent.append(c)
        c = remote(src, dst, ecs.at[slot], ecr.at[slot], core=1)
        c.start()
        sent.append(c)
        other = espot(y=-i, x=-j, z=-k, core=1)
        late.append(remote(other, other, ecs.at[slot], ecr.at[slot], core=1))
    for c in late:
        c.wait_recv()
    for c in sent:
        c.wait_send()


def reduce_grads(nrow, ncol, da, db, dc, dd, de, loss):
    sh = Shapes(nrow, ncol)
    half = nrow * ncol // 2
    side = math.isqrt(nrow)
    n = {"x": side, "y": nrow // side, "z": ncol // 2}
    S = jax.ShapeDtypeStruct
    V = pltpu.VMEM
    anyspec = pl.BlockSpec(memory_space=pl.ANY)
    vm = pl.BlockSpec(memory_space=pltpu.VMEM)
    sem = pltpu.SemaphoreType.DMA
    kinds = [sh.blocks[m] + (bf,) for m in "ABCD"] + [(sh.erows, 256, f32)]
    order = [ORDER[s] for s in (0, 1, 1, 1, 1)]
    nz = n["z"]
    scratch = []
    for count in (
        lambda p, q: half, lambda p, q: half, lambda p, q: (n[q] - 1) * n[p] * nz,
        lambda p, q: (n[p] - 1) * nz, lambda p, q: nz - 1,
    ):
        scratch += [V((count(p, q), r, l), t) for (r, l, t), (p, q) in zip(kinds, order)]
    scratch += [V((sh.erows + 8, 256), f32)]
    big = n["x"] * n["y"] * nz - min(n["x"], n["y"]) * nz
    scratch += [sem((5, half))] * 4 + [sem((5, big)), sem((5, max(n["x"], n["y"]) * nz)), sem((5, nz))] + [sem((half,))] * 4
    return pl.pallas_call(
        functools.partial(reduce_kernel, nrow, ncol),
        in_specs=[anyspec] * 5 + [vm], out_specs=[vm] * 5,
        out_shape=[S(sh.blocks[m], f32) for m in "ABCD"] + [S((nrow * ncol, sh.erows + 8, 256), f32)],
        scratch_shapes=scratch,
        compiler_params=pltpu.CompilerParams(collective_id=1, has_side_effects=True, vmem_limit_bytes=60 << 20),
        name="reduce_grads",
    )(da, db, dc, dd, de, loss)


def windows(nrow, ncol, weights):
    sh = Shapes(nrow, ncol)
    row, col = lax.axis_index("row"), lax.axis_index("col")

    def put(v, which, index, wide, lanes):
        if wide == lanes:
            return v
        shift = index * wide - sh.start(which, index)
        return lax.dynamic_update_slice(jnp.zeros((v.shape[0], lanes), v.dtype), v, (0, shift))
    a, b, c, d = (w.astype(bf) for w in weights)
    return put(a, "A", col, sh.awide, sh.alanes), put(b.T, "B", row, sh.bwide, sh.blanes), c, d.T


def unwindow(nrow, ncol, ga, gb, gc, gd):
    sh = Shapes(nrow, ncol)
    row, col = lax.axis_index("row"), lax.axis_index("col")

    def take(v, which, index, wide, lanes):
        if wide == lanes:
            return v
        return lax.dynamic_slice(v, (0, index * wide - sh.start(which, index)), (v.shape[0], wide))
    return take(ga, "A", col, sh.awide, sh.alanes), take(gb, "B", row, sh.bwide, sh.blanes).T, gc, gd.T


def tile_plan(sh, which):
    wide, count = (sh.awide, sh.ncol) if which == "A" else (sh.bwide, sh.nrow)
    alone, shared = [], []
    for c in range(count):
        first, end = wide * c // 128, -(-(wide * (c + 1)) // 128)
        base = sh.start(which, c) // 128
        lo = first + 1 if (wide * c) % 128 else first
        hi = end - 1 if (wide * (c + 1)) % 128 else end
        alone.append((c, lo, hi, base))
        if hi < end:
            shared.append((c, hi, base, sh.start(which, c + 1) // 128))
    return alone, shared


MOST = 6


def joiner(sh, which, src, dst, tmp, sem):
    alone, shared = tile_plan(sh, which)
    copies = []
    for c, lo, hi, at in alone:
        copies.append((src.at[c, :, pl.ds((lo - at) * 128, (hi - lo) * 128)], dst.at[:, pl.ds(lo * 128, (hi - lo) * 128)]))
    for u, (c, t, at, nxt) in enumerate(shared):
        copies.append((src.at[c, :, pl.ds((t - at) * 128, 128)], dst.at[:, pl.ds(t * 128, 128)]))
        copies.append((src.at[c + 1, :, pl.ds((t - nxt) * 128, 128)], tmp.at[u % MOST]))
    late = {len(alone) + 2 * u + 1 for u in range(MOST, len(shared))}
    make = lambda i: pltpu.make_async_copy(*copies[i], sem.at[i])
    made = [make(i) for i in range(len(copies)) if i not in late]
    for m in made:
        m.start()

    def end():
        for m in made:
            m.wait()
        for u, (c, t, at, nxt) in enumerate(shared):
            if u >= MOST:
                m = make(len(alone) + 2 * u + 1)
                m.start()
                m.wait()
            dst[:, t * 128 : (t + 1) * 128] += tmp[u % MOST]
    return end


def joiner_scratch(sh):
    V = pltpu.VMEM
    counts = [(len(a), len(s)) for a, s in (tile_plan(sh, "A"), tile_plan(sh, "B"))]
    return [V((D, 5 * D + FF + DD), bf), V((D, FF), bf)] + [V((min(max(s, 1), MOST), D, 128), bf) for _, s in counts] + [
        pltpu.SemaphoreType.DMA((a + 2 * s,)) for a, s in counts]


EG = 4 * ES
O_Q, O_P, O_F, O_E = D, 4 * D, 5 * D, 5 * D + FF


def enc_fwd_kernel(sh, pix, keepc, pos3, sv, awin, bwin,
                   y, kept, xh1, xh2, xhf, rs1, rs2, rsf, a1, a2, e16, o, qkv, p, hid, gp, x, bias, win, wout, atmp, btmp, asem, bsem):
    enda = joiner(sh, "A", awin, win, atmp, asem)
    endb = joiner(sh, "B", bwin, wout, btmp, bsem)
    n = pix.shape[0]
    M = n * ES
    R = M // 2
    W = D
    for i in range(0, n, 2):
        two = []
        for b in (i, i + 1):
            kc = keepc[b * ES : (b + 1) * ES, :]
            pick = (kc == lax.broadcasted_iota(jnp.int32, (ES, DS), 1)).astype(f32).astype(bf)
            two.append(nn(pick, pix[b]))
        kept[i * ES : (i + 2) * ES, :] = jnp.concatenate(two, axis=0).astype(bf)
    enda()
    for lo in range(0, M, EG):
        sl = slice(lo, lo + EG)
        kc = keepc[sl, :]
        pick = (kc == lax.broadcasted_iota(jnp.int32, (EG, DS), 1)).astype(f32).astype(bf)
        v = nn(kept[sl, :], win[:, 0:W]) + part(sv, 10)
        v = v + nn(pick, pos3[0:DS, :]) + nn(pick, pos3[DS : 2 * DS, :]) + nn(pick, pos3[2 * DS :, :])
        x[sl, :] = jnp.where(kc < PATCHES, v, jnp.where(kc == NOROW - 1, part(sv, 11), 0.0))

    def ln1(r):
        xh, rs, a = norm_rows(x[r, :], part(sv, 0), part(sv, 1))
        xh1[r, :] = xh
        rs1[r, :] = rs
        a1[r, :] = a.astype(bf)
    rows(M, R, ln1)
    qkv[:, 0:W] = (nn(a1[...], win[:, O_Q : O_Q + W]) + sv[:, OFF[2] : OFF[2] + W]).astype(bf)
    qkv[:, W : 2 * W] = nn(a1[...], win[:, O_Q + W : O_Q + 2 * W]).astype(bf)
    qkv[:, 2 * W :] = (nn(a1[...], win[:, O_Q + 2 * W : O_P]) + sv[:, OFF[2] + W : OFF[3]]).astype(bf)

    ki = lax.broadcasted_iota(jnp.int32, (EG, EG), 0)
    qi = lax.broadcasted_iota(jnp.int32, (EG, EG), 1)
    same = jnp.zeros((EG, EG), jnp.bool_)
    for j in range(4):
        same = same | ((ki >= j * ES) & (ki < j * ES + KEEP + 1) & (qi >= j * ES) & (qi < (j + 1) * ES))
    bias[...] = jnp.where(same, 0.0, -1e30).astype(f32)

    @pl.loop(0, n // 4)
    def _(i):
        rsl = pl.ds(pl.multiple_of(i * EG, 16), EG)
        for g in range(6):
            att_fwd(qkv, o, p, bias[...], rsl, W, g, i * 12 + g * 2, 64)

    x[...] += nn(o[...], win[:, O_P : O_P + W]) + part(sv, 3)

    def ln2(r):
        xh, rs, a = norm_rows(x[r, :], part(sv, 4), part(sv, 5))
        xh2[r, :] = xh
        rs2[r, :] = rs
        a2[r, :] = a.astype(bf)
    rows(M, R, ln2)

    for c in range(0, FF, 512):
        h = nn(a2[...], win[:, O_F + c : O_F + c + 512])
        g, dg_ = gelu_pair(h + sv[:, OFF[6] + c : OFF[6] + c + 512])
        hid[:, c : c + 512] = g.astype(bf)
        gp[:, c : c + 512] = dg_.astype(bf)
    endb()
    x[...] += nt(hid[...], wout[...]) + part(sv, 7)

    def lnf(r):
        xh, rs, a = norm_rows(x[r, :], part(sv, 8), part(sv, 9))
        xhf[r, :] = xh
        rsf[r, :] = rs
        e16[r, :] = a.astype(bf)
    rows(M, R, lnf)
    y[...] = nn(e16[...], win[:, O_E:]) + part(sv, 12)


def vspec(k):
    return [pl.BlockSpec(memory_space=pltpu.VMEM)] * k


def encoder_fwd(sh, pix, keepc, pos3, sv, awin, bwin):
    n = pix.shape[0]
    M = n * ES
    S = jax.ShapeDtypeStruct
    V = pltpu.VMEM
    outs = [S((M, DD), f32), S((M, D), bf), S((M, D), f32), S((M, D), f32), S((M, D), f32),
            S((M, 1), f32), S((M, 1), f32), S((M, 1), f32), S((M, D), bf), S((M, D), bf), S((M, D), bf), S((M, D), bf),
            S((M, 3 * D), bf), S((n // 4 * HEADS, EG, EG), bf), S((M, FF), bf), S((M, FF), bf)]
    return pl.pallas_call(
        functools.partial(enc_fwd_kernel, sh),
        in_specs=vspec(4) + [pl.BlockSpec(memory_space=pl.ANY)] * 2, out_specs=vspec(len(outs)), out_shape=outs,
        scratch_shapes=[V((M, D), f32), V((EG, EG), f32)] + joiner_scratch(sh),
        compiler_params=pltpu.CompilerParams(vmem_limit_bytes=60 << 20),
        name="encoder_fwd",
    )(pix, keepc, pos3, sv, awin, bwin)


def enc_bwd_kernel(sh, dy, keepc, sv, awin, bwin, kept, xh1_in, xh2, xhf_in, rs1, rs2, rsf, a1_in, a2, e16_in, o, qkv, p, hid, gp,
                   dwin, dwout, dsm, x, t, d16, dh16, stage, xb, ab, sem, lsem, win, wout, atmp, btmp, asem, bsem):
    def fetch(i, src, dst):
        copy = pltpu.make_async_copy(src, dst, lsem.at[i])
        copy.start()
        return copy

    at_e, at_xhf = fetch(0, e16_in, ab), fetch(1, xhf_in, xb)
    enda = joiner(sh, "A", awin, win, atmp, asem)
    endb = joiner(sh, "B", bwin, wout, btmp, bsem)
    M = dy.shape[0]
    R = M // 2
    W = D
    dsm[...] = jnp.zeros_like(dsm)

    def save(where, sums):
        for (i, lo), v in zip(where, sums):
            dsm[:, OFF[i] + lo : OFF[i] + lo + v.shape[1]] += v

    shots = []

    def put(out, base, value):
        width = value.shape[1]
        slot = len(shots) % 2
        if len(shots) >= 2:
            shots[-2].wait()
        stage[slot, :, 0:width] = value.astype(bf)
        copy = pltpu.make_async_copy(stage.at[slot, :, pl.ds(0, width)], out.at[:, pl.ds(base, width)], sem.at[slot])
        copy.start()
        shots.append(copy)

    def emb(r):
        v = dy[r, :]
        d16[r, 0:DD] = v.astype(bf)
        return [v]
    save([(12, 0)], rows_sum(M, R, [DD], emb))
    at_e.wait()
    put(dwin, O_E, dg(ab[...], d16[:, 0:DD], 0, 0))
    at_a = fetch(2, a1_in, ab)
    enda()
    endb()
    t[...] = nt(d16[:, 0:DD], win[:, O_E:])

    at_xhf.wait()

    def lnfb(r):
        da = t[r, :]
        xh = xb[r, :]
        dx = norm_back(da, xh, rsf[r, :], part(sv, 8))
        x[r, :] = dx
        d16[r, :] = dx.astype(bf)
        return da * xh, da, dx
    save([(8, 0), (9, 0), (7, 0)], rows_sum(M, R, [W] * 3, lnfb))
    at_xh1 = fetch(3, xh1_in, xb)
    for c in range(0, FF, W):
        put(dwout, c, dg(d16[...], hid[:, c : c + W], 0, 0))
        dh = nn(d16[...], wout[:, c : c + W]) * gp[:, c : c + W].astype(f32)
        dsm[:, OFF[6] + c : OFF[6] + c + W] += rsum(dh)
        dh16[:, c : c + W] = dh.astype(bf)
        put(dwin, O_F + c, dg(a2[...], dh16[:, c : c + W], 0, 0))
    t[...] = nt(dh16[...], win[:, O_F:O_E])
    dqkv = dh16

    def ln2b(r):
        da = t[r, :]
        xh = xh2[r, :]
        dx = x[r, :] + norm_back(da, xh, rs2[r, :], part(sv, 4))
        x[r, :] = dx
        d16[r, :] = dx.astype(bf)
        return da * xh, da, dx
    save([(4, 0), (5, 0), (3, 0)], rows_sum(M, R, [W] * 3, ln2b))
    put(dwin, O_P, dg(o[...], d16[...], 0, 0))
    d16[...] = nt(d16[...], win[:, O_P:O_F]).astype(bf)

    @pl.loop(0, M // EG)
    def _(i):
        rsl = pl.ds(pl.multiple_of(i * EG, 16), EG)
        for g in range(6):
            att_bwd(qkv, d16, p, dqkv, rsl, W, g, i * 12 + g * 2, 64)

    at_a.wait()
    for c in range(0, 3 * D, W):
        put(dwin, O_Q + c, dg(ab[...], dqkv[:, c : c + W], 0, 0))
    save([(2, 0), (2, W)], rows_sum(M, R, [W, W], lambda r: [dqkv[r, 0:W].astype(f32), dqkv[r, 2 * W : 3 * W].astype(f32)]))
    t[...] = nt(dqkv[:, 0 : 3 * W], win[:, O_Q:O_P])
    at_xh1.wait()

    def ln1b(r):
        da = t[r, :]
        xh = xb[r, :]
        dx = x[r, :] + norm_back(da, xh, rs1[r, :], part(sv, 0))
        kc = keepc[r, :]
        only = jnp.where(kc < PATCHES, dx, 0.0)
        d16[r, :] = only.astype(bf)
        return da * xh, da, jnp.where(kc == NOROW - 1, dx, 0.0), only
    save([(0, 0), (1, 0), (11, 0), (10, 0)], rows_sum(M, R, [W] * 4, ln1b))
    put(dwin, 0, dg(kept[...], d16[...], 0, 0))
    for c in shots[-2:]:
        c.wait()


def encoder_bwd(sh, dy, keepc, sv, awin, bwin, saved):
    M = dy.shape[0]
    S = jax.ShapeDtypeStruct
    V = pltpu.VMEM
    anyspec = pl.BlockSpec(memory_space=pl.ANY)
    return pl.pallas_call(
        functools.partial(enc_bwd_kernel, sh),
        in_specs=[anyspec if i in (3, 4, 6, 8, 12, 14) else spec for i, spec in enumerate(vspec(5 + len(saved)))],
        out_specs=[anyspec, anyspec, pl.BlockSpec(memory_space=pltpu.VMEM)],
        out_shape=[S((D, 5 * D + FF + DD), bf), S((D, FF), bf), S((1, SMALL), f32)],
        scratch_shapes=[V((M, D), f32), V((M, D), f32), V((M, D), bf), V((M, FF), bf), V((2, D, D), bf), V((M, D), f32), V((M, D), bf),
                        pltpu.SemaphoreType.DMA((2,)), pltpu.SemaphoreType.DMA((4,))] + joiner_scratch(sh),
        compiler_params=pltpu.CompilerParams(vmem_limit_bytes=63 << 20),
        name="encoder_bwd",
    )(dy, keepc, sv, awin, bwin, *saved)


def sincos_np(width):
    quarter = width // 4
    freq = (1.0 / np.float32(10000.0) ** (np.arange(quarter, dtype=np.float32) / np.float32(quarter))).astype(np.float32)
    pos = np.arange(GRID * GRID)
    cp = (pos % GRID).astype(np.float32)[:, None] * freq[None, :]
    rp = (pos // GRID).astype(np.float32)[:, None] * freq[None, :]
    return np.concatenate([np.sin(cp), np.cos(cp), np.sin(rp), np.cos(rp)], axis=1).astype(np.float32)


def tables():
    dec = np.zeros((DS, DD), np.float32)
    dec[:PATCHES] = sincos_np(DD)
    enc = np.zeros((DS, D), np.float32)
    enc[:PATCHES] = sincos_np(D)
    b = ml_dtypes.bfloat16
    hi = enc.astype(b)
    mid = (enc - hi.astype(np.float32)).astype(b)
    lo = (enc - hi.astype(np.float32) - mid.astype(np.float32)).astype(b)
    return dec, np.concatenate([hi, mid, lo], axis=0)


def adamw(weight, first, second, grad):
    first = 0.9 * first + (1.0 - 0.9) * grad
    second = 0.999 * second + (1.0 - 0.999) * grad * grad
    first_hat = first / (1.0 - 0.9**STEP)
    second_hat = second / (1.0 - 0.999**STEP)
    weight = weight - 0.08 * (first_hat / (jnp.sqrt(second_hat) + 1e-08) + 0.05 * weight)
    return (weight, first, second)


def local(pixels, keep_idx, restore, *state):
    weights, firsts, seconds = state[0:6], state[6:12], state[12:18]
    nrow, ncol = lax.axis_size("row"), lax.axis_size("col")
    sh = Shapes(nrow, ncol)
    n = pixels.shape[0]
    denom = 1.0 * n * nrow * ncol * (PATCHES - KEEP)

    dec_pos, enc_pos = tables()
    pix = jnp.pad(pixels, ((0, 0), (0, DS - PATCHES), (0, 0)))
    fill = lambda count, value: jnp.full((n, count), value, jnp.int32)
    keepc = jnp.concatenate([keep_idx, fill(1, NOROW - 1), fill(ES - KEEP - 1, NOROW)], axis=1).reshape(n * ES, 1)
    code = jnp.concatenate([jnp.where(restore < KEEP, restore, 64), fill(1, KEEP), fill(DS - PATCHES - 1, NOROW)], axis=1)
    head, sv = weights[4], weights[5].reshape(1, SMALL)

    aw, bw, c, dt = gather_weights(nrow, ncol, *windows(nrow, ncol, weights[0:4]))
    y, *saved = encoder_fwd(sh, pix, keepc, jnp.asarray(enc_pos), sv, aw, bw)
    dy, dc, ddt, dhead, dsm_d, loss = decoder(
        y.reshape(n, ES, DD), code.reshape(n, DS, 1), code.reshape(n, 1, DS), pix, jnp.asarray(dec_pos), sv, c, dt, head, 1.0 / denom)
    da, dbt, dsm_e = encoder_bwd(sh, dy.reshape(n * ES, DD), keepc, sv, aw, bw, saved)

    count = nrow * ncol * sh.erows * 256
    flat = jnp.concatenate([dhead.reshape(-1), (dsm_d + dsm_e).reshape(-1), jnp.zeros((count - DD * PIX - SMALL,), f32)])
    ga, gb, gc, gd, ge = reduce_grads(nrow, ncol, da, dbt, dc, ddt, flat.reshape(nrow * ncol, sh.erows, 256), loss)
    flat = ge[:, : sh.erows].reshape(-1)
    grads = [*unwindow(nrow, ncol, ga, gb, gc, gd), flat[: DD * PIX].reshape(DD, PIX), flat[DD * PIX : DD * PIX + SMALL]]
    aux = jnp.sum(ge[:, sh.erows], axis=0)
    norm = jnp.sqrt(jnp.sum(aux[:128]))
    loss = aux[128]
    factor = 0.0001 / jnp.maximum(norm, 0.0001)
    done = [adamw(w, m, v, g * factor) for w, m, v, g in zip(weights, firsts, seconds, grads)]
    return tuple(d[0] for d in done) + tuple(d[1] for d in done) + tuple(d[2] for d in done) + (loss, norm)


def solution(mesh):
    both = P(("row", "col"))
    big = [P("row", "col")] * 4 + [P()] * 2
    return jax.shard_map(
        local,
        mesh=mesh,
        in_specs=(both, both, both, *big, *big, *big),
        out_specs=(*big, *big, *big, P(), P()),
        check_vma=False,
    )
```

```python
import functools
import math

import jax
import jax.numpy as jnp
import ml_dtypes
import numpy as np
from jax import lax
from jax.experimental import pallas as pl
from jax.experimental.pallas import tpu as pltpu
from jax.sharding import PartitionSpec as P

D = 768
HEADS = 12
FF = 3072
DD = 512
DHEADS = 16
DFF = 2048
PIX = 768
GRID = 14
PATCHES = 196
KEEP = 49
STEP = 10
SMALL = 21248
ES = 56
DS = 208
SEL = 80
NOROW = 255
f32 = jnp.float32
bf = jnp.bfloat16

LENS = [
    D, D, 2 * D, D, D, D, FF, D, D, D, D, D,
    DD, DD, DD, DD, 2 * DD, DD, DD, DD, DFF, DD, DD, DD, PIX,
]
OFF = [0]
for piece in LENS:
    OFF.append(OFF[-1] + piece)


def part(ref, i):
    return ref[:, OFF[i] : OFF[i + 1]]


def dg(a, b, ca, cb):
    return lax.dot_general(a, b, (((ca,), (cb,)), ((), ())), preferred_element_type=f32)


def nn(a, b):
    return dg(a, b, 1, 0)


def nt(a, b):
    return dg(a, b, 1, 1)


def rows(total, size, fn):
    @pl.loop(0, total // size)
    def _(i):
        fn(pl.ds(pl.multiple_of(i * size, size), size))


def rows_sum(total, size, widths, fn):
    def body(i, carry):
        parts = fn(pl.ds(pl.multiple_of(i * size, size), size))
        return tuple(c + jnp.sum(v.reshape(size // 8, 8, v.shape[1]), axis=0) for c, v in zip(carry, parts))
    carry = lax.fori_loop(0, total // size, body, tuple(jnp.zeros((8, w), f32) for w in widths))
    return [rsum(c) for c in carry]


def pieces(x):
    hi = x.astype(bf)
    rest = x - hi.astype(f32)
    mid = rest.astype(bf)
    low = (rest - mid.astype(f32)).astype(bf)
    return hi, mid, low


def gelu_pair(x):
    ax = jnp.abs(x)
    d = 1.0 + (0.3275911 * 0.7071067811865476) * ax
    r = pl.reciprocal(d, approx=True)
    t = r * (2.0 - d * r)
    e = jnp.exp(-0.5 * (x * x))
    poly = ((((0.5 * 1.061405429 * t - 0.5 * 1.453152027) * t + 0.5 * 1.421413741) * t
             - 0.5 * 0.284496736) * t + 0.5 * 0.254829592) * t
    q = poly * e
    phi = jnp.where(x >= 0.0, 1.0 - q, q)
    return x * phi, phi + x * (e * 0.3989422804014327)


def norm_rows(x, gain, shift):
    c = x - jnp.mean(x, axis=1, keepdims=True)
    rs = lax.rsqrt(jnp.mean(c * c, axis=1, keepdims=True) + 1e-06)
    xh = c * rs
    return xh, rs, xh * gain + shift


def norm_back(da, xh, rs, gain):
    g = da * gain
    m1 = jnp.mean(g, axis=1, keepdims=True)
    m2 = jnp.mean(g * xh, axis=1, keepdims=True)
    return rs * (g - m1 - xh * m2)


def rsum(x):
    return jnp.sum(x, axis=0, keepdims=True)


def lanes_of(x, h, hd):
    lane = lax.broadcasted_iota(jnp.int32, (1, 128), 1)
    return jnp.where((lane >= h * hd) & (lane < (h + 1) * hd), x, jnp.zeros_like(x))


def stack(x, hd):
    return jnp.concatenate([lanes_of(x, h, hd) for h in range(128 // hd)], axis=0)


def unstack(x, hd):
    n = x.shape[0] * hd // 128
    out = None
    for h in range(128 // hd):
        t = lanes_of(x[h * n : (h + 1) * n], h, hd)
        out = t if out is None else out + t
    return out


def att_fwd(qkv, o, p, bias, rsl, width, g, slot, hd):
    c0 = g * 128
    q = qkv[rsl, c0 : c0 + 128]
    k = qkv[rsl, c0 + width : c0 + width + 128]
    v = qkv[rsl, c0 + 2 * width : c0 + 2 * width + 128]
    n = q.shape[0]
    every = nt(stack(k, hd), q)
    probs = []
    for h in range(128 // hd):
        s = every[h * n : (h + 1) * n] * (hd ** -0.5 * 1.4426950408889634) + bias
        e = jnp.exp2(s - jnp.max(s, axis=0, keepdims=True))
        pr = (e * (1.0 / jnp.sum(e, axis=0, keepdims=True))).astype(bf)
        p[slot + h] = pr
        probs.append(pr)
    o[rsl, c0 : c0 + 128] = dg(jnp.concatenate(probs, axis=0), stack(v, hd), 0, 0).astype(bf)


def att_bwd(qkv, do, p, dqkv, rsl, width, g, slot, hd):
    c0 = g * 128
    c1, c2 = c0 + width, c0 + 2 * width
    q = qkv[rsl, c0 : c0 + 128]
    k = qkv[rsl, c1 : c1 + 128]
    v = qkv[rsl, c2 : c2 + 128]
    d = do[rsl, c0 : c0 + 128]
    n = q.shape[0]
    probs = jnp.concatenate([p[slot + h] for h in range(128 // hd)], axis=0)
    every = nt(stack(v, hd), d)
    back = []
    for h in range(128 // hd):
        pf = probs[h * n : (h + 1) * n].astype(f32)
        t = pf * every[h * n : (h + 1) * n].astype(bf).astype(f32)
        back.append(((t - pf * jnp.sum(t, axis=0, keepdims=True)) * (hd ** -0.5)).astype(bf))
    back = jnp.concatenate(back, axis=0)
    dqkv[rsl, c0 : c0 + 128] = dg(back, stack(k, hd), 0, 0).astype(bf)
    dqkv[rsl, c1 : c1 + 128] = unstack(nn(back, q), hd).astype(bf)
    dqkv[rsl, c2 : c2 + 128] = unstack(nn(probs, d), hd).astype(bf)


def dec_kernel(scale, nb, y, coder, pix, pos, sv, win, wout, hw,
               dy, win_out, wout_out, dhw, dsm, loss,
               dwin, dwout, x, t, xh1, xh2, xhf, rs1, rs2, rsf, tm, tr, a1, a2, u, o, qkv, p, hid, gp, dpr, d16, hide, lacc):
    M = nb * DS
    R = M
    W = DD

    @pl.when(pl.program_id(0) == 0)
    def _():
        dsm[...] = jnp.zeros_like(dsm)
        loss[...] = jnp.zeros_like(loss)
        lacc[...] = jnp.zeros_like(lacc)
        dpr[...] = jnp.zeros_like(dpr)
        for ref in (dwin, dwout, dhw):
            rows(ref.shape[0], 16, lambda r: ref.__setitem__((r, slice(None)), jnp.zeros((16, ref.shape[1]), f32)))

    def put(where, sums):
        for (i, lo), v in zip(where, sums):
            dsm[:, OFF[i] + lo : OFF[i] + lo + v.shape[1]] += v

    for b in range(nb):
        pick = (coder[b] == lax.broadcasted_iota(jnp.int32, (SEL, DS), 0)).astype(f32).astype(bf)
        tok = jnp.where(lax.broadcasted_iota(jnp.int32, (8, W), 0) == 0, part(sv, 13), 0.0)
        table = jnp.concatenate([y[b], jnp.zeros((8, W), f32), tok, jnp.zeros((8, W), f32)], axis=0)
        z = pos[...]
        for piece in pieces(table):
            z = z + dg(pick, piece, 0, 0)
        x[b * DS : (b + 1) * DS, :] = z
        mark = (lax.broadcasted_iota(jnp.int32, (SEL, 128), 0) == 64).astype(f32).astype(bf)
        hide[b * DS : (b + 1) * DS, :] = dg(pick, mark, 0, 0)[:, 0:1]

    def ln1(r):
        xh, rs, a = norm_rows(x[r, :], part(sv, 14), part(sv, 15))
        xh1[r, :] = xh
        rs1[r, :] = rs
        a1[r, :] = a.astype(bf)
    rows(M, R, ln1)

    qkv[:, 0:W] = (nn(a1[...], win[:, 0:W]) + sv[:, OFF[16] : OFF[16] + W]).astype(bf)
    qkv[:, W : 2 * W] = nn(a1[...], win[:, W : 2 * W]).astype(bf)
    qkv[:, 2 * W :] = (nn(a1[...], win[:, 2 * W : 3 * W]) + sv[:, OFF[16] + W : OFF[17]]).astype(bf)

    bias = jnp.where(lax.broadcasted_iota(jnp.int32, (DS, 1), 0) <= PATCHES, 0.0, -1e30).astype(f32)

    @pl.loop(0, nb)
    def _(i):
        rsl = pl.ds(pl.multiple_of(i * DS, 16), DS)
        for g in range(4):
            att_fwd(qkv, o, p, bias, rsl, W, g, i * 16 + g * 4, 32)

    x[...] += nn(o[...], win[:, 3 * W : 4 * W]) + part(sv, 17)

    def ln2(r):
        xh, rs, a = norm_rows(x[r, :], part(sv, 18), part(sv, 19))
        xh2[r, :] = xh
        rs2[r, :] = rs
        a2[r, :] = a.astype(bf)
    rows(M, R, ln2)

    CW = 512
    for c in range(0, DFF, CW):
        h = nn(a2[...], win[:, 4 * W + c : 4 * W + c + CW])
        g, dg_ = gelu_pair(h + sv[:, OFF[20] + c : OFF[20] + c + CW])
        hid[:, c : c + CW] = g.astype(bf)
        gp[:, c : c + CW] = dg_.astype(bf)

    x[...] += nt(hid[...], wout[...]) + part(sv, 21)

    def lnf(r):
        xh, rs, a = norm_rows(x[r, :], part(sv, 22), part(sv, 23))
        xhf[r, :] = xh
        rsf[r, :] = rs
        u[r, :] = a.astype(bf)
    rows(M, R, lnf)

    for b in range(nb):
        v = pix[b].astype(f32)
        m = jnp.mean(v, axis=1, keepdims=True)
        c = v - m
        tm[b * DS : b * DS + PATCHES, :] = m
        tr[b * DS : b * DS + PATCHES, :] = lax.rsqrt(jnp.mean(c * c, axis=1, keepdims=True) + 1e-06)

    for c in range(0, PIX, 256):
        pr = nn(u[...], hw[:, c : c + 256].astype(bf)) + sv[:, OFF[24] + c : OFF[24] + c + 256]
        for b in range(nb):
            sl = slice(b * DS, b * DS + PATCHES)
            tgt = (pix[b, :, c : c + 256].astype(f32) - tm[sl, :]) * tr[sl, :]
            diff = jnp.where(hide[sl, :] > 0.5, pr[sl] - tgt, 0.0)
            lacc[...] += rsum(diff * diff)
            dp = diff * (2.0 * scale / PIX)
            dsm[:, OFF[24] + c : OFF[24] + c + 256] += rsum(dp)
            dpr[sl, c : c + 256] = dp.astype(bf)

    for c in range(0, PIX, 256):
        dhw[2 * c : 2 * c + DD, :] += dg(u[...], dpr[:, c : c + 256], 0, 0)
    t[...] = nt(dpr[...], hw[...].astype(bf))

    def lnfb(r):
        da = t[r, :]
        xh = xhf[r, :]
        dx = norm_back(da, xh, rsf[r, :], part(sv, 22))
        x[r, :] = dx
        d16[r, :] = dx.astype(bf)
        return da * xh, da, dx
    put([(22, 0), (23, 0), (21, 0)], rows_sum(M, R, [W] * 3, lnfb))

    dwout[...] += dg(d16[...], hid[...], 0, 0)
    for c in range(0, DFF, CW):
        dh = nn(d16[...], wout[:, c : c + CW]) * gp[:, c : c + CW].astype(f32)
        dsm[:, OFF[20] + c : OFF[20] + c + CW] += rsum(dh)
        gp[:, c : c + CW] = dh.astype(bf)
    dwin[:, 4 * W :] += dg(a2[...], gp[...], 0, 0)
    t[...] = nt(gp[...], win[:, 4 * W :])

    def ln2b(r):
        da = t[r, :]
        xh = xh2[r, :]
        dx = x[r, :] + norm_back(da, xh, rs2[r, :], part(sv, 18))
        x[r, :] = dx
        d16[r, :] = dx.astype(bf)
        return da * xh, da, dx
    put([(18, 0), (19, 0), (17, 0)], rows_sum(M, R, [W] * 3, ln2b))

    dwin[:, 3 * W : 4 * W] += dg(o[...], d16[...], 0, 0)
    o[...] = nt(d16[...], win[:, 3 * W : 4 * W]).astype(bf)
    dqkv = gp

    @pl.loop(0, nb)
    def _(i):
        rsl = pl.ds(pl.multiple_of(i * DS, 16), DS)
        for g in range(4):
            att_bwd(qkv, o, p, dqkv, rsl, W, g, i * 16 + g * 4, 32)

    dwin[:, 0 : 3 * W] += dg(a1[...], dqkv[:, 0 : 3 * W], 0, 0)
    put([(16, 0), (16, W)], rows_sum(M, R, [W, W], lambda r: [dqkv[r, 0:W].astype(f32), dqkv[r, 2 * W : 3 * W].astype(f32)]))
    t[...] = nt(dqkv[:, 0 : 3 * W], win[:, 0 : 3 * W])

    def ln1b(r):
        da = t[r, :]
        xh = xh1[r, :]
        x[r, :] = x[r, :] + norm_back(da, xh, rs1[r, :], part(sv, 14))
        return da * xh, da
    put([(14, 0), (15, 0)], rows_sum(M, R, [W] * 2, ln1b))

    for b in range(nb):
        pick = (coder[b] == lax.broadcasted_iota(jnp.int32, (SEL, DS), 0)).astype(f32).astype(bf)
        out = None
        for piece in pieces(x[b * DS : (b + 1) * DS, :]):
            v = nn(pick, piece)
            out = v if out is None else out + v
        dy[b] = out[0:ES]
        dsm[:, OFF[13] : OFF[14]] += out[64:65]

    @pl.when(pl.program_id(0) == pl.num_programs(0) - 1)
    def _():
        loss[...] = jnp.broadcast_to(jnp.sum(lacc[...], axis=1, keepdims=True) * (scale / PIX), (1, 128))
        for src, dst in ((dwin, win_out), (dwout, wout_out)):
            rows(DD, 16, lambda r: dst.__setitem__((r, slice(None)), src[r, :].astype(bf)))


def decoder(y, coder, pix, pos, sv, win, wout, hw, scale, nb=2):
    n = y.shape[0]
    M = nb * DS
    whole = lambda a: pl.BlockSpec(a.shape, lambda i: (0,) * a.ndim, pipeline_mode=pl.Buffered(1))
    fixed = lambda s: pl.BlockSpec(s, lambda i: (0,) * len(s), pipeline_mode=pl.Buffered(1))
    blk = lambda s: pl.BlockSpec((nb,) + s, lambda i: (i, 0, 0))
    V = pltpu.VMEM
    return pl.pallas_call(
        functools.partial(dec_kernel, scale, nb),
        grid=(n // nb,),
        in_specs=[blk((ES, DD)), blk((1, DS)), blk((PATCHES, PIX)), whole(pos), whole(sv), whole(win), whole(wout), whole(hw)],
        out_specs=[blk((ES, DD)), fixed(win.shape), fixed(wout.shape), fixed((3 * DD, 256)), fixed((1, SMALL)), fixed((1, 128))],
        out_shape=[
            jax.ShapeDtypeStruct((n, ES, DD), f32), jax.ShapeDtypeStruct(win.shape, bf),
            jax.ShapeDtypeStruct(wout.shape, bf), jax.ShapeDtypeStruct((3 * DD, 256), f32),
            jax.ShapeDtypeStruct((1, SMALL), f32), jax.ShapeDtypeStruct((1, 128), f32)],
        scratch_shapes=[
            V(win.shape, f32), V(wout.shape, f32),
            V((M, DD), f32), V((M, DD), f32), V((M, DD), f32), V((M, DD), f32), V((M, DD), f32),
            V((M, 1), f32), V((M, 1), f32), V((M, 1), f32), V((M, 1), f32), V((M, 1), f32),
            V((M, DD), bf), V((M, DD), bf), V((M, DD), bf), V((M, DD), bf), V((M, 3 * DD), bf),
            V((nb * DHEADS, DS, DS), bf), V((M, DFF), bf), V((M, DFF), bf), V((M, PIX), bf), V((M, DD), bf), V((M, 1), f32),
            V((1, 256), f32)],
        compiler_params=pltpu.CompilerParams(vmem_limit_bytes=60 << 20),
        name="decoder",
    )(y, coder, pix, pos, sv, win, wout, hw)


class Place:
    def __init__(self, nrow, ncol):
        side = math.isqrt(nrow)
        self.nrow, self.ncol = nrow, ncol
        self.n = {"x": side, "y": nrow // side, "z": ncol // 2}
        row, col = lax.axis_index("row"), lax.axis_index("col")
        self.at = {"x": row % side, "y": row // side, "z": col // 2, "core": col % 2}

    def moved(self, **by):
        at = {}
        for k, v in self.at.items():
            step = by.get(k, 0)
            size = 2 if k == "core" else self.n[k]
            at[k] = v if step % size == 0 else lax.rem(v + (step % size), size)
        return at["y"] * self.n["x"] + at["x"], at["z"] * 2 + at["core"]

    def greet(self):
        sem = pltpu.get_barrier_semaphore()
        count = 0
        for axis in ("x", "y", "z", "core"):
            size = 2 if axis == "core" else self.n[axis]
            for step in range(1, size):
                pl.semaphore_signal(sem, inc=1, device_id=self.moved(**{axis: step}), device_id_type=pl.DeviceIdType.MESH)
                count += 1
        pl.semaphore_wait(sem, count)

    def remote(self, src, dst, ssem, rsem, **by):
        return pltpu.make_async_remote_copy(src, dst, ssem, rsem, device_id=self.moved(**by), device_id_type=pl.DeviceIdType.MESH)


ORDER = {
    "A0": ("z", "x", "y"), "A1": ("z", "y", "x"), "B": ("y", "x", "z"),
    "C": ("z", "x", "y"), "D": ("z", "y", "x"), "E": ("z", "y", "x"),
}
DIRECT = ("E",)


class Shapes:
    def __init__(self, nrow, ncol):
        self.nrow, self.ncol = nrow, ncol
        self.half = nrow * ncol // 2
        side = math.isqrt(nrow)
        self.n = {"x": side, "y": nrow // side, "z": ncol // 2}
        self.awide, self.bwide = (5 * D + FF + DD) // ncol, FF // nrow
        self.alanes, self.blanes = self.window(self.awide, ncol), self.window(self.bwide, nrow)
        self.arows, self.brows = D // nrow, D // ncol
        self.acut = self.arows // 32 * 16
        self.crows, self.clanes = DD // nrow, (4 * DD + DFF) // ncol
        self.drows, self.dlanes = DD // ncol, DFF // nrow
        self.erows = -(-(DD * PIX + SMALL) // (nrow * ncol * 256 * 8)) * 8
        self.blocks = {
            "A0": (self.acut, self.alanes), "A1": (self.arows - self.acut, self.alanes), "B": (self.brows, self.blanes),
            "C": (self.crows, self.clanes), "D": (self.drows, self.dlanes), "E": (self.erows, 256)}

    @staticmethod
    def window(wide, count):
        return max(-(-((wide * c) % 128 + wide) // 128) * 128 for c in range(count))

    def start(self, which, index):
        wide, lanes, total = (self.awide, self.alanes, 5 * D + FF + DD) if which == "A" else (self.bwide, self.blanes, FF)
        first = (wide * index) // 128
        last = (total - lanes) // 128
        if isinstance(index, int):
            return min(first, last) * 128
        return jnp.minimum(first, last) * 128

    def axes(self, m):
        return ORDER[m], tuple(self.n[a] for a in ORDER[m])

    def steps(self, mats, back):
        out = []
        for pos, m in enumerate(mats):
            _, (na, nb, nc) = self.axes(m)
            for i in range(nc):
                for j in range(nb):
                    for k in range(na):
                        key = (na - 1 - k) + (nb - 1 - j) + (nc - 1 - i) if back else i + j + (min(k, 1) if m in DIRECT else k)
                        out.append((key, pos, m, i, j, k))
        return [t[2:] for t in sorted(out)]

    def onward(self, m, i, j, k):
        (a, b, c), (na, nb, nc) = self.axes(m)
        slot = (i * nb + j) * na + k
        out = []
        if m in DIRECT and i == j == k == 0:
            out += [(a, t, t) for t in range(1, na)]
        if m not in DIRECT and i == j == 0 and k < na - 1:
            out.append((a, 1, slot + 1))
        if i == 0 and j < nb - 1:
            out.append((b, 1, slot + na))
        if i < nc - 1:
            out.append((c, 1, slot + na * nb))
        return slot, out


def spread(place, sh, mats, first, spot, send, recv, csend, crecv):
    sent, late = [], []
    for m, i, j, k in sh.steps(mats, False):
        (a, b, c), _ = sh.axes(m)
        slot, onward = sh.onward(m, i, j, k)
        by = {c: -i, b: -j, a: -k}
        dst = spot(m, *place.moved(**by))
        own = i == j == k == 0
        src = first(m) if own else dst
        if not own:
            place.remote(dst, dst, send[m].at[slot], recv[m].at[slot], core=1).wait_recv()
        for axis, far, there in onward:
            copy = place.remote(src, dst, send[m].at[there], recv[m].at[there], **{axis: far})
            copy.start()
            sent.append(copy)
        copy = place.remote(src, dst, csend[m].at[slot], crecv[m].at[slot], core=1)
        copy.start()
        sent.append(copy)
        other = spot(m, *place.moved(core=1, **by))
        late.append(place.remote(other, other, csend[m].at[slot], crecv[m].at[slot], core=1))
    for copy in late:
        copy.wait_recv()
    for copy in sent:
        copy.wait_send()


def block_at(sh, m, ref, row, col, gathered):
    mul = pl.multiple_of
    if m in ("A0", "A1"):
        skip = 0 if m == "A0" else sh.acut
        r = pl.ds(mul(row * sh.arows + skip, 16), sh.blocks[m][0])
        return ref.at[col, r, :] if gathered else ref.at[r, pl.ds(mul(sh.start("A", col), 128), sh.alanes)]
    if m == "B":
        r = pl.ds(mul(col * sh.brows, 16), sh.brows)
        return ref.at[row, r, :] if gathered else ref.at[r, pl.ds(mul(sh.start("B", row), 128), sh.blanes)]
    if m == "C":
        return ref.at[pl.ds(mul(row * sh.crows, 16), sh.crows), pl.ds(mul(col * sh.clanes, 128), sh.clanes)]
    if m == "D":
        return ref.at[pl.ds(mul(col * sh.drows, 16), sh.drows), pl.ds(mul(row * sh.dlanes, 128), sh.dlanes)]
    return ref.at[row * sh.ncol + col]


def gather_kernel(sh, mats, *refs):
    place = Place(sh.nrow, sh.ncol)
    whole = sorted({m[0] for m in mats})
    n = len(whole)
    ins, outs = dict(zip(whole, refs[:n])), dict(zip(whole, refs[n : 2 * n]))
    sems = refs[2 * n :]
    send, recv, csend, crecv = (dict(zip(mats, sems[t * len(mats) :])) for t in range(4))
    lsem = sems[4 * len(mats)]

    def spot(m, row, col):
        return block_at(sh, m, outs[m[0]], row, col, True)

    def first(m):
        if m == "A0":
            return ins["A"].at[pl.ds(0, sh.acut), :]
        if m == "A1":
            return ins["A"].at[pl.ds(sh.acut, sh.arows - sh.acut), :]
        return ins[m]

    place.greet()
    own = [pltpu.make_async_copy(first(m), spot(m, *place.moved()), lsem.at[i]) for i, m in enumerate(mats)]
    for copy in own:
        copy.start()
    spread(place, sh, mats, first, spot, send, recv, csend, crecv)
    for copy in own:
        copy.wait()


def gather_weights(sh, mats, *blocks):
    S = jax.ShapeDtypeStruct
    anyspec = pl.BlockSpec(memory_space=pl.ANY)
    sem = pltpu.SemaphoreType.DMA
    out = {"A": S((sh.ncol, D, sh.alanes), bf), "B": S((sh.nrow, D, sh.blanes), bf), "C": S((DD, 4 * DD + DFF), bf), "D": S((DD, DFF), bf)}
    out = [out[m] for m in sorted({m[0] for m in mats})]
    return pl.pallas_call(
        functools.partial(gather_kernel, sh, mats),
        in_specs=[anyspec] * len(out), out_specs=[anyspec] * len(out), out_shape=out,
        scratch_shapes=[sem((sh.half,))] * (4 * len(mats)) + [sem((len(mats),))],
        compiler_params=pltpu.CompilerParams(collective_id=0, has_side_effects=True),
        name="gather_weights",
    )(*blocks)


def reduce_kernel(sh, mats, *refs):
    refs = list(refs)

    def take(names):
        return {m: refs.pop(0) for m in names}
    whole = sorted({m[0] for m in mats})
    ins = take(whole)
    aux = refs.pop(0)
    outs = take([m for m in whole if m != "E"])
    eall = refs.pop(0)
    acc, sib, rc, rb, ra = (take(mats) for _ in range(5))
    csend, crecv, send, recv = (take(mats) for _ in range(4))
    ge, lsem, erecv, ecr = refs
    place = Place(sh.nrow, sh.ncol)

    def spot(m, row, col):
        return block_at(sh, m, ins[m[0]], row, col, False)

    place.greet()
    steps = sh.steps(mats, True)
    sent = []
    for m, i, j, k in steps:
        (a, b, c), _ = sh.axes(m)
        slot, _ = sh.onward(m, i, j, k)
        by = {c: -i, b: -j, a: -k}
        copy = place.remote(spot(m, *place.moved(core=1, **by)), sib[m].at[slot], csend[m].at[slot], crecv[m].at[slot], core=1)
        copy.start()
        sent.append((m, copy))
        pltpu.make_async_copy(spot(m, *place.moved(**by)), acc[m].at[slot], lsem.at[mats.index(m)]).start()
    for m in mats:
        pltpu.make_async_copy(acc[m], acc[m], lsem.at[mats.index(m)]).wait()
    for m, i, j, k in steps:
        (a, b, c), (na, nb, nc) = sh.axes(m)
        slot, onward = sh.onward(m, i, j, k)
        place.remote(sib[m].at[slot], sib[m].at[slot], csend[m].at[slot], crecv[m].at[slot], core=1).wait_recv()
        terms = [(sib[m], slot)]
        for axis, far, from_slot in onward:
            buf = {a: ra, b: rb, c: rc}[axis][m]
            here = from_slot - {a: 1, b: na, c: na * nb}[axis]
            place.remote(buf.at[here], buf.at[here], send[m].at[slot], recv[m].at[from_slot], core=1).wait_recv()
            terms.append((buf, here))
        last = i == j == k == 0
        total, lanes = sh.blocks[m]

        def add(r, m=m, terms=terms, last=last, slot=slot):
            v = acc[m][slot, r, :].astype(f32)
            for ref, here in terms:
                v = v + ref[here, r, :].astype(f32)
            if not last:
                acc[m][slot, r, :] = v.astype(acc[m].dtype)
            elif m == "E":
                ge[r, :] = v
            elif m == "A1":
                outs["A"][pl.ds(pl.multiple_of(r.start + sh.acut, 16), r.size), :] = v
            else:
                outs[m[0]][r, :] = v
        rows(total, 8 if m == "E" else (32 if total % 32 == 0 else 16), add)
        if last:
            continue
        if i > 0:
            axis, buf, there = c, rc, slot - na * nb
        elif j > 0:
            axis, buf, there = b, rb, slot - na
        else:
            axis, buf, there = a, ra, slot - 1
        far = k if m in DIRECT and buf is ra else 1
        copy = place.remote(acc[m].at[slot], buf[m].at[there], send[m].at[slot], recv[m].at[slot], **{axis: -far})
        copy.start()
        sent.append((m, copy))

    row, col = place.moved()
    la = lax.broadcasted_iota(jnp.int32, (1, sh.alanes), 1) + (sh.start("A", col) - col * sh.awide)
    lb = lax.broadcasted_iota(jnp.int32, (1, sh.blanes), 1) + (sh.start("B", row) - row * sh.bwide)
    er = sh.erows
    sq = jnp.zeros((1, 128), f32)
    values = [ge[0:er, :]]
    for m, ref in outs.items():
        v = ref[...]
        if m == "A":
            v = jnp.where((la >= 0) & (la < sh.awide), v, 0.0)
        if m == "B":
            v = jnp.where((lb >= 0) & (lb < sh.bwide), v, 0.0)
        values.append(v)
    for v in values:
        w = rsum(v * v)
        for c0 in range(0, w.shape[1], 128):
            sq = sq + w[:, c0 : c0 + 128]
    ge[er : er + 8, :] = jnp.concatenate([jnp.broadcast_to(sq, (8, 128)), jnp.broadcast_to(aux[...], (8, 128))], axis=1)
    eall[row * sh.ncol + col] = ge[...]
    for m, copy in sent:
        copy.wait_send()
    one = lambda v: {"E": v}
    spread(place, sh, ["E"], lambda m: ge, lambda m, r, c: eall.at[r * sh.ncol + c], one(send["E"]), one(erecv), one(csend["E"]), one(ecr))


def reduce_grads(sh, mats, aux, *grads):
    S = jax.ShapeDtypeStruct
    V = pltpu.VMEM
    anyspec = pl.BlockSpec(memory_space=pl.ANY)
    vm = pl.BlockSpec(memory_space=pltpu.VMEM)
    sem = pltpu.SemaphoreType.DMA
    whole = [m for m in sorted({m[0] for m in mats}) if m != "E"]
    outs = {"A": (sh.arows, sh.alanes)} | {m: sh.blocks[m] for m in "BCD"}
    scratch = []
    for count in (
        lambda na, nb, nc: na * nb * nc, lambda na, nb, nc: na * nb * nc, lambda na, nb, nc: (nc - 1) * nb * na,
        lambda na, nb, nc: (nb - 1) * na, lambda na, nb, nc: na - 1,
    ):
        scratch += [V((count(*sh.axes(m)[1]),) + sh.blocks[m], f32 if m == "E" else bf) for m in mats]
    scratch += [sem((sh.half,))] * (4 * len(mats))
    scratch += [V((sh.erows + 8, 256), f32), sem((len(mats),)), sem((sh.half,)), sem((sh.half,))]
    return pl.pallas_call(
        functools.partial(reduce_kernel, sh, mats),
        in_specs=[anyspec] * (len(whole) + 1) + [vm], out_specs=[vm] * (len(whole) + 1),
        out_shape=[S(outs[m], f32) for m in whole] + [S((sh.nrow * sh.ncol, sh.erows + 8, 256), f32)],
        scratch_shapes=scratch,
        compiler_params=pltpu.CompilerParams(collective_id=1, has_side_effects=True, vmem_limit_bytes=60 << 20),
        name="reduce_grads",
    )(*grads, aux)


def windows(sh, weights):
    row, col = lax.axis_index("row"), lax.axis_index("col")

    def put(v, which, index, wide, lanes):
        if wide == lanes:
            return v
        shift = index * wide - sh.start(which, index)
        return lax.dynamic_update_slice(jnp.zeros((v.shape[0], lanes), v.dtype), v, (0, shift))
    a, b, c, d = (w.astype(bf) for w in weights)
    return put(a, "A", col, sh.awide, sh.alanes), put(b.T, "B", row, sh.bwide, sh.blanes), c, d.T


GATHERED = ["A0", "A1", "B", "C", "D"]
REDUCED = ["A0", "A1", "B", "C", "D", "E"]


def tile_plan(sh, which):
    wide, count = (sh.awide, sh.ncol) if which == "A" else (sh.bwide, sh.nrow)
    alone, shared = [], []
    for c in range(count):
        first, end = wide * c // 128, -(-(wide * (c + 1)) // 128)
        base = sh.start(which, c) // 128
        lo = first + 1 if (wide * c) % 128 else first
        hi = end - 1 if (wide * (c + 1)) % 128 else end
        alone.append((c, lo, hi, base))
        if hi < end:
            shared.append((c, hi, base, sh.start(which, c + 1) // 128))
    return alone, shared


MOST = 6


def joiner(sh, which, src, dst, tmp, sem):
    alone, shared = tile_plan(sh, which)
    copies = []
    for c, lo, hi, at in alone:
        copies.append((src.at[c, :, pl.ds((lo - at) * 128, (hi - lo) * 128)], dst.at[:, pl.ds(lo * 128, (hi - lo) * 128)]))
    for u, (c, t, at, nxt) in enumerate(shared):
        copies.append((src.at[c, :, pl.ds((t - at) * 128, 128)], dst.at[:, pl.ds(t * 128, 128)]))
        copies.append((src.at[c + 1, :, pl.ds((t - nxt) * 128, 128)], tmp.at[u % MOST]))
    late = {len(alone) + 2 * u + 1 for u in range(MOST, len(shared))}
    make = lambda i: pltpu.make_async_copy(*copies[i], sem.at[i])
    made = [make(i) for i in range(len(copies)) if i not in late]
    for m in made:
        m.start()

    def end():
        for m in made:
            m.wait()
        for u, (c, t, at, nxt) in enumerate(shared):
            if u >= MOST:
                m = make(len(alone) + 2 * u + 1)
                m.start()
                m.wait()
            dst[:, t * 128 : (t + 1) * 128] += tmp[u % MOST]
    return end


def joiner_scratch(sh):
    V = pltpu.VMEM
    counts = [(len(a), len(s)) for a, s in (tile_plan(sh, "A"), tile_plan(sh, "B"))]
    return [V((D, 5 * D + FF + DD), bf), V((D, FF), bf)] + [V((min(max(s, 1), MOST), D, 128), bf) for _, s in counts] + [
        pltpu.SemaphoreType.DMA((a + 2 * s,)) for a, s in counts]


EG = 4 * ES
O_Q, O_P, O_F, O_E = D, 4 * D, 5 * D, 5 * D + FF


def enc_fwd_kernel(sh, pix, keep, pos3, sv, awin, bwin,
                   y, kept, xh1, xh2, xhf, rs1, rs2, rsf, a1, a2, e16, o, qkv, p, hid, gp, x, bias, win, wout, atmp, btmp, asem, bsem):
    enda = joiner(sh, "A", awin, win, atmp, asem)
    endb = joiner(sh, "B", bwin, wout, btmp, bsem)
    n = pix.shape[0]
    M = n * ES
    R = M // 2
    W = D
    kind = lax.rem(lax.broadcasted_iota(jnp.int32, (EG, 1), 0), ES)
    for i in range(0, n, 2):
        two = []
        for b in (i, i + 1):
            pick = (keep[b] == lax.broadcasted_iota(jnp.int32, (PATCHES, ES), 0)).astype(f32).astype(bf)
            two.append(dg(pick, pix[b], 0, 0))
            at = pos3[0:PATCHES, :], pos3[DS : DS + PATCHES, :], pos3[2 * DS : 2 * DS + PATCHES, :]
            x[b * ES : (b + 1) * ES, :] = dg(pick, at[0], 0, 0) + dg(pick, at[1], 0, 0) + dg(pick, at[2], 0, 0)
        kept[i * ES : (i + 2) * ES, :] = jnp.concatenate(two, axis=0).astype(bf)
    enda()
    for lo in range(0, M, EG):
        sl = slice(lo, lo + EG)
        v = x[sl, :] + nn(kept[sl, :], win[:, 0:W]) + part(sv, 10)
        x[sl, :] = jnp.where(kind < KEEP, v, jnp.where(kind == KEEP, part(sv, 11), 0.0))

    def ln1(r):
        xh, rs, a = norm_rows(x[r, :], part(sv, 0), part(sv, 1))
        xh1[r, :] = xh
        rs1[r, :] = rs
        a1[r, :] = a.astype(bf)
    rows(M, R, ln1)
    qkv[:, 0:W] = (nn(a1[...], win[:, O_Q : O_Q + W]) + sv[:, OFF[2] : OFF[2] + W]).astype(bf)
    qkv[:, W : 2 * W] = nn(a1[...], win[:, O_Q + W : O_Q + 2 * W]).astype(bf)
    qkv[:, 2 * W :] = (nn(a1[...], win[:, O_Q + 2 * W : O_P]) + sv[:, OFF[2] + W : OFF[3]]).astype(bf)

    ki = lax.broadcasted_iota(jnp.int32, (EG, EG), 0)
    qi = lax.broadcasted_iota(jnp.int32, (EG, EG), 1)
    same = jnp.zeros((EG, EG), jnp.bool_)
    for j in range(4):
        same = same | ((ki >= j * ES) & (ki < j * ES + KEEP + 1) & (qi >= j * ES) & (qi < (j + 1) * ES))
    bias[...] = jnp.where(same, 0.0, -1e30).astype(f32)

    @pl.loop(0, n // 4)
    def _(i):
        rsl = pl.ds(pl.multiple_of(i * EG, 16), EG)
        for g in range(6):
            att_fwd(qkv, o, p, bias[...], rsl, W, g, i * 12 + g * 2, 64)

    x[...] += nn(o[...], win[:, O_P : O_P + W]) + part(sv, 3)

    def ln2(r):
        xh, rs, a = norm_rows(x[r, :], part(sv, 4), part(sv, 5))
        xh2[r, :] = xh
        rs2[r, :] = rs
        a2[r, :] = a.astype(bf)
    rows(M, R, ln2)

    for c in range(0, FF, 512):
        h = nn(a2[...], win[:, O_F + c : O_F + c + 512])
        g, dg_ = gelu_pair(h + sv[:, OFF[6] + c : OFF[6] + c + 512])
        hid[:, c : c + 512] = g.astype(bf)
        gp[:, c : c + 512] = dg_.astype(bf)
    endb()
    x[...] += nt(hid[...], wout[...]) + part(sv, 7)

    def lnf(r):
        xh, rs, a = norm_rows(x[r, :], part(sv, 8), part(sv, 9))
        xhf[r, :] = xh
        rsf[r, :] = rs
        e16[r, :] = a.astype(bf)
    rows(M, R, lnf)
    y[...] = nn(e16[...], win[:, O_E:]) + part(sv, 12)


def vspec(k):
    return [pl.BlockSpec(memory_space=pltpu.VMEM)] * k


def encoder_fwd(sh, pix, keep, pos3, sv, awin, bwin):
    n = pix.shape[0]
    M = n * ES
    S = jax.ShapeDtypeStruct
    V = pltpu.VMEM
    outs = [S((M, DD), f32), S((M, D), bf), S((M, D), f32), S((M, D), f32), S((M, D), f32),
            S((M, 1), f32), S((M, 1), f32), S((M, 1), f32), S((M, D), bf), S((M, D), bf), S((M, D), bf), S((M, D), bf),
            S((M, 3 * D), bf), S((n // 4 * HEADS, EG, EG), bf), S((M, FF), bf), S((M, FF), bf)]
    return pl.pallas_call(
        functools.partial(enc_fwd_kernel, sh),
        in_specs=vspec(4) + [pl.BlockSpec(memory_space=pl.ANY)] * 2, out_specs=vspec(len(outs)), out_shape=outs,
        scratch_shapes=[V((M, D), f32), V((EG, EG), f32)] + joiner_scratch(sh),
        compiler_params=pltpu.CompilerParams(vmem_limit_bytes=60 << 20),
        name="encoder_fwd",
    )(pix, keep, pos3, sv, awin, bwin)


def enc_bwd_kernel(sh, dy, dsm_in, dhw, sv, awin, bwin, kept, xh1_in, xh2, xhf_in, rs1, rs2, rsf, a1_in, a2, e16_in, o, qkv, p, hid, gp,
                   dwin, dwout, eout, dsm, etail, x, t, d16, dh16, stage, xb, ab, sem, lsem, win, wout, atmp, btmp, asem, bsem):
    def fetch(i, src, dst):
        copy = pltpu.make_async_copy(src, dst, lsem.at[i])
        copy.start()
        return copy

    at_e, at_xhf = fetch(0, e16_in, ab), fetch(1, xhf_in, xb)
    enda = joiner(sh, "A", awin, win, atmp, asem)
    endb = joiner(sh, "B", bwin, wout, btmp, bsem)
    M = dy.shape[0]
    R = M // 2
    W = D
    dsm[...] = dsm_in[...]
    head = fetch(4, dhw, eout.at[pl.ds(0, 3 * DD), :])

    def save(where, sums):
        for (i, lo), v in zip(where, sums):
            dsm[:, OFF[i] + lo : OFF[i] + lo + v.shape[1]] += v

    shots = []

    def put(out, base, value):
        width = value.shape[1]
        slot = len(shots) % 2
        if len(shots) >= 2:
            shots[-2].wait()
        stage[slot, :, 0:width] = value.astype(bf)
        copy = pltpu.make_async_copy(stage.at[slot, :, pl.ds(0, width)], out.at[:, pl.ds(base, width)], sem.at[slot])
        copy.start()
        shots.append(copy)

    def emb(r):
        v = dy[r, :]
        d16[r, 0:DD] = v.astype(bf)
        return [v]
    save([(12, 0)], rows_sum(M, R, [DD], emb))
    at_e.wait()
    put(dwin, O_E, dg(ab[...], d16[:, 0:DD], 0, 0))
    at_a = fetch(2, a1_in, ab)
    enda()
    endb()
    t[...] = nt(d16[:, 0:DD], win[:, O_E:])

    at_xhf.wait()

    def lnfb(r):
        da = t[r, :]
        xh = xb[r, :]
        dx = norm_back(da, xh, rsf[r, :], part(sv, 8))
        x[r, :] = dx
        d16[r, :] = dx.astype(bf)
        return da * xh, da, dx
    save([(8, 0), (9, 0), (7, 0)], rows_sum(M, R, [W] * 3, lnfb))
    at_xh1 = fetch(3, xh1_in, xb)
    for c in range(0, FF, W):
        put(dwout, c, dg(d16[...], hid[:, c : c + W], 0, 0))
        dh = nn(d16[...], wout[:, c : c + W]) * gp[:, c : c + W].astype(f32)
        dsm[:, OFF[6] + c : OFF[6] + c + W] += rsum(dh)
        dh16[:, c : c + W] = dh.astype(bf)
        put(dwin, O_F + c, dg(a2[...], dh16[:, c : c + W], 0, 0))
    t[...] = nt(dh16[...], win[:, O_F:O_E])
    dqkv = dh16

    def ln2b(r):
        da = t[r, :]
        xh = xh2[r, :]
        dx = x[r, :] + norm_back(da, xh, rs2[r, :], part(sv, 4))
        x[r, :] = dx
        d16[r, :] = dx.astype(bf)
        return da * xh, da, dx
    save([(4, 0), (5, 0), (3, 0)], rows_sum(M, R, [W] * 3, ln2b))
    put(dwin, O_P, dg(o[...], d16[...], 0, 0))
    d16[...] = nt(d16[...], win[:, O_P:O_F]).astype(bf)

    @pl.loop(0, M // EG)
    def _(i):
        rsl = pl.ds(pl.multiple_of(i * EG, 16), EG)
        for g in range(6):
            att_bwd(qkv, d16, p, dqkv, rsl, W, g, i * 12 + g * 2, 64)

    at_a.wait()
    for c in range(0, 3 * D, W):
        put(dwin, O_Q + c, dg(ab[...], dqkv[:, c : c + W], 0, 0))
    save([(2, 0), (2, W)], rows_sum(M, R, [W, W], lambda r: [dqkv[r, 0:W].astype(f32), dqkv[r, 2 * W : 3 * W].astype(f32)]))
    t[...] = nt(dqkv[:, 0 : 3 * W], win[:, O_Q:O_P])
    at_xh1.wait()

    def ln1b(r):
        da = t[r, :]
        xh = xb[r, :]
        dx = x[r, :] + norm_back(da, xh, rs1[r, :], part(sv, 0))
        kind = lax.rem(lax.broadcasted_iota(jnp.int32, (r.size, 1), 0), ES)
        only = jnp.where(kind < KEEP, dx, 0.0)
        d16[r, :] = only.astype(bf)
        return da * xh, da, jnp.where(kind == KEEP, dx, 0.0), only
    save([(0, 0), (1, 0), (11, 0), (10, 0)], rows_sum(M, R, [W] * 4, ln1b))
    put(dwin, 0, dg(kept[...], d16[...], 0, 0))
    etail[...] = jnp.zeros_like(etail)
    for i in range(SMALL // 256):
        etail[i : i + 1, :] = dsm[:, i * 256 : (i + 1) * 256]
    tail = fetch(5, etail, eout.at[pl.ds(3 * DD, etail.shape[0]), :])
    for c in shots[-2:] + [head, tail]:
        c.wait()


def encoder_bwd(sh, dy, dsm, dhw, sv, awin, bwin, saved):
    M = dy.shape[0]
    count = sh.nrow * sh.ncol * sh.erows
    S = jax.ShapeDtypeStruct
    V = pltpu.VMEM
    anyspec = pl.BlockSpec(memory_space=pl.ANY)
    return pl.pallas_call(
        functools.partial(enc_bwd_kernel, sh),
        in_specs=[anyspec if i in (2, 4, 5, 7, 9, 13, 15) else spec for i, spec in enumerate(vspec(6 + len(saved)))],
        out_specs=[anyspec] * 3,
        out_shape=[S((D, 5 * D + FF + DD), bf), S((D, FF), bf), S((count, 256), f32)],
        scratch_shapes=[V((1, SMALL), f32), V((count - 3 * DD, 256), f32), V((M, D), f32), V((M, D), f32), V((M, D), bf), V((M, FF), bf), V((2, D, D), bf), V((M, D), f32), V((M, D), bf),
                        pltpu.SemaphoreType.DMA((2,)), pltpu.SemaphoreType.DMA((6,))] + joiner_scratch(sh),
        compiler_params=pltpu.CompilerParams(vmem_limit_bytes=63 << 20),
        name="encoder_bwd",
    )(dy, dsm, dhw, sv, awin, bwin, *saved)


def sincos_np(width):
    quarter = width // 4
    freq = (1.0 / np.float32(10000.0) ** (np.arange(quarter, dtype=np.float32) / np.float32(quarter))).astype(np.float32)
    pos = np.arange(GRID * GRID)
    cp = (pos % GRID).astype(np.float32)[:, None] * freq[None, :]
    rp = (pos // GRID).astype(np.float32)[:, None] * freq[None, :]
    return np.concatenate([np.sin(cp), np.cos(cp), np.sin(rp), np.cos(rp)], axis=1).astype(np.float32)


def tables():
    dec = np.zeros((DS, DD), np.float32)
    dec[:PATCHES] = sincos_np(DD)
    enc = np.zeros((DS, D), np.float32)
    enc[:PATCHES] = sincos_np(D)
    b = ml_dtypes.bfloat16
    hi = enc.astype(b)
    mid = (enc - hi.astype(np.float32)).astype(b)
    lo = (enc - hi.astype(np.float32) - mid.astype(np.float32)).astype(b)
    return dec, np.concatenate([hi, mid, lo], axis=0)


def adamw(weight, first, second, grad):
    first = 0.9 * first + (1.0 - 0.9) * grad
    second = 0.999 * second + (1.0 - 0.999) * grad * grad
    first_hat = first / (1.0 - 0.9**STEP)
    second_hat = second / (1.0 - 0.999**STEP)
    weight = weight - 0.08 * (first_hat / (jnp.sqrt(second_hat) + 1e-08) + 0.05 * weight)
    return (weight, first, second)


def update_kernel(sh, ga, gb, gc, gd, eall, *refs):
    weights, firsts, seconds = refs[0:6], refs[6:12], refs[12:18]
    new, mo, vo = refs[18:24], refs[24:30], refs[30:36]
    result, e2d = refs[36], refs[37]
    er = sh.erows
    row, col = lax.axis_index("row"), lax.axis_index("col")
    squares = jnp.zeros((1, 128), f32)
    losses = jnp.zeros((1, 128), f32)
    for i in range(sh.nrow * sh.ncol):
        e2d[i * er : (i + 1) * er, :] = eall[i, 0:er, :]
        squares = squares + eall[i, er : er + 1, 0:128]
        losses = losses + eall[i, er : er + 1, 128:256]
    norm = jnp.sqrt(jnp.sum(squares, axis=1, keepdims=True))
    factor = 0.0001 / jnp.maximum(norm, 0.0001)
    result[...] = jnp.where(lax.broadcasted_iota(jnp.int32, (1, 128), 1) == 0, losses, norm)

    def aligned(g, which, index, wide, lanes):
        if wide == lanes:
            return g
        return pltpu.roll(g, lax.rem(lanes - (index * wide - sh.start(which, index)), lanes), 1)[:, 0:wide]

    def apply(i, at, grad):
        out = adamw(weights[i][at], firsts[i][at], seconds[i][at], grad * factor)
        new[i][at], mo[i][at], vo[i][at] = out

    every = (slice(None), slice(None))
    apply(0, every, aligned(ga[...], "A", col, sh.awide, sh.alanes))
    apply(1, every, aligned(gb[...], "B", row, sh.bwide, sh.blanes))
    apply(2, every, gc[...])
    apply(3, every, gd[...])
    for c in range(0, PIX, 256):
        apply(4, (slice(None), slice(c, c + 256)), e2d[2 * c : 2 * c + DD, :])
    for i in range(SMALL // 256):
        for h in (0, 1):
            apply(5, (slice(2 * i + h, 2 * i + h + 1), slice(None)), e2d[3 * DD + i : 3 * DD + i + 1, h * 128 : (h + 1) * 128])


def update(sh, grads, weights, firsts, seconds):
    S = jax.ShapeDtypeStruct
    turn = lambda t: [v.T if i % 6 in (1, 3) else v for i, v in enumerate(t)]
    flat = lambda t: turn([v.reshape(SMALL // 128, 128) if v.ndim == 1 else v for v in t])
    state = flat(weights) + flat(firsts) + flat(seconds)
    outs = pl.pallas_call(
        functools.partial(update_kernel, sh),
        in_specs=vspec(5 + 18), out_specs=vspec(19),
        out_shape=[S(v.shape, f32) for v in state] + [S((1, 128), f32)],
        scratch_shapes=[pltpu.VMEM((sh.nrow * sh.ncol * sh.erows, 256), f32)],
        compiler_params=pltpu.CompilerParams(vmem_limit_bytes=60 << 20),
        name="update",
    )(*grads, *state)
    small = lambda v: v.reshape(SMALL) if v.shape == (SMALL // 128, 128) else v
    return tuple(turn([small(v) for v in outs[:18]])) + (outs[18][0, 0], outs[18][0, 1])


def local(pixels, keep_idx, restore, *state):
    weights, firsts, seconds = state[0:6], state[6:12], state[12:18]
    nrow, ncol = lax.axis_size("row"), lax.axis_size("col")
    sh = Shapes(nrow, ncol)
    n = pixels.shape[0]
    denom = 1.0 * n * nrow * ncol * (PATCHES - KEEP)

    dec_pos, enc_pos = tables()
    fill = lambda count, value: jnp.full((n, count), value, jnp.int32)
    keep = jnp.concatenate([keep_idx, fill(ES - KEEP, NOROW)], axis=1).reshape(n, 1, ES)
    code = jnp.concatenate([jnp.where(restore < KEEP, restore, 64), fill(1, KEEP), fill(DS - PATCHES - 1, NOROW)], axis=1)
    head, sv = weights[4], weights[5].reshape(1, SMALL)

    aw, bw, c, dt = gather_weights(sh, GATHERED, *windows(sh, weights[0:4]))
    y, *saved = encoder_fwd(sh, pixels, keep, jnp.asarray(enc_pos), sv, aw, bw)
    dy, dc, ddt, dhead, dsm, loss = decoder(
        y.reshape(n, ES, DD), code.reshape(n, 1, DS), pixels, jnp.asarray(dec_pos), sv, c, dt, head, 1.0 / denom)
    da, dbt, shared = encoder_bwd(sh, dy.reshape(n * ES, DD), dsm, dhead, sv, aw, bw, saved)
    sums = reduce_grads(sh, REDUCED, loss, da, dbt, dc, ddt, shared.reshape(nrow * ncol, sh.erows, 256))
    return update(sh, sums, weights, firsts, seconds)


def solution(mesh):
    both = P(("row", "col"))
    big = [P("row", "col")] * 4 + [P()] * 2
    return jax.shard_map(
        local,
        mesh=mesh,
        in_specs=(both, both, both, *big, *big, *big),
        out_specs=(*big, *big, *big, P(), P()),
        check_vma=False,
    )
```

```python
import functools
import math

import jax
import jax.numpy as jnp
import ml_dtypes
import numpy as np
from jax import lax
from jax.experimental import pallas as pl
from jax.experimental.pallas import tpu as pltpu
from jax.sharding import PartitionSpec as P

D = 768
HEADS = 12
FF = 3072
DD = 512
DHEADS = 16
DFF = 2048
PIX = 768
GRID = 14
PATCHES = 196
KEEP = 49
STEP = 10
SMALL = 21248
ES = 56
DS = 208
SEL = 80
NOROW = 255
f32 = jnp.float32
bf = jnp.bfloat16

LENS = [
    D, D, 2 * D, D, D, D, FF, D, D, D, D, D,
    DD, DD, DD, DD, 2 * DD, DD, DD, DD, DFF, DD, DD, DD, PIX,
]
OFF = [0]
for piece in LENS:
    OFF.append(OFF[-1] + piece)


def part(ref, i):
    return ref[:, OFF[i] : OFF[i + 1]]


def dg(a, b, ca, cb):
    return lax.dot_general(a, b, (((ca,), (cb,)), ((), ())), preferred_element_type=f32)


def nn(a, b):
    return dg(a, b, 1, 0)


def nt(a, b):
    return dg(a, b, 1, 1)


def rows(total, size, fn):
    @pl.loop(0, total // size)
    def _(i):
        fn(pl.ds(pl.multiple_of(i * size, size), size))


def rows_sum(total, size, widths, fn):
    def body(i, carry):
        parts = fn(pl.ds(pl.multiple_of(i * size, size), size))
        return tuple(c + jnp.sum(v.reshape(size // 8, 8, v.shape[1]), axis=0) for c, v in zip(carry, parts))
    carry = lax.fori_loop(0, total // size, body, tuple(jnp.zeros((8, w), f32) for w in widths))
    return [rsum(c) for c in carry]


def pieces(x):
    hi = x.astype(bf)
    rest = x - hi.astype(f32)
    mid = rest.astype(bf)
    low = (rest - mid.astype(f32)).astype(bf)
    return hi, mid, low


def gelu_pair(x):
    ax = jnp.abs(x)
    d = 1.0 + (0.3275911 * 0.7071067811865476) * ax
    r = pl.reciprocal(d, approx=True)
    t = r * (2.0 - d * r)
    e = jnp.exp(-0.5 * (x * x))
    poly = ((((0.5 * 1.061405429 * t - 0.5 * 1.453152027) * t + 0.5 * 1.421413741) * t
             - 0.5 * 0.284496736) * t + 0.5 * 0.254829592) * t
    q = poly * e
    phi = jnp.where(x >= 0.0, 1.0 - q, q)
    return x * phi, phi + x * (e * 0.3989422804014327)


def norm_rows(x, gain, shift):
    c = x - jnp.mean(x, axis=1, keepdims=True)
    rs = lax.rsqrt(jnp.mean(c * c, axis=1, keepdims=True) + 1e-06)
    xh = c * rs
    return xh, rs, xh * gain + shift


def norm_back(da, xh, rs, gain):
    g = da * gain
    m1 = jnp.mean(g, axis=1, keepdims=True)
    m2 = jnp.mean(g * xh, axis=1, keepdims=True)
    return rs * (g - m1 - xh * m2)


def rsum(x):
    return jnp.sum(x, axis=0, keepdims=True)


def lanes_of(x, h, hd):
    lane = lax.broadcasted_iota(jnp.int32, (1, 128), 1)
    return jnp.where((lane >= h * hd) & (lane < (h + 1) * hd), x, jnp.zeros_like(x))


def stack(x, hd):
    return jnp.concatenate([lanes_of(x, h, hd) for h in range(128 // hd)], axis=0)


def unstack(x, hd):
    n = x.shape[0] * hd // 128
    out = None
    for h in range(128 // hd):
        t = lanes_of(x[h * n : (h + 1) * n], h, hd)
        out = t if out is None else out + t
    return out


def att_fwd(qkv, o, p, bias, rsl, width, g, slot, hd):
    c0 = g * 128
    q = qkv[rsl, c0 : c0 + 128]
    k = qkv[rsl, c0 + width : c0 + width + 128]
    v = qkv[rsl, c0 + 2 * width : c0 + 2 * width + 128]
    n = q.shape[0]
    every = nt(stack(k, hd), q)
    probs = []
    for h in range(128 // hd):
        s = every[h * n : (h + 1) * n] * (hd ** -0.5 * 1.4426950408889634) + bias
        e = jnp.exp2(s - jnp.max(s, axis=0, keepdims=True))
        pr = (e * (1.0 / jnp.sum(e, axis=0, keepdims=True))).astype(bf)
        p[slot + h] = pr
        probs.append(pr)
    o[rsl, c0 : c0 + 128] = dg(jnp.concatenate(probs, axis=0), stack(v, hd), 0, 0).astype(bf)


def att_bwd(qkv, do, p, dqkv, rsl, width, g, slot, hd):
    c0 = g * 128
    c1, c2 = c0 + width, c0 + 2 * width
    q = qkv[rsl, c0 : c0 + 128]
    k = qkv[rsl, c1 : c1 + 128]
    v = qkv[rsl, c2 : c2 + 128]
    d = do[rsl, c0 : c0 + 128]
    n = q.shape[0]
    probs = jnp.concatenate([p[slot + h] for h in range(128 // hd)], axis=0)
    every = nt(stack(v, hd), d)
    back = []
    for h in range(128 // hd):
        pf = probs[h * n : (h + 1) * n].astype(f32)
        t = pf * every[h * n : (h + 1) * n].astype(bf).astype(f32)
        back.append(((t - pf * jnp.sum(t, axis=0, keepdims=True)) * (hd ** -0.5)).astype(bf))
    back = jnp.concatenate(back, axis=0)
    dqkv[rsl, c0 : c0 + 128] = dg(back, stack(k, hd), 0, 0).astype(bf)
    dqkv[rsl, c1 : c1 + 128] = unstack(nn(back, q), hd).astype(bf)
    dqkv[rsl, c2 : c2 + 128] = unstack(nn(probs, d), hd).astype(bf)


def dec_kernel(scale, nb, y, coder, pix, pos, sv, win, wout, hw,
               dy, win_out, wout_out, dhw, dsm, loss,
               dwin, dwout, x, t, xh1, xh2, xhf, rs1, rs2, rsf, tm, tr, a1, a2, u, o, qkv, p, hid, gp, dpr, d16, hide, lacc):
    M = nb * DS
    R = M
    W = DD

    @pl.when(pl.program_id(0) == 0)
    def _():
        dsm[...] = jnp.zeros_like(dsm)
        loss[...] = jnp.zeros_like(loss)
        lacc[...] = jnp.zeros_like(lacc)
        dpr[...] = jnp.zeros_like(dpr)
        for ref in (dwin, dwout, dhw):
            rows(ref.shape[0], 16, lambda r: ref.__setitem__((r, slice(None)), jnp.zeros((16, ref.shape[1]), f32)))

    def put(where, sums):
        for (i, lo), v in zip(where, sums):
            dsm[:, OFF[i] + lo : OFF[i] + lo + v.shape[1]] += v

    for b in range(nb):
        pick = (coder[b] == lax.broadcasted_iota(jnp.int32, (SEL, DS), 0)).astype(f32).astype(bf)
        tok = jnp.where(lax.broadcasted_iota(jnp.int32, (8, W), 0) == 0, part(sv, 13), 0.0)
        table = jnp.concatenate([y[b], jnp.zeros((8, W), f32), tok, jnp.zeros((8, W), f32)], axis=0)
        z = pos[...]
        for piece in pieces(table):
            z = z + dg(pick, piece, 0, 0)
        x[b * DS : (b + 1) * DS, :] = z
        mark = (lax.broadcasted_iota(jnp.int32, (SEL, 128), 0) == 64).astype(f32).astype(bf)
        hide[b * DS : (b + 1) * DS, :] = dg(pick, mark, 0, 0)[:, 0:1]

    def ln1(r):
        xh, rs, a = norm_rows(x[r, :], part(sv, 14), part(sv, 15))
        xh1[r, :] = xh
        rs1[r, :] = rs
        a1[r, :] = a.astype(bf)
    rows(M, R, ln1)

    qkv[:, 0:W] = (nn(a1[...], win[:, 0:W]) + sv[:, OFF[16] : OFF[16] + W]).astype(bf)
    qkv[:, W : 2 * W] = nn(a1[...], win[:, W : 2 * W]).astype(bf)
    qkv[:, 2 * W :] = (nn(a1[...], win[:, 2 * W : 3 * W]) + sv[:, OFF[16] + W : OFF[17]]).astype(bf)

    bias = jnp.where(lax.broadcasted_iota(jnp.int32, (DS, 1), 0) <= PATCHES, 0.0, -1e30).astype(f32)

    @pl.loop(0, nb)
    def _(i):
        rsl = pl.ds(pl.multiple_of(i * DS, 16), DS)
        for g in range(4):
            att_fwd(qkv, o, p, bias, rsl, W, g, i * 16 + g * 4, 32)

    x[...] += nn(o[...], win[:, 3 * W : 4 * W]) + part(sv, 17)

    def ln2(r):
        xh, rs, a = norm_rows(x[r, :], part(sv, 18), part(sv, 19))
        xh2[r, :] = xh
        rs2[r, :] = rs
        a2[r, :] = a.astype(bf)
    rows(M, R, ln2)

    CW = 512
    for c in range(0, DFF, CW):
        h = nn(a2[...], win[:, 4 * W + c : 4 * W + c + CW])
        g, dg_ = gelu_pair(h + sv[:, OFF[20] + c : OFF[20] + c + CW])
        hid[:, c : c + CW] = g.astype(bf)
        gp[:, c : c + CW] = dg_.astype(bf)

    x[...] += nt(hid[...], wout[...]) + part(sv, 21)

    def lnf(r):
        xh, rs, a = norm_rows(x[r, :], part(sv, 22), part(sv, 23))
        xhf[r, :] = xh
        rsf[r, :] = rs
        u[r, :] = a.astype(bf)
    rows(M, R, lnf)

    for b in range(nb):
        v = pix[b].astype(f32)
        m = jnp.mean(v, axis=1, keepdims=True)
        c = v - m
        tm[b * DS : b * DS + PATCHES, :] = m
        tr[b * DS : b * DS + PATCHES, :] = lax.rsqrt(jnp.mean(c * c, axis=1, keepdims=True) + 1e-06)

    for c in range(0, PIX, 256):
        pr = nn(u[...], hw[:, c : c + 256].astype(bf)) + sv[:, OFF[24] + c : OFF[24] + c + 256]
        for b in range(nb):
            sl = slice(b * DS, b * DS + PATCHES)
            tgt = (pix[b, :, c : c + 256].astype(f32) - tm[sl, :]) * tr[sl, :]
            diff = jnp.where(hide[sl, :] > 0.5, pr[sl] - tgt, 0.0)
            lacc[...] += rsum(diff * diff)
            dp = diff * (2.0 * scale / PIX)
            dsm[:, OFF[24] + c : OFF[24] + c + 256] += rsum(dp)
            dpr[sl, c : c + 256] = dp.astype(bf)

    for c in range(0, PIX, 256):
        dhw[2 * c : 2 * c + DD, :] += dg(u[...], dpr[:, c : c + 256], 0, 0)
    t[...] = nt(dpr[...], hw[...].astype(bf))

    def lnfb(r):
        da = t[r, :]
        xh = xhf[r, :]
        dx = norm_back(da, xh, rsf[r, :], part(sv, 22))
        x[r, :] = dx
        d16[r, :] = dx.astype(bf)
        return da * xh, da, dx
    put([(22, 0), (23, 0), (21, 0)], rows_sum(M, R, [W] * 3, lnfb))

    dwout[...] += dg(d16[...], hid[...], 0, 0)
    for c in range(0, DFF, CW):
        dh = nn(d16[...], wout[:, c : c + CW]) * gp[:, c : c + CW].astype(f32)
        dsm[:, OFF[20] + c : OFF[20] + c + CW] += rsum(dh)
        gp[:, c : c + CW] = dh.astype(bf)
    dwin[:, 4 * W :] += dg(a2[...], gp[...], 0, 0)
    t[...] = nt(gp[...], win[:, 4 * W :])

    def ln2b(r):
        da = t[r, :]
        xh = xh2[r, :]
        dx = x[r, :] + norm_back(da, xh, rs2[r, :], part(sv, 18))
        x[r, :] = dx
        d16[r, :] = dx.astype(bf)
        return da * xh, da, dx
    put([(18, 0), (19, 0), (17, 0)], rows_sum(M, R, [W] * 3, ln2b))

    dwin[:, 3 * W : 4 * W] += dg(o[...], d16[...], 0, 0)
    o[...] = nt(d16[...], win[:, 3 * W : 4 * W]).astype(bf)
    dqkv = gp

    @pl.loop(0, nb)
    def _(i):
        rsl = pl.ds(pl.multiple_of(i * DS, 16), DS)
        for g in range(4):
            att_bwd(qkv, o, p, dqkv, rsl, W, g, i * 16 + g * 4, 32)

    dwin[:, 0 : 3 * W] += dg(a1[...], dqkv[:, 0 : 3 * W], 0, 0)
    put([(16, 0), (16, W)], rows_sum(M, R, [W, W], lambda r: [dqkv[r, 0:W].astype(f32), dqkv[r, 2 * W : 3 * W].astype(f32)]))
    t[...] = nt(dqkv[:, 0 : 3 * W], win[:, 0 : 3 * W])

    def ln1b(r):
        da = t[r, :]
        xh = xh1[r, :]
        x[r, :] = x[r, :] + norm_back(da, xh, rs1[r, :], part(sv, 14))
        return da * xh, da
    put([(14, 0), (15, 0)], rows_sum(M, R, [W] * 2, ln1b))

    for b in range(nb):
        pick = (coder[b] == lax.broadcasted_iota(jnp.int32, (SEL, DS), 0)).astype(f32).astype(bf)
        out = None
        for piece in pieces(x[b * DS : (b + 1) * DS, :]):
            v = nn(pick, piece)
            out = v if out is None else out + v
        dy[b] = out[0:ES]
        dsm[:, OFF[13] : OFF[14]] += out[64:65]

    @pl.when(pl.program_id(0) == pl.num_programs(0) - 1)
    def _():
        loss[...] = jnp.broadcast_to(jnp.sum(lacc[...], axis=1, keepdims=True) * (scale / PIX), (1, 128))
        for src, dst in ((dwin, win_out), (dwout, wout_out)):
            rows(DD, 16, lambda r: dst.__setitem__((r, slice(None)), src[r, :].astype(bf)))


def decoder(y, coder, pix, pos, sv, win, wout, hw, scale, nb=2):
    n = y.shape[0]
    M = nb * DS
    whole = lambda a: pl.BlockSpec(a.shape, lambda i: (0,) * a.ndim, pipeline_mode=pl.Buffered(1))
    fixed = lambda s: pl.BlockSpec(s, lambda i: (0,) * len(s), pipeline_mode=pl.Buffered(1))
    blk = lambda s: pl.BlockSpec((nb,) + s, lambda i: (i, 0, 0))
    V = pltpu.VMEM
    return pl.pallas_call(
        functools.partial(dec_kernel, scale, nb),
        grid=(n // nb,),
        in_specs=[blk((ES, DD)), blk((1, DS)), blk((PATCHES, PIX)), whole(pos), whole(sv), whole(win), whole(wout), whole(hw)],
        out_specs=[blk((ES, DD)), fixed(win.shape), fixed(wout.shape), fixed((3 * DD, 256)), fixed((1, SMALL)), fixed((1, 128))],
        out_shape=[
            jax.ShapeDtypeStruct((n, ES, DD), f32), jax.ShapeDtypeStruct(win.shape, bf),
            jax.ShapeDtypeStruct(wout.shape, bf), jax.ShapeDtypeStruct((3 * DD, 256), f32),
            jax.ShapeDtypeStruct((1, SMALL), f32), jax.ShapeDtypeStruct((1, 128), f32)],
        scratch_shapes=[
            V(win.shape, f32), V(wout.shape, f32),
            V((M, DD), f32), V((M, DD), f32), V((M, DD), f32), V((M, DD), f32), V((M, DD), f32),
            V((M, 1), f32), V((M, 1), f32), V((M, 1), f32), V((M, 1), f32), V((M, 1), f32),
            V((M, DD), bf), V((M, DD), bf), V((M, DD), bf), V((M, DD), bf), V((M, 3 * DD), bf),
            V((nb * DHEADS, DS, DS), bf), V((M, DFF), bf), V((M, DFF), bf), V((M, PIX), bf), V((M, DD), bf), V((M, 1), f32),
            V((1, 256), f32)],
        compiler_params=pltpu.CompilerParams(vmem_limit_bytes=60 << 20),
        name="decoder",
    )(y, coder, pix, pos, sv, win, wout, hw)


class Place:
    def __init__(self, nrow, ncol):
        side = math.isqrt(nrow)
        self.nrow, self.ncol = nrow, ncol
        self.n = {"x": side, "y": nrow // side, "z": ncol // 2}
        row, col = lax.axis_index("row"), lax.axis_index("col")
        self.at = {"x": row % side, "y": row // side, "z": col // 2, "core": col % 2}

    def moved(self, **by):
        at = {}
        for k, v in self.at.items():
            step = by.get(k, 0)
            size = 2 if k == "core" else self.n[k]
            at[k] = v if step % size == 0 else lax.rem(v + (step % size), size)
        return at["y"] * self.n["x"] + at["x"], at["z"] * 2 + at["core"]

    def greet(self):
        sem = pltpu.get_barrier_semaphore()
        count = 0
        for axis in ("x", "y", "z", "core"):
            size = 2 if axis == "core" else self.n[axis]
            for step in range(1, size):
                pl.semaphore_signal(sem, inc=1, device_id=self.moved(**{axis: step}), device_id_type=pl.DeviceIdType.MESH)
                count += 1
        pl.semaphore_wait(sem, count)

    def remote(self, src, dst, ssem, rsem, **by):
        return pltpu.make_async_remote_copy(src, dst, ssem, rsem, device_id=self.moved(**by), device_id_type=pl.DeviceIdType.MESH)


ORDER = {
    "A0": ("z", "x", "y"), "A1": ("z", "y", "x"), "A2": ("x", "y", "z"), "B": ("z", "y", "x"),
    "C": ("z", "x", "y"), "D": ("y", "x", "z"), "E": ("z", "y", "x"),
}
DIRECT = ("E",)


class Shapes:
    def __init__(self, nrow, ncol):
        self.nrow, self.ncol = nrow, ncol
        self.half = nrow * ncol // 2
        side = math.isqrt(nrow)
        self.n = {"x": side, "y": nrow // side, "z": ncol // 2}
        self.awide, self.bwide = (5 * D + FF + DD) // ncol, FF // nrow
        self.alanes, self.blanes = self.window(self.awide, ncol), self.window(self.bwide, nrow)
        self.arows, self.brows = D // nrow, D // ncol
        cut = [self.arows * t // 12 // 16 * 16 for t in (5, 4)]
        self.acut = (0, cut[0], cut[0] + cut[1], self.arows)
        self.crows, self.clanes = DD // nrow, (4 * DD + DFF) // ncol
        self.drows, self.dlanes = DD // ncol, DFF // nrow
        self.erows = -(-(DD * PIX + SMALL) // (nrow * ncol * 256 * 8)) * 8
        self.blocks = {
            "A0": (cut[0], self.alanes), "A1": (cut[1], self.alanes), "A2": (self.arows - self.acut[2], self.alanes), "B": (self.brows, self.blanes),
            "C": (self.crows, self.clanes), "D": (self.drows, self.dlanes), "E": (self.erows, 256)}

    @staticmethod
    def window(wide, count):
        return max(-(-((wide * c) % 128 + wide) // 128) * 128 for c in range(count))

    def start(self, which, index):
        wide, lanes, total = (self.awide, self.alanes, 5 * D + FF + DD) if which == "A" else (self.bwide, self.blanes, FF)
        first = (wide * index) // 128
        last = (total - lanes) // 128
        if isinstance(index, int):
            return min(first, last) * 128
        return jnp.minimum(first, last) * 128

    def axes(self, m):
        return ORDER[m], tuple(self.n[a] for a in ORDER[m])

    def steps(self, mats, back, keys=False):
        out = []
        for pos, m in enumerate(mats):
            _, (na, nb, nc) = self.axes(m)
            for i in range(nc):
                for j in range(nb):
                    for k in range(na):
                        key = (na - 1 - k) + (nb - 1 - j) + (nc - 1 - i) if back else i + j + (min(k, 1) if m in DIRECT else k)
                        out.append((key, pos, m, i, j, k))
        return [t if keys else t[2:] for t in sorted(out)]

    def onward(self, m, i, j, k):
        (a, b, c), (na, nb, nc) = self.axes(m)
        slot = (i * nb + j) * na + k
        out = []
        if m in DIRECT and i == j == k == 0:
            out += [(a, t, t) for t in range(1, na)]
        if m not in DIRECT and i == j == 0 and k < na - 1:
            out.append((a, 1, slot + 1))
        if i == 0 and j < nb - 1:
            out.append((b, 1, slot + na))
        if i < nc - 1:
            out.append((c, 1, slot + na * nb))
        return slot, out


class Spread:
    def __init__(self, place, sh, first, spot, send, recv, csend, crecv):
        self.place, self.sh, self.first, self.spot = place, sh, first, spot
        self.send, self.recv, self.csend, self.crecv = send, recv, csend, crecv
        self.sent, self.late = [], []

    def step(self, m, i, j, k):
        place = self.place
        (a, b, c), _ = self.sh.axes(m)
        slot, onward = self.sh.onward(m, i, j, k)
        by = {c: -i, b: -j, a: -k}
        dst = self.spot(m, *place.moved(**by))
        own = i == j == k == 0
        src = self.first(m) if own else dst
        csend, crecv = self.csend[m].at[slot], self.crecv[m].at[slot]
        if not own:
            place.remote(dst, dst, self.send[m].at[slot], self.recv[m].at[slot], core=1).wait_recv()
        for axis, far, there in onward:
            copy = place.remote(src, dst, self.send[m].at[there], self.recv[m].at[there], **{axis: far})
            copy.start()
            self.sent.append(copy)
        copy = place.remote(src, dst, csend, crecv, core=1)
        copy.start()
        self.sent.append(copy)
        other = self.spot(m, *place.moved(core=1, **by))
        self.late.append((m, place.remote(other, other, csend, crecv, core=1)))

    def arrived(self, which):
        for m, copy in self.late:
            if m[0] in which:
                copy.wait_recv()
        self.late = [t for t in self.late if t[0][0] not in which]

    def end(self):
        self.arrived("ABCDE")
        for copy in self.sent:
            copy.wait_send()


def block_at(sh, m, ref, row, col, gathered):
    mul = pl.multiple_of
    if m[0] == "A":
        skip = sh.acut[int(m[1])]
        r = pl.ds(mul(row * sh.arows + skip, 16), sh.blocks[m][0])
        return ref.at[col, r, :] if gathered else ref.at[r, pl.ds(mul(sh.start("A", col), 128), sh.alanes)]
    if m == "B":
        r = pl.ds(mul(col * sh.brows, 16), sh.brows)
        return ref.at[row, r, :] if gathered else ref.at[r, pl.ds(mul(sh.start("B", row), 128), sh.blanes)]
    if m == "C":
        return ref.at[pl.ds(mul(row * sh.crows, 16), sh.crows), pl.ds(mul(col * sh.clanes, 128), sh.clanes)]
    if m == "D":
        return ref.at[pl.ds(mul(col * sh.drows, 16), sh.drows), pl.ds(mul(row * sh.dlanes, 128), sh.dlanes)]
    return ref.at[row * sh.ncol + col]


def start_gather(sh, mats, ins, outs, sems):
    place = Place(sh.nrow, sh.ncol)
    send, recv, csend, crecv = (dict(zip(mats, sems[t * len(mats) :])) for t in range(4))
    lsem = sems[4 * len(mats)]

    def spot(m, row, col):
        return block_at(sh, m, outs[m[0]], row, col, True)

    def first(m):
        if m[0] == "A":
            return ins["A"].at[pl.ds(sh.acut[int(m[1])], sh.blocks[m][0]), :]
        return ins[m]

    place.greet()
    own = [pltpu.make_async_copy(first(m), spot(m, *place.moved()), lsem.at[i]) for i, m in enumerate(mats)]
    for copy in own:
        copy.start()
    return Spread(place, sh, first, spot, send, recv, csend, crecv), dict(zip(mats, own))


def reduce_kernel(sh, mats, *refs):
    refs = list(refs)

    def take(names):
        return {m: refs.pop(0) for m in names}
    whole = sorted({m[0] for m in mats})
    ins = take(whole)
    aux = refs.pop(0)
    outs = take([m for m in whole if m != "E"])
    eall = refs.pop(0)
    acc, sib, rc, rb, ra = (take(mats) for _ in range(5))
    csend, crecv, send, recv = (take(mats) for _ in range(4))
    ge, lsem, erecv, ecr = refs
    place = Place(sh.nrow, sh.ncol)

    def spot(m, row, col):
        return block_at(sh, m, ins[m[0]], row, col, False)

    place.greet()
    steps = sh.steps(mats, True)
    sent = []
    for m, i, j, k in steps:
        (a, b, c), _ = sh.axes(m)
        slot, _ = sh.onward(m, i, j, k)
        by = {c: -i, b: -j, a: -k}
        copy = place.remote(spot(m, *place.moved(core=1, **by)), sib[m].at[slot], csend[m].at[0], crecv[m].at[slot], core=1)
        copy.start()
        pltpu.make_async_copy(spot(m, *place.moved(**by)), acc[m].at[slot], lsem.at[mats.index(m)]).start()
    for m in mats:
        pltpu.make_async_copy(acc[m], acc[m], lsem.at[mats.index(m)]).wait()
    for m, i, j, k in steps:
        (a, b, c), (na, nb, nc) = sh.axes(m)
        slot, onward = sh.onward(m, i, j, k)
        place.remote(sib[m].at[slot], sib[m].at[slot], csend[m].at[0], crecv[m].at[slot], core=1).wait_recv()
        terms = [(sib[m], slot)]
        for axis, far, from_slot in onward:
            buf = {a: ra, b: rb, c: rc}[axis][m]
            here = from_slot - {a: 1, b: na, c: na * nb}[axis]
            place.remote(buf.at[here], buf.at[here], send[m].at[slot], recv[m].at[from_slot], core=1).wait_recv()
            terms.append((buf, here))
        last = i == j == k == 0
        total, lanes = sh.blocks[m]

        def add(r, m=m, terms=terms, last=last, slot=slot):
            v = acc[m][slot, r, :].astype(f32)
            for ref, here in terms:
                v = v + ref[here, r, :].astype(f32)
            if not last:
                acc[m][slot, r, :] = v.astype(acc[m].dtype)
            elif m == "E":
                ge[r, :] = v
            elif m[0] == "A":
                outs["A"][pl.ds(pl.multiple_of(r.start + sh.acut[int(m[1])], 16), r.size), :] = v
            else:
                outs[m[0]][r, :] = v
        rows(total, 8 if m == "E" else (16), add)
        if last:
            continue
        if i > 0:
            axis, buf, there = c, rc, slot - na * nb
        elif j > 0:
            axis, buf, there = b, rb, slot - na
        else:
            axis, buf, there = a, ra, slot - 1
        far = k if m in DIRECT and buf is ra else 1
        copy = place.remote(acc[m].at[slot], buf[m].at[there], send[m].at[slot], recv[m].at[slot], **{axis: -far})
        copy.start()
        sent.append((m, copy))

    row, col = place.moved()
    la = lax.broadcasted_iota(jnp.int32, (1, sh.alanes), 1) + (sh.start("A", col) - col * sh.awide)
    lb = lax.broadcasted_iota(jnp.int32, (1, sh.blanes), 1) + (sh.start("B", row) - row * sh.bwide)
    er = sh.erows
    sq = jnp.zeros((1, 128), f32)
    values = [ge[0:er, :]]
    for m, ref in outs.items():
        v = ref[...]
        if m == "A":
            v = jnp.where((la >= 0) & (la < sh.awide), v, 0.0)
        if m == "B":
            v = jnp.where((lb >= 0) & (lb < sh.bwide), v, 0.0)
        values.append(v)
    for v in values:
        w = rsum(v * v)
        for c0 in range(0, w.shape[1], 128):
            sq = sq + w[:, c0 : c0 + 128]
    ge[er : er + 8, :] = jnp.concatenate([jnp.broadcast_to(sq, (8, 128)), jnp.broadcast_to(aux[...], (8, 128))], axis=1)
    eall[row * sh.ncol + col] = ge[...]
    for m, copy in sent:
        copy.wait_send()
    for m in mats:
        place.remote(sib[m], sib[m], csend[m].at[0], crecv[m].at[0], core=1).wait_send()
    one = lambda v: {"E": v}
    run = Spread(place, sh, lambda m: ge, lambda m, r, c: eall.at[r * sh.ncol + c], one(send["E"]), one(erecv), one(csend["E"]), one(ecr))
    for step in sh.steps(["E"], False):
        run.step(*step)
    run.end()


def reduce_grads(sh, mats, aux, *grads):
    S = jax.ShapeDtypeStruct
    V = pltpu.VMEM
    anyspec = pl.BlockSpec(memory_space=pl.ANY)
    vm = pl.BlockSpec(memory_space=pltpu.VMEM)
    sem = pltpu.SemaphoreType.DMA
    whole = [m for m in sorted({m[0] for m in mats}) if m != "E"]
    outs = {"A": (sh.arows, sh.alanes)} | {m: sh.blocks[m] for m in "BCD"}
    scratch = []
    for count in (
        lambda na, nb, nc: na * nb * nc, lambda na, nb, nc: na * nb * nc, lambda na, nb, nc: (nc - 1) * nb * na,
        lambda na, nb, nc: (nb - 1) * na, lambda na, nb, nc: na - 1,
    ):
        scratch += [V((count(*sh.axes(m)[1]),) + sh.blocks[m], f32 if m == "E" else bf) for m in mats]
    scratch += [sem((sh.half if m == "E" else 1,)) for m in mats] + [sem((sh.half,))] * (3 * len(mats))
    scratch += [V((sh.erows + 8, 256), f32), sem((len(mats),)), sem((sh.half,)), sem((sh.half,))]
    return pl.pallas_call(
        functools.partial(reduce_kernel, sh, mats),
        in_specs=[anyspec] * (len(whole) + 1) + [vm], out_specs=[vm] * (len(whole) + 1),
        out_shape=[S(outs[m], f32) for m in whole] + [S((sh.nrow * sh.ncol, sh.erows + 8, 256), f32)],
        scratch_shapes=scratch,
        compiler_params=pltpu.CompilerParams(collective_id=1, has_side_effects=True, vmem_limit_bytes=60 << 20),
        name="reduce_grads",
    )(*grads, aux)


def windows(sh, weights):
    row, col = lax.axis_index("row"), lax.axis_index("col")

    def put(v, which, index, wide, lanes):
        if wide == lanes:
            return v
        shift = index * wide - sh.start(which, index)
        return lax.dynamic_update_slice(jnp.zeros((v.shape[0], lanes), v.dtype), v, (0, shift))
    a, b, c, d = (w.astype(bf) for w in weights)
    return put(a, "A", col, sh.awide, sh.alanes), put(b.T, "B", row, sh.bwide, sh.blanes), c, d.T


GATHERED = ["A0", "A1", "A2", "B", "C", "D"]
REDUCED = ["A0", "A1", "A2", "B", "C", "D", "E"]


def tile_plan(sh, which):
    wide, count = (sh.awide, sh.ncol) if which == "A" else (sh.bwide, sh.nrow)
    alone, shared = [], []
    for c in range(count):
        first, end = wide * c // 128, -(-(wide * (c + 1)) // 128)
        base = sh.start(which, c) // 128
        lo = first + 1 if (wide * c) % 128 else first
        hi = end - 1 if (wide * (c + 1)) % 128 else end
        alone.append((c, lo, hi, base))
        if hi < end:
            shared.append((c, hi, base, sh.start(which, c + 1) // 128))
    return alone, shared


MOST = 6


def joiner(sh, which, src, dst, tmp, sem):
    alone, shared = tile_plan(sh, which)
    copies = []
    for c, lo, hi, at in alone:
        copies.append((src.at[c, :, pl.ds((lo - at) * 128, (hi - lo) * 128)], dst.at[:, pl.ds(lo * 128, (hi - lo) * 128)]))
    for u, (c, t, at, nxt) in enumerate(shared):
        copies.append((src.at[c, :, pl.ds((t - at) * 128, 128)], dst.at[:, pl.ds(t * 128, 128)]))
        copies.append((src.at[c + 1, :, pl.ds((t - nxt) * 128, 128)], tmp.at[u % MOST]))
    late = {len(alone) + 2 * u + 1 for u in range(MOST, len(shared))}
    make = lambda i: pltpu.make_async_copy(*copies[i], sem.at[i])
    made = [make(i) for i in range(len(copies)) if i not in late]
    for m in made:
        m.start()

    def end():
        for m in made:
            m.wait()
        for u, (c, t, at, nxt) in enumerate(shared):
            if u >= MOST:
                m = make(len(alone) + 2 * u + 1)
                m.start()
                m.wait()
            dst[:, t * 128 : (t + 1) * 128] += tmp[u % MOST]
    return end


def joiner_scratch(sh):
    V = pltpu.VMEM
    counts = [(len(a), len(s)) for a, s in (tile_plan(sh, "A"), tile_plan(sh, "B"))]
    return [V((D, 5 * D + FF + DD), bf), V((D, FF), bf)] + [V((min(max(s, 1), MOST), D, 128), bf) for _, s in counts] + [
        pltpu.SemaphoreType.DMA((a + 2 * s,)) for a, s in counts]


EG = 4 * ES
O_Q, O_P, O_F, O_E = D, 4 * D, 5 * D, 5 * D + FF


def enc_fwd_kernel(sh, pix, keep, pos3, sv, ain, bin_, cin, din,
                   y, kept, xh1, xh2, xhf, rs1, rs2, rsf, a1, a2, e16, o, qkv, p, hid, gp, awin, bwin, cout, dout,
                   x, bias, win, wout, atmp, btmp, asem, bsem, *sems):
    n = pix.shape[0]
    M = n * ES
    R = M // 2
    W = D
    run, own = start_gather(sh, GATHERED, dict(zip("ABCD", (ain, bin_, cin, din))), dict(zip("ABCD", (awin, bwin, cout, dout))), sems)
    ahead = sh.steps(["A0", "A1", "A2", "B"], False)
    for step in ahead[:4]:
        run.step(*step)

    kind = lax.rem(lax.broadcasted_iota(jnp.int32, (EG, 1), 0), ES)
    for i in range(0, n, 2):
        two = []
        for b in (i, i + 1):
            pick = (keep[b] == lax.broadcasted_iota(jnp.int32, (PATCHES, ES), 0)).astype(f32).astype(bf)
            two.append(dg(pick, pix[b], 0, 0))
            at = pos3[0:PATCHES, :], pos3[DS : DS + PATCHES, :], pos3[2 * DS : 2 * DS + PATCHES, :]
            x[b * ES : (b + 1) * ES, :] = dg(pick, at[0], 0, 0) + dg(pick, at[1], 0, 0) + dg(pick, at[2], 0, 0)
        kept[i * ES : (i + 2) * ES, :] = jnp.concatenate(two, axis=0).astype(bf)
    ki = lax.broadcasted_iota(jnp.int32, (EG, EG), 0)
    qi = lax.broadcasted_iota(jnp.int32, (EG, EG), 1)
    same = jnp.zeros((EG, EG), jnp.bool_)
    for j in range(4):
        same = same | ((ki >= j * ES) & (ki < j * ES + KEEP + 1) & (qi >= j * ES) & (qi < (j + 1) * ES))
    bias[...] = jnp.where(same, 0.0, -1e30).astype(f32)
    for step in ahead[4:]:
        run.step(*step)

    todo = sh.steps(["C", "D"], False)
    each = -(-len(todo) // 32)

    def tick(count=each):
        for _ in range(min(count, len(todo))):
            run.step(*todo.pop(0))
    tick(2)
    run.arrived("A")
    for m in ("A0", "A1", "A2"):
        own[m].wait()
    enda = joiner(sh, "A", awin, win, atmp, asem)
    run.arrived("B")
    own["B"].wait()
    endb = joiner(sh, "B", bwin, wout, btmp, bsem)
    enda()
    for lo in range(0, M, EG):
        sl = slice(lo, lo + EG)
        v = x[sl, :] + nn(kept[sl, :], win[:, 0:W]) + part(sv, 10)
        x[sl, :] = jnp.where(kind < KEEP, v, jnp.where(kind == KEEP, part(sv, 11), 0.0))
        tick()

    def ln1(r):
        xh, rs, a = norm_rows(x[r, :], part(sv, 0), part(sv, 1))
        xh1[r, :] = xh
        rs1[r, :] = rs
        a1[r, :] = a.astype(bf)
    rows(M, R, ln1)
    tick()
    qkv[:, 0:W] = (nn(a1[...], win[:, O_Q : O_Q + W]) + sv[:, OFF[2] : OFF[2] + W]).astype(bf)
    tick()
    qkv[:, W : 2 * W] = nn(a1[...], win[:, O_Q + W : O_Q + 2 * W]).astype(bf)
    tick()
    qkv[:, 2 * W :] = (nn(a1[...], win[:, O_Q + 2 * W : O_P]) + sv[:, OFF[2] + W : OFF[3]]).astype(bf)
    tick()
    for i in range(n // 4):
        for g in range(6):
            att_fwd(qkv, o, p, bias[...], slice(i * EG, (i + 1) * EG), W, g, i * 12 + g * 2, 64)
            if g % GROUPS == GROUPS - 1:
                tick(GROUPS * each)

    x[...] += nn(o[...], win[:, O_P : O_P + W]) + part(sv, 3)
    tick()

    def ln2(r):
        xh, rs, a = norm_rows(x[r, :], part(sv, 4), part(sv, 5))
        xh2[r, :] = xh
        rs2[r, :] = rs
        a2[r, :] = a.astype(bf)
    rows(M, R, ln2)
    tick()

    for c in range(0, FF, 512):
        h = nn(a2[...], win[:, O_F + c : O_F + c + 512])
        g, dg_ = gelu_pair(h + sv[:, OFF[6] + c : OFF[6] + c + 512])
        hid[:, c : c + 512] = g.astype(bf)
        gp[:, c : c + 512] = dg_.astype(bf)
        tick()
    endb()
    x[...] += nt(hid[...], wout[...]) + part(sv, 7)
    tick()

    def lnf(r):
        xh, rs, a = norm_rows(x[r, :], part(sv, 8), part(sv, 9))
        xhf[r, :] = xh
        rsf[r, :] = rs
        e16[r, :] = a.astype(bf)
    rows(M, R, lnf)
    tick()
    y[...] = nn(e16[...], win[:, O_E:]) + part(sv, 12)
    tick(len(todo))
    run.end()
    own["C"].wait()
    own["D"].wait()


GROUPS = 3


def vspec(k):
    return [pl.BlockSpec(memory_space=pltpu.VMEM)] * k


def encoder_fwd(sh, pix, keep, pos3, sv, *blocks):
    n = pix.shape[0]
    M = n * ES
    S = jax.ShapeDtypeStruct
    V = pltpu.VMEM
    sem = pltpu.SemaphoreType.DMA
    anyspec = pl.BlockSpec(memory_space=pl.ANY)
    outs = [S((M, DD), f32), S((M, D), bf), S((M, D), f32), S((M, D), f32), S((M, D), f32),
            S((M, 1), f32), S((M, 1), f32), S((M, 1), f32), S((M, D), bf), S((M, D), bf), S((M, D), bf), S((M, D), bf),
            S((M, 3 * D), bf), S((n // 4 * HEADS, EG, EG), bf), S((M, FF), bf), S((M, FF), bf)]
    weights = [S((sh.ncol, D, sh.alanes), bf), S((sh.nrow, D, sh.blanes), bf), S((DD, 4 * DD + DFF), bf), S((DD, DFF), bf)]
    out = pl.pallas_call(
        functools.partial(enc_fwd_kernel, sh),
        in_specs=vspec(4) + [anyspec] * 4, out_specs=vspec(len(outs)) + [anyspec] * 4, out_shape=outs + weights,
        scratch_shapes=[V((M, D), f32), V((EG, EG), f32)] + joiner_scratch(sh) + [sem((sh.half,))] * (4 * len(GATHERED)) + [sem((len(GATHERED),))],
        compiler_params=pltpu.CompilerParams(vmem_limit_bytes=60 << 20, collective_id=0, has_side_effects=True),
        name="encoder_fwd",
    )(pix, keep, pos3, sv, *blocks)
    return out[0], out[1 : len(outs)], out[len(outs) :]


def enc_bwd_kernel(sh, dy, dsm_in, dhw, sv, awin, bwin, kept, xh1_in, xh2, xhf_in, rs1, rs2, rsf, a1_in, a2, e16_in, o, qkv, p, hid, gp,
                   dwin, dwout, eout, dsm, etail, x, t, d16, dh16, stage, xb, ab, sem, lsem, win, wout, atmp, btmp, asem, bsem):
    def fetch(i, src, dst):
        copy = pltpu.make_async_copy(src, dst, lsem.at[i])
        copy.start()
        return copy

    at_e, at_xhf = fetch(0, e16_in, ab), fetch(1, xhf_in, xb)
    enda = joiner(sh, "A", awin, win, atmp, asem)
    endb = joiner(sh, "B", bwin, wout, btmp, bsem)
    M = dy.shape[0]
    R = M // 2
    W = D
    dsm[...] = dsm_in[...]
    head = fetch(4, dhw, eout.at[pl.ds(0, 3 * DD), :])

    def save(where, sums):
        for (i, lo), v in zip(where, sums):
            dsm[:, OFF[i] + lo : OFF[i] + lo + v.shape[1]] += v

    shots = []

    def put(out, base, value):
        width = value.shape[1]
        slot = len(shots) % 2
        if len(shots) >= 2:
            shots[-2].wait()
        stage[slot, :, 0:width] = value.astype(bf)
        copy = pltpu.make_async_copy(stage.at[slot, :, pl.ds(0, width)], out.at[:, pl.ds(base, width)], sem.at[slot])
        copy.start()
        shots.append(copy)

    def emb(r):
        v = dy[r, :]
        d16[r, 0:DD] = v.astype(bf)
        return [v]
    save([(12, 0)], rows_sum(M, R, [DD], emb))
    at_e.wait()
    put(dwin, O_E, dg(ab[...], d16[:, 0:DD], 0, 0))
    at_a = fetch(2, a1_in, ab)
    enda()
    endb()
    t[...] = nt(d16[:, 0:DD], win[:, O_E:])

    at_xhf.wait()

    def lnfb(r):
        da = t[r, :]
        xh = xb[r, :]
        dx = norm_back(da, xh, rsf[r, :], part(sv, 8))
        x[r, :] = dx
        d16[r, :] = dx.astype(bf)
        return da * xh, da, dx
    save([(8, 0), (9, 0), (7, 0)], rows_sum(M, R, [W] * 3, lnfb))
    at_xh1 = fetch(3, xh1_in, xb)
    for c in range(0, FF, W):
        put(dwout, c, dg(d16[...], hid[:, c : c + W], 0, 0))
        dh = nn(d16[...], wout[:, c : c + W]) * gp[:, c : c + W].astype(f32)
        dsm[:, OFF[6] + c : OFF[6] + c + W] += rsum(dh)
        dh16[:, c : c + W] = dh.astype(bf)
        put(dwin, O_F + c, dg(a2[...], dh16[:, c : c + W], 0, 0))
    t[...] = nt(dh16[...], win[:, O_F:O_E])
    dqkv = dh16

    def ln2b(r):
        da = t[r, :]
        xh = xh2[r, :]
        dx = x[r, :] + norm_back(da, xh, rs2[r, :], part(sv, 4))
        x[r, :] = dx
        d16[r, :] = dx.astype(bf)
        return da * xh, da, dx
    save([(4, 0), (5, 0), (3, 0)], rows_sum(M, R, [W] * 3, ln2b))
    put(dwin, O_P, dg(o[...], d16[...], 0, 0))
    d16[...] = nt(d16[...], win[:, O_P:O_F]).astype(bf)

    @pl.loop(0, M // EG)
    def _(i):
        rsl = pl.ds(pl.multiple_of(i * EG, 16), EG)
        for g in range(6):
            att_bwd(qkv, d16, p, dqkv, rsl, W, g, i * 12 + g * 2, 64)

    at_a.wait()
    for c in range(0, 3 * D, W):
        put(dwin, O_Q + c, dg(ab[...], dqkv[:, c : c + W], 0, 0))
    save([(2, 0), (2, W)], rows_sum(M, R, [W, W], lambda r: [dqkv[r, 0:W].astype(f32), dqkv[r, 2 * W : 3 * W].astype(f32)]))
    t[...] = nt(dqkv[:, 0 : 3 * W], win[:, O_Q:O_P])
    at_xh1.wait()

    def ln1b(r):
        da = t[r, :]
        xh = xb[r, :]
        dx = x[r, :] + norm_back(da, xh, rs1[r, :], part(sv, 0))
        kind = lax.rem(lax.broadcasted_iota(jnp.int32, (r.size, 1), 0), ES)
        only = jnp.where(kind < KEEP, dx, 0.0)
        d16[r, :] = only.astype(bf)
        return da * xh, da, jnp.where(kind == KEEP, dx, 0.0), only
    save([(0, 0), (1, 0), (11, 0), (10, 0)], rows_sum(M, R, [W] * 4, ln1b))
    put(dwin, 0, dg(kept[...], d16[...], 0, 0))
    etail[...] = jnp.zeros_like(etail)
    for i in range(SMALL // 256):
        etail[i : i + 1, :] = dsm[:, i * 256 : (i + 1) * 256]
    tail = fetch(5, etail, eout.at[pl.ds(3 * DD, etail.shape[0]), :])
    for c in shots[-2:] + [head, tail]:
        c.wait()


def encoder_bwd(sh, dy, dsm, dhw, sv, awin, bwin, saved):
    M = dy.shape[0]
    count = sh.nrow * sh.ncol * sh.erows
    S = jax.ShapeDtypeStruct
    V = pltpu.VMEM
    anyspec = pl.BlockSpec(memory_space=pl.ANY)
    return pl.pallas_call(
        functools.partial(enc_bwd_kernel, sh),
        in_specs=[anyspec if i in (2, 4, 5, 7, 9, 13, 15) else spec for i, spec in enumerate(vspec(6 + len(saved)))],
        out_specs=[anyspec] * 3,
        out_shape=[S((D, 5 * D + FF + DD), bf), S((D, FF), bf), S((count, 256), f32)],
        scratch_shapes=[V((1, SMALL), f32), V((count - 3 * DD, 256), f32), V((M, D), f32), V((M, D), f32), V((M, D), bf), V((M, FF), bf), V((2, D, D), bf), V((M, D), f32), V((M, D), bf),
                        pltpu.SemaphoreType.DMA((2,)), pltpu.SemaphoreType.DMA((6,))] + joiner_scratch(sh),
        compiler_params=pltpu.CompilerParams(vmem_limit_bytes=63 << 20),
        name="encoder_bwd",
    )(dy, dsm, dhw, sv, awin, bwin, *saved)


def sincos_np(width):
    quarter = width // 4
    freq = (1.0 / np.float32(10000.0) ** (np.arange(quarter, dtype=np.float32) / np.float32(quarter))).astype(np.float32)
    pos = np.arange(GRID * GRID)
    cp = (pos % GRID).astype(np.float32)[:, None] * freq[None, :]
    rp = (pos // GRID).astype(np.float32)[:, None] * freq[None, :]
    return np.concatenate([np.sin(cp), np.cos(cp), np.sin(rp), np.cos(rp)], axis=1).astype(np.float32)


def tables():
    dec = np.zeros((DS, DD), np.float32)
    dec[:PATCHES] = sincos_np(DD)
    enc = np.zeros((DS, D), np.float32)
    enc[:PATCHES] = sincos_np(D)
    b = ml_dtypes.bfloat16
    hi = enc.astype(b)
    mid = (enc - hi.astype(np.float32)).astype(b)
    lo = (enc - hi.astype(np.float32) - mid.astype(np.float32)).astype(b)
    return dec, np.concatenate([hi, mid, lo], axis=0)


def adamw(weight, first, second, grad):
    first = 0.9 * first + (1.0 - 0.9) * grad
    second = 0.999 * second + (1.0 - 0.999) * grad * grad
    first_hat = first / (1.0 - 0.9**STEP)
    second_hat = second / (1.0 - 0.999**STEP)
    weight = weight - 0.08 * (first_hat / (jnp.sqrt(second_hat) + 1e-08) + 0.05 * weight)
    return (weight, first, second)


def update_kernel(sh, ga, gb, gc, gd, eall, *refs):
    weights, firsts, seconds = refs[0:6], refs[6:12], refs[12:18]
    new, mo, vo = refs[18:24], refs[24:30], refs[30:36]
    result, e2d = refs[36], refs[37]
    er = sh.erows
    row, col = lax.axis_index("row"), lax.axis_index("col")
    squares = jnp.zeros((1, 128), f32)
    losses = jnp.zeros((1, 128), f32)
    for i in range(sh.nrow * sh.ncol):
        e2d[i * er : (i + 1) * er, :] = eall[i, 0:er, :]
        squares = squares + eall[i, er : er + 1, 0:128]
        losses = losses + eall[i, er : er + 1, 128:256]
    norm = jnp.sqrt(jnp.sum(squares, axis=1, keepdims=True))
    factor = 0.0001 / jnp.maximum(norm, 0.0001)
    result[...] = jnp.where(lax.broadcasted_iota(jnp.int32, (1, 128), 1) == 0, losses, norm)

    def aligned(g, which, index, wide, lanes):
        if wide == lanes:
            return g
        return pltpu.roll(g, lax.rem(lanes - (index * wide - sh.start(which, index)), lanes), 1)[:, 0:wide]

    def apply(i, at, grad):
        out = adamw(weights[i][at], firsts[i][at], seconds[i][at], grad * factor)
        new[i][at], mo[i][at], vo[i][at] = out

    every = (slice(None), slice(None))
    apply(0, every, aligned(ga[...], "A", col, sh.awide, sh.alanes))
    apply(1, every, aligned(gb[...], "B", row, sh.bwide, sh.blanes))
    apply(2, every, gc[...])
    apply(3, every, gd[...])
    for c in range(0, PIX, 256):
        apply(4, (slice(None), slice(c, c + 256)), e2d[2 * c : 2 * c + DD, :])
    for i in range(SMALL // 256):
        for h in (0, 1):
            apply(5, (slice(2 * i + h, 2 * i + h + 1), slice(None)), e2d[3 * DD + i : 3 * DD + i + 1, h * 128 : (h + 1) * 128])


def update(sh, grads, weights, firsts, seconds):
    S = jax.ShapeDtypeStruct
    turn = lambda t: [v.T if i % 6 in (1, 3) else v for i, v in enumerate(t)]
    flat = lambda t: turn([v.reshape(SMALL // 128, 128) if v.ndim == 1 else v for v in t])
    state = flat(weights) + flat(firsts) + flat(seconds)
    outs = pl.pallas_call(
        functools.partial(update_kernel, sh),
        in_specs=vspec(5 + 18), out_specs=vspec(19),
        out_shape=[S(v.shape, f32) for v in state] + [S((1, 128), f32)],
        scratch_shapes=[pltpu.VMEM((sh.nrow * sh.ncol * sh.erows, 256), f32)],
        compiler_params=pltpu.CompilerParams(vmem_limit_bytes=60 << 20),
        name="update",
    )(*grads, *state)
    small = lambda v: v.reshape(SMALL) if v.shape == (SMALL // 128, 128) else v
    return tuple(turn([small(v) for v in outs[:18]])) + (outs[18][0, 0], outs[18][0, 1])


def local(pixels, keep_idx, restore, *state):
    weights, firsts, seconds = state[0:6], state[6:12], state[12:18]
    nrow, ncol = lax.axis_size("row"), lax.axis_size("col")
    sh = Shapes(nrow, ncol)
    n = pixels.shape[0]
    denom = 1.0 * n * nrow * ncol * (PATCHES - KEEP)

    dec_pos, enc_pos = tables()
    fill = lambda count, value: jnp.full((n, count), value, jnp.int32)
    keep = jnp.concatenate([keep_idx, fill(ES - KEEP, NOROW)], axis=1).reshape(n, 1, ES)
    code = jnp.concatenate([jnp.where(restore < KEEP, restore, 64), fill(1, KEEP), fill(DS - PATCHES - 1, NOROW)], axis=1)
    head, sv = weights[4], weights[5].reshape(1, SMALL)

    y, saved, (aw, bw, c, dt) = encoder_fwd(sh, pixels, keep, jnp.asarray(enc_pos), sv, *windows(sh, weights[0:4]))
    dy, dc, ddt, dhead, dsm, loss = decoder(
        y.reshape(n, ES, DD), code.reshape(n, 1, DS), pixels, jnp.asarray(dec_pos), sv, c, dt, head, 1.0 / denom)
    da, dbt, shared = encoder_bwd(sh, dy.reshape(n * ES, DD), dsm, dhead, sv, aw, bw, saved)
    sums = reduce_grads(sh, REDUCED, loss, da, dbt, dc, ddt, shared.reshape(nrow * ncol, sh.erows, 256))
    return update(sh, sums, weights, firsts, seconds)


def solution(mesh):
    both = P(("row", "col"))
    big = [P("row", "col")] * 4 + [P()] * 2
    return jax.shard_map(
        local,
        mesh=mesh,
        in_specs=(both, both, both, *big, *big, *big),
        out_specs=(*big, *big, *big, P(), P()),
        check_vma=False,
    )
```

```python
import functools
import math

import jax
import jax.numpy as jnp
import ml_dtypes
import numpy as np
from jax import lax
from jax.experimental import pallas as pl
from jax.experimental.pallas import tpu as pltpu
from jax.sharding import PartitionSpec as P

D = 768
HEADS = 12
FF = 3072
DD = 512
DHEADS = 16
DFF = 2048
PIX = 768
GRID = 14
PATCHES = 196
KEEP = 49
STEP = 10
SMALL = 21248
ES = 56
DS = 208
SEL = 80
NOROW = 255
f32 = jnp.float32
bf = jnp.bfloat16

LENS = [
    D, D, 2 * D, D, D, D, FF, D, D, D, D, D,
    DD, DD, DD, DD, 2 * DD, DD, DD, DD, DFF, DD, DD, DD, PIX,
]
OFF = [0]
for piece in LENS:
    OFF.append(OFF[-1] + piece)


def part(ref, i):
    return ref[:, OFF[i] : OFF[i + 1]]


def dg(a, b, ca, cb):
    return lax.dot_general(a, b, (((ca,), (cb,)), ((), ())), preferred_element_type=f32)


def nn(a, b):
    return dg(a, b, 1, 0)


def nt(a, b):
    return dg(a, b, 1, 1)


def rows(total, size, fn):
    @pl.loop(0, total // size)
    def _(i):
        fn(pl.ds(pl.multiple_of(i * size, size), size))


def rows_sum(total, size, widths, fn):
    def body(i, carry):
        parts = fn(pl.ds(pl.multiple_of(i * size, size), size))
        return tuple(c + jnp.sum(v.reshape(size // 8, 8, v.shape[1]), axis=0) for c, v in zip(carry, parts))
    carry = lax.fori_loop(0, total // size, body, tuple(jnp.zeros((8, w), f32) for w in widths))
    return [rsum(c) for c in carry]


def pieces(x):
    hi = x.astype(bf)
    rest = x - hi.astype(f32)
    mid = rest.astype(bf)
    low = (rest - mid.astype(f32)).astype(bf)
    return hi, mid, low


def gelu_pair(x):
    ax = jnp.abs(x)
    d = 1.0 + (0.3275911 * 0.7071067811865476) * ax
    r = pl.reciprocal(d, approx=True)
    t = r * (2.0 - d * r)
    e = jnp.exp(-0.5 * (x * x))
    poly = ((((0.5 * 1.061405429 * t - 0.5 * 1.453152027) * t + 0.5 * 1.421413741) * t
             - 0.5 * 0.284496736) * t + 0.5 * 0.254829592) * t
    q = poly * e
    phi = jnp.where(x >= 0.0, 1.0 - q, q)
    return x * phi, phi + x * (e * 0.3989422804014327)


def norm_rows(x, gain, shift):
    c = x - jnp.mean(x, axis=1, keepdims=True)
    rs = lax.rsqrt(jnp.mean(c * c, axis=1, keepdims=True) + 1e-06)
    xh = c * rs
    return xh, rs, xh * gain + shift


def norm_back(da, xh, rs, gain):
    g = da * gain
    m1 = jnp.mean(g, axis=1, keepdims=True)
    m2 = jnp.mean(g * xh, axis=1, keepdims=True)
    return rs * (g - m1 - xh * m2)


def rsum(x):
    return jnp.sum(x, axis=0, keepdims=True)


def lanes_of(x, h, hd):
    lane = lax.broadcasted_iota(jnp.int32, (1, 128), 1)
    return jnp.where((lane >= h * hd) & (lane < (h + 1) * hd), x, jnp.zeros_like(x))


def stack(x, hd):
    return jnp.concatenate([lanes_of(x, h, hd) for h in range(128 // hd)], axis=0)


def unstack(x, hd):
    n = x.shape[0] * hd // 128
    out = None
    for h in range(128 // hd):
        t = lanes_of(x[h * n : (h + 1) * n], h, hd)
        out = t if out is None else out + t
    return out


def att_fwd(qkv, o, p, bias, rsl, width, g, slot, hd):
    c0 = g * 128
    q = qkv[rsl, c0 : c0 + 128]
    k = qkv[rsl, c0 + width : c0 + width + 128]
    v = qkv[rsl, c0 + 2 * width : c0 + 2 * width + 128]
    n = q.shape[0]
    every = nt(stack(k, hd), q)
    probs = []
    for h in range(128 // hd):
        s = every[h * n : (h + 1) * n] * (hd ** -0.5 * 1.4426950408889634) + bias
        e = jnp.exp2(s - jnp.max(s, axis=0, keepdims=True))
        pr = (e * (1.0 / jnp.sum(e, axis=0, keepdims=True))).astype(bf)
        p[slot + h] = pr
        probs.append(pr)
    o[rsl, c0 : c0 + 128] = dg(jnp.concatenate(probs, axis=0), stack(v, hd), 0, 0).astype(bf)


def att_bwd(qkv, do, p, dqkv, rsl, width, g, slot, hd):
    c0 = g * 128
    c1, c2 = c0 + width, c0 + 2 * width
    q = qkv[rsl, c0 : c0 + 128]
    k = qkv[rsl, c1 : c1 + 128]
    v = qkv[rsl, c2 : c2 + 128]
    d = do[rsl, c0 : c0 + 128]
    n = q.shape[0]
    probs = jnp.concatenate([p[slot + h] for h in range(128 // hd)], axis=0)
    every = nt(stack(v, hd), d)
    back = []
    for h in range(128 // hd):
        pf = probs[h * n : (h + 1) * n].astype(f32)
        t = pf * every[h * n : (h + 1) * n].astype(bf).astype(f32)
        back.append(((t - pf * jnp.sum(t, axis=0, keepdims=True)) * (hd ** -0.5)).astype(bf))
    back = jnp.concatenate(back, axis=0)
    dqkv[rsl, c0 : c0 + 128] = dg(back, stack(k, hd), 0, 0).astype(bf)
    dqkv[rsl, c1 : c1 + 128] = unstack(nn(back, q), hd).astype(bf)
    dqkv[rsl, c2 : c2 + 128] = unstack(nn(probs, d), hd).astype(bf)


def dec_kernel(scale, nb, y, coder, pix, pos, sv, win, wout, hw,
               dy, win_out, wout_out, dhw, dsm, loss,
               dwin, dwout, x, t, xh1, xh2, xhf, rs1, rs2, rsf, tm, tr, a1, a2, u, o, qkv, p, hid, gp, dpr, d16, hide, lacc):
    M = nb * DS
    R = M
    W = DD

    @pl.when(pl.program_id(0) == 0)
    def _():
        dsm[...] = jnp.zeros_like(dsm)
        loss[...] = jnp.zeros_like(loss)
        lacc[...] = jnp.zeros_like(lacc)
        dpr[...] = jnp.zeros_like(dpr)
        for ref in (dwin, dwout, dhw):
            rows(ref.shape[0], 16, lambda r: ref.__setitem__((r, slice(None)), jnp.zeros((16, ref.shape[1]), f32)))

    def put(where, sums):
        for (i, lo), v in zip(where, sums):
            dsm[:, OFF[i] + lo : OFF[i] + lo + v.shape[1]] += v

    for b in range(nb):
        pick = (coder[b] == lax.broadcasted_iota(jnp.int32, (SEL, DS), 0)).astype(f32).astype(bf)
        tok = jnp.where(lax.broadcasted_iota(jnp.int32, (8, W), 0) == 0, part(sv, 13), 0.0)
        table = jnp.concatenate([y[b], jnp.zeros((8, W), f32), tok, jnp.zeros((8, W), f32)], axis=0)
        z = pos[...]
        for piece in pieces(table):
            z = z + dg(pick, piece, 0, 0)
        x[b * DS : (b + 1) * DS, :] = z
        mark = (lax.broadcasted_iota(jnp.int32, (SEL, 128), 0) == 64).astype(f32).astype(bf)
        hide[b * DS : (b + 1) * DS, :] = dg(pick, mark, 0, 0)[:, 0:1]

    def ln1(r):
        xh, rs, a = norm_rows(x[r, :], part(sv, 14), part(sv, 15))
        xh1[r, :] = xh
        rs1[r, :] = rs
        a1[r, :] = a.astype(bf)
    rows(M, R, ln1)

    qkv[:, 0:W] = (nn(a1[...], win[:, 0:W]) + sv[:, OFF[16] : OFF[16] + W]).astype(bf)
    qkv[:, W : 2 * W] = nn(a1[...], win[:, W : 2 * W]).astype(bf)
    qkv[:, 2 * W :] = (nn(a1[...], win[:, 2 * W : 3 * W]) + sv[:, OFF[16] + W : OFF[17]]).astype(bf)

    bias = jnp.where(lax.broadcasted_iota(jnp.int32, (DS, 1), 0) <= PATCHES, 0.0, -1e30).astype(f32)

    for i in range(nb):
        rsl = slice(i * DS, (i + 1) * DS)
        for g in range(4):
            att_fwd(qkv, o, p, bias, rsl, W, g, i * 16 + g * 4, 32)

    x[...] += nn(o[...], win[:, 3 * W : 4 * W]) + part(sv, 17)

    def ln2(r):
        xh, rs, a = norm_rows(x[r, :], part(sv, 18), part(sv, 19))
        xh2[r, :] = xh
        rs2[r, :] = rs
        a2[r, :] = a.astype(bf)
    rows(M, R, ln2)

    CW = 512
    for c in range(0, DFF, CW):
        h = nn(a2[...], win[:, 4 * W + c : 4 * W + c + CW])
        g, dg_ = gelu_pair(h + sv[:, OFF[20] + c : OFF[20] + c + CW])
        hid[:, c : c + CW] = g.astype(bf)
        gp[:, c : c + CW] = dg_.astype(bf)

    x[...] += nt(hid[...], wout[...]) + part(sv, 21)

    def lnf(r):
        xh, rs, a = norm_rows(x[r, :], part(sv, 22), part(sv, 23))
        xhf[r, :] = xh
        rsf[r, :] = rs
        u[r, :] = a.astype(bf)
    rows(M, R, lnf)

    for b in range(nb):
        v = pix[b].astype(f32)
        m = jnp.mean(v, axis=1, keepdims=True)
        c = v - m
        tm[b * DS : b * DS + PATCHES, :] = m
        tr[b * DS : b * DS + PATCHES, :] = lax.rsqrt(jnp.mean(c * c, axis=1, keepdims=True) + 1e-06)

    for c in range(0, PIX, 256):
        pr = nn(u[...], hw[:, c : c + 256].astype(bf)) + sv[:, OFF[24] + c : OFF[24] + c + 256]
        for b in range(nb):
            sl = slice(b * DS, b * DS + PATCHES)
            tgt = (pix[b, :, c : c + 256].astype(f32) - tm[sl, :]) * tr[sl, :]
            diff = jnp.where(hide[sl, :] > 0.5, pr[sl] - tgt, 0.0)
            lacc[...] += rsum(diff * diff)
            dp = diff * (2.0 * scale / PIX)
            dsm[:, OFF[24] + c : OFF[24] + c + 256] += rsum(dp)
            dpr[sl, c : c + 256] = dp.astype(bf)

    for c in range(0, PIX, 256):
        dhw[2 * c : 2 * c + DD, :] += dg(u[...], dpr[:, c : c + 256], 0, 0)
    t[...] = nt(dpr[...], hw[...].astype(bf))

    def lnfb(r):
        da = t[r, :]
        xh = xhf[r, :]
        dx = norm_back(da, xh, rsf[r, :], part(sv, 22))
        x[r, :] = dx
        d16[r, :] = dx.astype(bf)
        return da * xh, da, dx
    put([(22, 0), (23, 0), (21, 0)], rows_sum(M, R, [W] * 3, lnfb))

    dwout[...] += dg(d16[...], hid[...], 0, 0)
    for c in range(0, DFF, CW):
        dh = nn(d16[...], wout[:, c : c + CW]) * gp[:, c : c + CW].astype(f32)
        dsm[:, OFF[20] + c : OFF[20] + c + CW] += rsum(dh)
        gp[:, c : c + CW] = dh.astype(bf)
    dwin[:, 4 * W :] += dg(a2[...], gp[...], 0, 0)
    t[...] = nt(gp[...], win[:, 4 * W :])

    def ln2b(r):
        da = t[r, :]
        xh = xh2[r, :]
        dx = x[r, :] + norm_back(da, xh, rs2[r, :], part(sv, 18))
        x[r, :] = dx
        d16[r, :] = dx.astype(bf)
        return da * xh, da, dx
    put([(18, 0), (19, 0), (17, 0)], rows_sum(M, R, [W] * 3, ln2b))

    dwin[:, 3 * W : 4 * W] += dg(o[...], d16[...], 0, 0)
    o[...] = nt(d16[...], win[:, 3 * W : 4 * W]).astype(bf)
    dqkv = gp

    for i in range(nb):
        rsl = slice(i * DS, (i + 1) * DS)
        for g in range(4):
            att_bwd(qkv, o, p, dqkv, rsl, W, g, i * 16 + g * 4, 32)

    dwin[:, 0 : 3 * W] += dg(a1[...], dqkv[:, 0 : 3 * W], 0, 0)
    put([(16, 0), (16, W)], rows_sum(M, R, [W, W], lambda r: [dqkv[r, 0:W].astype(f32), dqkv[r, 2 * W : 3 * W].astype(f32)]))
    t[...] = nt(dqkv[:, 0 : 3 * W], win[:, 0 : 3 * W])

    def ln1b(r):
        da = t[r, :]
        xh = xh1[r, :]
        x[r, :] = x[r, :] + norm_back(da, xh, rs1[r, :], part(sv, 14))
        return da * xh, da
    put([(14, 0), (15, 0)], rows_sum(M, R, [W] * 2, ln1b))

    for b in range(nb):
        pick = (coder[b] == lax.broadcasted_iota(jnp.int32, (SEL, DS), 0)).astype(f32).astype(bf)
        out = None
        for piece in pieces(x[b * DS : (b + 1) * DS, :]):
            v = nn(pick, piece)
            out = v if out is None else out + v
        dy[b] = out[0:ES]
        dsm[:, OFF[13] : OFF[14]] += out[64:65]

    @pl.when(pl.program_id(0) == pl.num_programs(0) - 1)
    def _():
        loss[...] = jnp.broadcast_to(jnp.sum(lacc[...], axis=1, keepdims=True) * (scale / PIX), (1, 128))
        for src, dst in ((dwin, win_out), (dwout, wout_out)):
            rows(DD, 16, lambda r: dst.__setitem__((r, slice(None)), src[r, :].astype(bf)))


def decoder(y, coder, pix, pos, sv, win, wout, hw, scale, nb=2):
    n = y.shape[0]
    M = nb * DS
    whole = lambda a: pl.BlockSpec(a.shape, lambda i: (0,) * a.ndim, pipeline_mode=pl.Buffered(1))
    fixed = lambda s: pl.BlockSpec(s, lambda i: (0,) * len(s), pipeline_mode=pl.Buffered(1))
    blk = lambda s: pl.BlockSpec((nb,) + s, lambda i: (i, 0, 0))
    V = pltpu.VMEM
    return pl.pallas_call(
        functools.partial(dec_kernel, scale, nb),
        grid=(n // nb,),
        in_specs=[blk((ES, DD)), blk((1, DS)), blk((PATCHES, PIX)), whole(pos), whole(sv), whole(win), whole(wout), whole(hw)],
        out_specs=[blk((ES, DD)), fixed(win.shape), fixed(wout.shape), fixed((3 * DD, 256)), fixed((1, SMALL)), fixed((1, 128))],
        out_shape=[
            jax.ShapeDtypeStruct((n, ES, DD), f32), jax.ShapeDtypeStruct(win.shape, bf),
            jax.ShapeDtypeStruct(wout.shape, bf), jax.ShapeDtypeStruct((3 * DD, 256), f32),
            jax.ShapeDtypeStruct((1, SMALL), f32), jax.ShapeDtypeStruct((1, 128), f32)],
        scratch_shapes=[
            V(win.shape, f32), V(wout.shape, f32),
            V((M, DD), f32), V((M, DD), f32), V((M, DD), f32), V((M, DD), f32), V((M, DD), f32),
            V((M, 1), f32), V((M, 1), f32), V((M, 1), f32), V((M, 1), f32), V((M, 1), f32),
            V((M, DD), bf), V((M, DD), bf), V((M, DD), bf), V((M, DD), bf), V((M, 3 * DD), bf),
            V((nb * DHEADS, DS, DS), bf), V((M, DFF), bf), V((M, DFF), bf), V((M, PIX), bf), V((M, DD), bf), V((M, 1), f32),
            V((1, 256), f32)],
        compiler_params=pltpu.CompilerParams(vmem_limit_bytes=60 << 20),
        name="decoder",
    )(y, coder, pix, pos, sv, win, wout, hw)


class Place:
    def __init__(self, nrow, ncol):
        side = math.isqrt(nrow)
        self.nrow, self.ncol = nrow, ncol
        self.n = {"x": side, "y": nrow // side, "z": ncol // 2}
        row, col = lax.axis_index("row"), lax.axis_index("col")
        self.at = {"x": row % side, "y": row // side, "z": col // 2, "core": col % 2}

    def moved(self, **by):
        at = {}
        for k, v in self.at.items():
            step = by.get(k, 0)
            size = 2 if k == "core" else self.n[k]
            at[k] = v if step % size == 0 else lax.rem(v + (step % size), size)
        return at["y"] * self.n["x"] + at["x"], at["z"] * 2 + at["core"]

    def greet(self):
        sem = pltpu.get_barrier_semaphore()
        count = 0
        for axis in ("x", "y", "z", "core"):
            size = 2 if axis == "core" else self.n[axis]
            for step in range(1, size):
                pl.semaphore_signal(sem, inc=1, device_id=self.moved(**{axis: step}), device_id_type=pl.DeviceIdType.MESH)
                count += 1
        pl.semaphore_wait(sem, count)

    def remote(self, src, dst, ssem, rsem, **by):
        return pltpu.make_async_remote_copy(src, dst, ssem, rsem, device_id=self.moved(**by), device_id_type=pl.DeviceIdType.MESH)


ORDER = {
    "A0": ("z", "x", "y"), "A1": ("z", "y", "x"), "A2": ("x", "y", "z"), "B": ("z", "y", "x"),
    "C": ("z", "x", "y"), "D": ("y", "x", "z"), "E": ("z", "y", "x"),
}
DIRECT = ("E",)


class Shapes:
    def __init__(self, nrow, ncol):
        self.nrow, self.ncol = nrow, ncol
        self.half = nrow * ncol // 2
        side = math.isqrt(nrow)
        self.n = {"x": side, "y": nrow // side, "z": ncol // 2}
        self.awide, self.bwide = (5 * D + FF + DD) // ncol, FF // nrow
        self.alanes, self.blanes = self.window(self.awide, ncol), self.window(self.bwide, nrow)
        self.arows, self.brows = D // nrow, D // ncol
        cut = [self.arows * t // 12 // 16 * 16 for t in (5, 4)]
        self.acut = (0, cut[0], cut[0] + cut[1], self.arows)
        self.crows, self.clanes = DD // nrow, (4 * DD + DFF) // ncol
        self.drows, self.dlanes = DD // ncol, DFF // nrow
        self.erows = -(-(DD * PIX + SMALL) // (nrow * ncol * 256 * 8)) * 8
        self.blocks = {
            "A0": (cut[0], self.alanes), "A1": (cut[1], self.alanes), "A2": (self.arows - self.acut[2], self.alanes), "B": (self.brows, self.blanes),
            "C": (self.crows, self.clanes), "D": (self.drows, self.dlanes), "E": (self.erows, 256)}

    @staticmethod
    def window(wide, count):
        return max(-(-((wide * c) % 128 + wide) // 128) * 128 for c in range(count))

    def start(self, which, index):
        wide, lanes, total = (self.awide, self.alanes, 5 * D + FF + DD) if which == "A" else (self.bwide, self.blanes, FF)
        first = (wide * index) // 128
        last = (total - lanes) // 128
        if isinstance(index, int):
            return min(first, last) * 128
        return jnp.minimum(first, last) * 128

    def axes(self, m):
        return ORDER[m], tuple(self.n[a] for a in ORDER[m])

    def steps(self, mats, back, keys=False):
        out = []
        for pos, m in enumerate(mats):
            _, (na, nb, nc) = self.axes(m)
            for i in range(nc):
                for j in range(nb):
                    for k in range(na):
                        key = (na - 1 - k) + (nb - 1 - j) + (nc - 1 - i) if back else i + j + (min(k, 1) if m in DIRECT else k)
                        out.append((key, pos, m, i, j, k))
        return [t if keys else t[2:] for t in sorted(out)]

    def onward(self, m, i, j, k):
        (a, b, c), (na, nb, nc) = self.axes(m)
        slot = (i * nb + j) * na + k
        out = []
        if m in DIRECT and i == j == k == 0:
            out += [(a, t, t) for t in range(1, na)]
        if m not in DIRECT and i == j == 0 and k < na - 1:
            out.append((a, 1, slot + 1))
        if i == 0 and j < nb - 1:
            out.append((b, 1, slot + na))
        if i < nc - 1:
            out.append((c, 1, slot + na * nb))
        return slot, out


class Spread:
    def __init__(self, place, sh, first, spot, send, recv, csend, crecv):
        self.place, self.sh, self.first, self.spot = place, sh, first, spot
        self.send, self.recv, self.csend, self.crecv = send, recv, csend, crecv
        self.sent, self.late = [], []

    def step(self, m, i, j, k):
        place = self.place
        (a, b, c), _ = self.sh.axes(m)
        slot, onward = self.sh.onward(m, i, j, k)
        by = {c: -i, b: -j, a: -k}
        dst = self.spot(m, *place.moved(**by))
        own = i == j == k == 0
        src = self.first(m) if own else dst
        csend, crecv = self.csend[m].at[slot], self.crecv[m].at[slot]
        if not own:
            place.remote(dst, dst, self.send[m].at[slot], self.recv[m].at[slot], core=1).wait_recv()
        for axis, far, there in onward:
            copy = place.remote(src, dst, self.send[m].at[there], self.recv[m].at[there], **{axis: far})
            copy.start()
            self.sent.append(copy)
        copy = place.remote(src, dst, csend, crecv, core=1)
        copy.start()
        self.sent.append(copy)
        other = self.spot(m, *place.moved(core=1, **by))
        self.late.append((m, place.remote(other, other, csend, crecv, core=1)))

    def arrived(self, which):
        for m, copy in self.late:
            if m[0] in which:
                copy.wait_recv()
        self.late = [t for t in self.late if t[0][0] not in which]

    def end(self):
        self.arrived("ABCDE")
        for copy in self.sent:
            copy.wait_send()


def block_at(sh, m, ref, row, col, gathered):
    mul = pl.multiple_of
    if m[0] == "A":
        skip = sh.acut[int(m[1])]
        r = pl.ds(mul(row * sh.arows + skip, 16), sh.blocks[m][0])
        return ref.at[col, r, :] if gathered else ref.at[r, pl.ds(mul(sh.start("A", col), 128), sh.alanes)]
    if m == "B":
        r = pl.ds(mul(col * sh.brows, 16), sh.brows)
        return ref.at[row, r, :] if gathered else ref.at[r, pl.ds(mul(sh.start("B", row), 128), sh.blanes)]
    if m == "C":
        return ref.at[pl.ds(mul(row * sh.crows, 16), sh.crows), pl.ds(mul(col * sh.clanes, 128), sh.clanes)]
    if m == "D":
        return ref.at[pl.ds(mul(col * sh.drows, 16), sh.drows), pl.ds(mul(row * sh.dlanes, 128), sh.dlanes)]
    return ref.at[row * sh.ncol + col]


def start_gather(sh, mats, ins, outs, sems):
    place = Place(sh.nrow, sh.ncol)
    send, recv, csend, crecv = (dict(zip(mats, sems[t * len(mats) :])) for t in range(4))
    lsem = sems[4 * len(mats)]

    def spot(m, row, col):
        return block_at(sh, m, outs[m[0]], row, col, True)

    def first(m):
        if m[0] == "A":
            return ins["A"].at[pl.ds(sh.acut[int(m[1])], sh.blocks[m][0]), :]
        return ins[m]

    place.greet()
    own = [pltpu.make_async_copy(first(m), spot(m, *place.moved()), lsem.at[i]) for i, m in enumerate(mats)]
    for copy in own:
        copy.start()
    return Spread(place, sh, first, spot, send, recv, csend, crecv), dict(zip(mats, own))


def reduce_kernel(sh, mats, *refs):
    refs = list(refs)

    def take(names):
        return {m: refs.pop(0) for m in names}
    whole = sorted({m[0] for m in mats})
    ins = take(whole)
    aux = refs.pop(0)
    outs = take([m for m in whole if m != "E"])
    eall = refs.pop(0)
    acc, sib, rc, rb, ra = (take(mats) for _ in range(5))
    csend, crecv, send, recv = (take(mats) for _ in range(4))
    ge, lsem, erecv, ecr = refs
    place = Place(sh.nrow, sh.ncol)

    def spot(m, row, col):
        return block_at(sh, m, ins[m[0]], row, col, False)

    place.greet()
    steps = sh.steps(mats, True)
    sent = []
    for m, i, j, k in steps:
        (a, b, c), _ = sh.axes(m)
        slot, _ = sh.onward(m, i, j, k)
        by = {c: -i, b: -j, a: -k}
        copy = place.remote(spot(m, *place.moved(core=1, **by)), sib[m].at[slot], csend[m].at[0], crecv[m].at[slot], core=1)
        copy.start()
        pltpu.make_async_copy(spot(m, *place.moved(**by)), acc[m].at[slot], lsem.at[mats.index(m)]).start()
    for m in mats:
        pltpu.make_async_copy(acc[m], acc[m], lsem.at[mats.index(m)]).wait()
    for m, i, j, k in steps:
        (a, b, c), (na, nb, nc) = sh.axes(m)
        slot, onward = sh.onward(m, i, j, k)
        place.remote(sib[m].at[slot], sib[m].at[slot], csend[m].at[0], crecv[m].at[slot], core=1).wait_recv()
        terms = [(sib[m], slot)]
        for axis, far, from_slot in onward:
            buf = {a: ra, b: rb, c: rc}[axis][m]
            here = from_slot - {a: 1, b: na, c: na * nb}[axis]
            place.remote(buf.at[here], buf.at[here], send[m].at[slot], recv[m].at[from_slot], core=1).wait_recv()
            terms.append((buf, here))
        last = i == j == k == 0
        total, lanes = sh.blocks[m]

        def add(r, m=m, terms=terms, last=last, slot=slot):
            v = acc[m][slot, r, :].astype(f32)
            for ref, here in terms:
                v = v + ref[here, r, :].astype(f32)
            if not last:
                acc[m][slot, r, :] = v.astype(acc[m].dtype)
            elif m == "E":
                ge[r, :] = v
            elif m[0] == "A":
                outs["A"][pl.ds(pl.multiple_of(r.start + sh.acut[int(m[1])], 16), r.size), :] = v
            else:
                outs[m[0]][r, :] = v
        rows(total, 8 if m == "E" else (16), add)
        if last:
            continue
        if i > 0:
            axis, buf, there = c, rc, slot - na * nb
        elif j > 0:
            axis, buf, there = b, rb, slot - na
        else:
            axis, buf, there = a, ra, slot - 1
        far = k if m in DIRECT and buf is ra else 1
        copy = place.remote(acc[m].at[slot], buf[m].at[there], send[m].at[slot], recv[m].at[slot], **{axis: -far})
        copy.start()
        sent.append((m, copy))

    row, col = place.moved()
    la = lax.broadcasted_iota(jnp.int32, (1, sh.alanes), 1) + (sh.start("A", col) - col * sh.awide)
    lb = lax.broadcasted_iota(jnp.int32, (1, sh.blanes), 1) + (sh.start("B", row) - row * sh.bwide)
    er = sh.erows
    sq = jnp.zeros((1, 128), f32)
    values = [ge[0:er, :]]
    for m, ref in outs.items():
        v = ref[...]
        if m == "A":
            v = jnp.where((la >= 0) & (la < sh.awide), v, 0.0)
        if m == "B":
            v = jnp.where((lb >= 0) & (lb < sh.bwide), v, 0.0)
        values.append(v)
    for v in values:
        w = rsum(v * v)
        for c0 in range(0, w.shape[1], 128):
            sq = sq + w[:, c0 : c0 + 128]
    ge[er : er + 8, :] = jnp.concatenate([jnp.broadcast_to(sq, (8, 128)), jnp.broadcast_to(aux[...], (8, 128))], axis=1)
    eall[row * sh.ncol + col] = ge[...]
    for m, copy in sent:
        copy.wait_send()
    for m in mats:
        place.remote(sib[m], sib[m], csend[m].at[0], crecv[m].at[0], core=1).wait_send()
    one = lambda v: {"E": v}
    run = Spread(place, sh, lambda m: ge, lambda m, r, c: eall.at[r * sh.ncol + c], one(send["E"]), one(erecv), one(csend["E"]), one(ecr))
    for step in sh.steps(["E"], False):
        run.step(*step)
    run.end()


def reduce_grads(sh, mats, aux, *grads):
    S = jax.ShapeDtypeStruct
    V = pltpu.VMEM
    anyspec = pl.BlockSpec(memory_space=pl.ANY)
    vm = pl.BlockSpec(memory_space=pltpu.VMEM)
    sem = pltpu.SemaphoreType.DMA
    whole = [m for m in sorted({m[0] for m in mats}) if m != "E"]
    outs = {"A": (sh.arows, sh.alanes)} | {m: sh.blocks[m] for m in "BCD"}
    scratch = []
    for count in (
        lambda na, nb, nc: na * nb * nc, lambda na, nb, nc: na * nb * nc, lambda na, nb, nc: (nc - 1) * nb * na,
        lambda na, nb, nc: (nb - 1) * na, lambda na, nb, nc: na - 1,
    ):
        scratch += [V((count(*sh.axes(m)[1]),) + sh.blocks[m], f32 if m == "E" else bf) for m in mats]
    scratch += [sem((sh.half if m == "E" else 1,)) for m in mats] + [sem((sh.half,))] * (3 * len(mats))
    scratch += [V((sh.erows + 8, 256), f32), sem((len(mats),)), sem((sh.half,)), sem((sh.half,))]
    return pl.pallas_call(
        functools.partial(reduce_kernel, sh, mats),
        in_specs=[anyspec] * (len(whole) + 1) + [vm], out_specs=[vm] * (len(whole) + 1),
        out_shape=[S(outs[m], f32) for m in whole] + [S((sh.nrow * sh.ncol, sh.erows + 8, 256), f32)],
        scratch_shapes=scratch,
        compiler_params=pltpu.CompilerParams(collective_id=1, has_side_effects=True, vmem_limit_bytes=60 << 20),
        name="reduce_grads",
    )(*grads, aux)


def prepare_kernel(sh, a, b, c, d, small, aout, bout, cout, dout, sv, awide, bwide):
    row, col = lax.axis_index("row"), lax.axis_index("col")

    def put(ref, out, wide, which, index):
        count, lanes = ref.shape[1], out.shape[1]
        if count == lanes:
            out[...] = ref[...].astype(bf)
            return
        wide[...] = jnp.zeros_like(wide)
        wide[:, 0:count] = ref[...]
        out[...] = pltpu.roll(wide[...], index * count - sh.start(which, index), 1).astype(bf)
    put(a, aout, awide, "A", col)
    put(b, bout, bwide, "B", row)
    cout[...] = c[...].astype(bf)
    dout[...] = d[...].astype(bf)
    for i in range(SMALL // 128):
        sv[:, i * 128 : (i + 1) * 128] = small[i : i + 1, :]


def prepare(sh, weights, small):
    a, b, c, d = weights
    S = jax.ShapeDtypeStruct
    alone = lambda m: (sh.brows, sh.blanes) if m == "B" else sh.blocks[m]
    return pl.pallas_call(
        functools.partial(prepare_kernel, sh),
        in_specs=vspec(5), out_specs=vspec(5),
        out_shape=[S((sh.arows, sh.alanes), bf)] + [S(alone(m), bf) for m in "BCD"] + [S((1, SMALL), f32)],
        scratch_shapes=[pltpu.VMEM((sh.arows, sh.alanes), f32), pltpu.VMEM((sh.brows, sh.blanes), f32)],
        name="prepare",
    )(a, b.T, c, d.T, small.reshape(SMALL // 128, 128))


GATHERED = ["A0", "A1", "A2", "B", "C", "D"]
REDUCED = ["A0", "A1", "A2", "B", "C", "D", "E"]


def tile_plan(sh, which):
    wide, count = (sh.awide, sh.ncol) if which == "A" else (sh.bwide, sh.nrow)
    alone, shared = [], []
    for c in range(count):
        first, end = wide * c // 128, -(-(wide * (c + 1)) // 128)
        base = sh.start(which, c) // 128
        lo = first + 1 if (wide * c) % 128 else first
        hi = end - 1 if (wide * (c + 1)) % 128 else end
        alone.append((c, lo, hi, base))
        if hi < end:
            shared.append((c, hi, base, sh.start(which, c + 1) // 128))
    return alone, shared


MOST = 6


def joiner(sh, which, src, dst, tmp, sem):
    alone, shared = tile_plan(sh, which)
    copies = []
    for c, lo, hi, at in alone:
        copies.append((src.at[c, :, pl.ds((lo - at) * 128, (hi - lo) * 128)], dst.at[:, pl.ds(lo * 128, (hi - lo) * 128)]))
    for u, (c, t, at, nxt) in enumerate(shared):
        copies.append((src.at[c, :, pl.ds((t - at) * 128, 128)], dst.at[:, pl.ds(t * 128, 128)]))
        copies.append((src.at[c + 1, :, pl.ds((t - nxt) * 128, 128)], tmp.at[u % MOST]))
    late = {len(alone) + 2 * u + 1 for u in range(MOST, len(shared))}
    make = lambda i: pltpu.make_async_copy(*copies[i], sem.at[i])
    made = [make(i) for i in range(len(copies)) if i not in late]
    for m in made:
        m.start()

    def end():
        for m in made:
            m.wait()
        for u, (c, t, at, nxt) in enumerate(shared):
            if u >= MOST:
                m = make(len(alone) + 2 * u + 1)
                m.start()
                m.wait()
            dst[:, t * 128 : (t + 1) * 128] += tmp[u % MOST]
    return end


def joiner_scratch(sh):
    V = pltpu.VMEM
    counts = [(len(a), len(s)) for a, s in (tile_plan(sh, "A"), tile_plan(sh, "B"))]
    return [V((D, 5 * D + FF + DD), bf), V((D, FF), bf)] + [V((min(max(s, 1), MOST), D, 128), bf) for _, s in counts] + [
        pltpu.SemaphoreType.DMA((a + 2 * s,)) for a, s in counts]


EG = 4 * ES
O_Q, O_P, O_F, O_E = D, 4 * D, 5 * D, 5 * D + FF


def enc_fwd_kernel(sh, pix, keep, pos3, sv, ain, bin_, cin, din,
                   y, kept, xh1, xh2, xhf, rs1, rs2, rsf, a1, a2, e16, o, qkv, p, hid, gp, awin, bwin, cout, dout,
                   x, bias, win, wout, atmp, btmp, asem, bsem, *sems):
    n = pix.shape[0]
    M = n * ES
    R = M // 2
    W = D
    run, own = start_gather(sh, GATHERED, dict(zip("ABCD", (ain, bin_, cin, din))), dict(zip("ABCD", (awin, bwin, cout, dout))), sems)
    ahead = sh.steps(["A0", "A1", "A2", "B"], False)
    for step in ahead[:4]:
        run.step(*step)

    kind = lax.rem(lax.broadcasted_iota(jnp.int32, (EG, 1), 0), ES)
    for i in range(0, n, 2):
        two = []
        for b in (i, i + 1):
            pick = (keep[b] == lax.broadcasted_iota(jnp.int32, (PATCHES, ES), 0)).astype(f32).astype(bf)
            two.append(dg(pick, pix[b], 0, 0))
            at = pos3[0:PATCHES, :], pos3[DS : DS + PATCHES, :], pos3[2 * DS : 2 * DS + PATCHES, :]
            x[b * ES : (b + 1) * ES, :] = dg(pick, at[0], 0, 0) + dg(pick, at[1], 0, 0) + dg(pick, at[2], 0, 0)
        kept[i * ES : (i + 2) * ES, :] = jnp.concatenate(two, axis=0).astype(bf)
    ki = lax.broadcasted_iota(jnp.int32, (EG, EG), 0)
    qi = lax.broadcasted_iota(jnp.int32, (EG, EG), 1)
    same = jnp.zeros((EG, EG), jnp.bool_)
    for j in range(4):
        same = same | ((ki >= j * ES) & (ki < j * ES + KEEP + 1) & (qi >= j * ES) & (qi < (j + 1) * ES))
    bias[...] = jnp.where(same, 0.0, -1e30).astype(f32)
    for step in ahead[4:]:
        run.step(*step)

    todo = sh.steps(["C", "D"], False)
    each = -(-len(todo) // 32)

    def tick(count=each):
        for _ in range(min(count, len(todo))):
            run.step(*todo.pop(0))
    tick(2)
    run.arrived("A")
    for m in ("A0", "A1", "A2"):
        own[m].wait()
    enda = joiner(sh, "A", awin, win, atmp, asem)
    run.arrived("B")
    own["B"].wait()
    endb = joiner(sh, "B", bwin, wout, btmp, bsem)
    enda()
    for lo in range(0, M, EG):
        sl = slice(lo, lo + EG)
        v = x[sl, :] + nn(kept[sl, :], win[:, 0:W]) + part(sv, 10)
        x[sl, :] = jnp.where(kind < KEEP, v, jnp.where(kind == KEEP, part(sv, 11), 0.0))
        tick()

    def ln1(r):
        xh, rs, a = norm_rows(x[r, :], part(sv, 0), part(sv, 1))
        xh1[r, :] = xh
        rs1[r, :] = rs
        a1[r, :] = a.astype(bf)
    rows(M, R, ln1)
    tick()
    qkv[:, 0:W] = (nn(a1[...], win[:, O_Q : O_Q + W]) + sv[:, OFF[2] : OFF[2] + W]).astype(bf)
    tick()
    qkv[:, W : 2 * W] = nn(a1[...], win[:, O_Q + W : O_Q + 2 * W]).astype(bf)
    tick()
    qkv[:, 2 * W :] = (nn(a1[...], win[:, O_Q + 2 * W : O_P]) + sv[:, OFF[2] + W : OFF[3]]).astype(bf)
    tick()
    for i in range(n // 4):
        for g in range(6):
            att_fwd(qkv, o, p, bias[...], slice(i * EG, (i + 1) * EG), W, g, i * 12 + g * 2, 64)
            if g % GROUPS == GROUPS - 1:
                tick(GROUPS * each)

    x[...] += nn(o[...], win[:, O_P : O_P + W]) + part(sv, 3)
    tick()

    def ln2(r):
        xh, rs, a = norm_rows(x[r, :], part(sv, 4), part(sv, 5))
        xh2[r, :] = xh
        rs2[r, :] = rs
        a2[r, :] = a.astype(bf)
    rows(M, R, ln2)
    tick()

    for c in range(0, FF, 512):
        h = nn(a2[...], win[:, O_F + c : O_F + c + 512])
        g, dg_ = gelu_pair(h + sv[:, OFF[6] + c : OFF[6] + c + 512])
        hid[:, c : c + 512] = g.astype(bf)
        gp[:, c : c + 512] = dg_.astype(bf)
        tick()
    endb()
    x[...] += nt(hid[...], wout[...]) + part(sv, 7)
    tick()

    def lnf(r):
        xh, rs, a = norm_rows(x[r, :], part(sv, 8), part(sv, 9))
        xhf[r, :] = xh
        rsf[r, :] = rs
        e16[r, :] = a.astype(bf)
    rows(M, R, lnf)
    tick()
    y[...] = nn(e16[...], win[:, O_E:]) + part(sv, 12)
    tick(len(todo))
    run.end()
    own["C"].wait()
    own["D"].wait()


GROUPS = 3


def vspec(k):
    return [pl.BlockSpec(memory_space=pltpu.VMEM)] * k


def encoder_fwd(sh, pix, keep, pos3, sv, *blocks):
    n = pix.shape[0]
    M = n * ES
    S = jax.ShapeDtypeStruct
    V = pltpu.VMEM
    sem = pltpu.SemaphoreType.DMA
    anyspec = pl.BlockSpec(memory_space=pl.ANY)
    outs = [S((M, DD), f32), S((M, D), bf), S((M, D), f32), S((M, D), f32), S((M, D), f32),
            S((M, 1), f32), S((M, 1), f32), S((M, 1), f32), S((M, D), bf), S((M, D), bf), S((M, D), bf), S((M, D), bf),
            S((M, 3 * D), bf), S((n // 4 * HEADS, EG, EG), bf), S((M, FF), bf), S((M, FF), bf)]
    weights = [S((sh.ncol, D, sh.alanes), bf), S((sh.nrow, D, sh.blanes), bf), S((DD, 4 * DD + DFF), bf), S((DD, DFF), bf)]
    out = pl.pallas_call(
        functools.partial(enc_fwd_kernel, sh),
        in_specs=vspec(4) + [anyspec] * 4, out_specs=vspec(len(outs)) + [anyspec] * 4, out_shape=outs + weights,
        scratch_shapes=[V((M, D), f32), V((EG, EG), f32)] + joiner_scratch(sh) + [sem((sh.half,))] * (4 * len(GATHERED)) + [sem((len(GATHERED),))],
        compiler_params=pltpu.CompilerParams(vmem_limit_bytes=60 << 20, collective_id=0, has_side_effects=True),
        name="encoder_fwd",
    )(pix, keep, pos3, sv, *blocks)
    return out[0], out[1 : len(outs)], out[len(outs) :]


def enc_bwd_kernel(sh, dy, dsm_in, dhw, sv, awin, bwin, kept, xh1_in, xh2, xhf_in, rs1, rs2, rsf, a1_in, a2, e16_in, o, qkv, p, hid, gp,
                   dwin, dwout, eout, dsm, etail, x, t, d16, dh16, stage, xb, ab, sem, lsem, win, wout, atmp, btmp, asem, bsem):
    def fetch(i, src, dst):
        copy = pltpu.make_async_copy(src, dst, lsem.at[i])
        copy.start()
        return copy

    at_e, at_xhf = fetch(0, e16_in, ab), fetch(1, xhf_in, xb)
    enda = joiner(sh, "A", awin, win, atmp, asem)
    endb = joiner(sh, "B", bwin, wout, btmp, bsem)
    M = dy.shape[0]
    R = M // 2
    W = D
    dsm[...] = dsm_in[...]
    head = fetch(4, dhw, eout.at[pl.ds(0, 3 * DD), :])

    def save(where, sums):
        for (i, lo), v in zip(where, sums):
            dsm[:, OFF[i] + lo : OFF[i] + lo + v.shape[1]] += v

    shots = []

    def put(out, base, value):
        width = value.shape[1]
        slot = len(shots) % 2
        if len(shots) >= 2:
            shots[-2].wait()
        stage[slot, :, 0:width] = value.astype(bf)
        copy = pltpu.make_async_copy(stage.at[slot, :, pl.ds(0, width)], out.at[:, pl.ds(base, width)], sem.at[slot])
        copy.start()
        shots.append(copy)

    def emb(r):
        v = dy[r, :]
        d16[r, 0:DD] = v.astype(bf)
        return [v]
    save([(12, 0)], rows_sum(M, R, [DD], emb))
    at_e.wait()
    put(dwin, O_E, dg(ab[...], d16[:, 0:DD], 0, 0))
    at_a = fetch(2, a1_in, ab)
    enda()
    endb()
    t[...] = nt(d16[:, 0:DD], win[:, O_E:])

    at_xhf.wait()

    def lnfb(r):
        da = t[r, :]
        xh = xb[r, :]
        dx = norm_back(da, xh, rsf[r, :], part(sv, 8))
        x[r, :] = dx
        d16[r, :] = dx.astype(bf)
        return da * xh, da, dx
    save([(8, 0), (9, 0), (7, 0)], rows_sum(M, R, [W] * 3, lnfb))
    at_xh1 = fetch(3, xh1_in, xb)
    for c in range(0, FF, W):
        put(dwout, c, dg(d16[...], hid[:, c : c + W], 0, 0))
        dh = nn(d16[...], wout[:, c : c + W]) * gp[:, c : c + W].astype(f32)
        dsm[:, OFF[6] + c : OFF[6] + c + W] += rsum(dh)
        dh16[:, c : c + W] = dh.astype(bf)
        put(dwin, O_F + c, dg(a2[...], dh16[:, c : c + W], 0, 0))
    t[...] = nt(dh16[...], win[:, O_F:O_E])
    dqkv = dh16

    def ln2b(r):
        da = t[r, :]
        xh = xh2[r, :]
        dx = x[r, :] + norm_back(da, xh, rs2[r, :], part(sv, 4))
        x[r, :] = dx
        d16[r, :] = dx.astype(bf)
        return da * xh, da, dx
    save([(4, 0), (5, 0), (3, 0)], rows_sum(M, R, [W] * 3, ln2b))
    put(dwin, O_P, dg(o[...], d16[...], 0, 0))
    d16[...] = nt(d16[...], win[:, O_P:O_F]).astype(bf)

    for i in range(M // EG):
        rsl = slice(i * EG, (i + 1) * EG)
        for g in range(6):
            att_bwd(qkv, d16, p, dqkv, rsl, W, g, i * 12 + g * 2, 64)

    at_a.wait()
    for c in range(0, 3 * D, W):
        put(dwin, O_Q + c, dg(ab[...], dqkv[:, c : c + W], 0, 0))
    save([(2, 0), (2, W)], rows_sum(M, R, [W, W], lambda r: [dqkv[r, 0:W].astype(f32), dqkv[r, 2 * W : 3 * W].astype(f32)]))
    t[...] = nt(dqkv[:, 0 : 3 * W], win[:, O_Q:O_P])
    at_xh1.wait()

    def ln1b(r):
        da = t[r, :]
        xh = xb[r, :]
        dx = x[r, :] + norm_back(da, xh, rs1[r, :], part(sv, 0))
        kind = lax.rem(lax.broadcasted_iota(jnp.int32, (r.size, 1), 0), ES)
        only = jnp.where(kind < KEEP, dx, 0.0)
        d16[r, :] = only.astype(bf)
        return da * xh, da, jnp.where(kind == KEEP, dx, 0.0), only
    save([(0, 0), (1, 0), (11, 0), (10, 0)], rows_sum(M, R, [W] * 4, ln1b))
    put(dwin, 0, dg(kept[...], d16[...], 0, 0))
    etail[...] = jnp.zeros_like(etail)
    for i in range(SMALL // 256):
        etail[i : i + 1, :] = dsm[:, i * 256 : (i + 1) * 256]
    tail = fetch(5, etail, eout.at[pl.ds(3 * DD, etail.shape[0]), :])
    for c in shots[-2:] + [head, tail]:
        c.wait()


def encoder_bwd(sh, dy, dsm, dhw, sv, awin, bwin, saved):
    M = dy.shape[0]
    count = sh.nrow * sh.ncol * sh.erows
    S = jax.ShapeDtypeStruct
    V = pltpu.VMEM
    anyspec = pl.BlockSpec(memory_space=pl.ANY)
    return pl.pallas_call(
        functools.partial(enc_bwd_kernel, sh),
        in_specs=[anyspec if i in (2, 4, 5, 7, 9, 13, 15) else spec for i, spec in enumerate(vspec(6 + len(saved)))],
        out_specs=[anyspec] * 3,
        out_shape=[S((D, 5 * D + FF + DD), bf), S((D, FF), bf), S((count, 256), f32)],
        scratch_shapes=[V((1, SMALL), f32), V((count - 3 * DD, 256), f32), V((M, D), f32), V((M, D), f32), V((M, D), bf), V((M, FF), bf), V((2, D, D), bf), V((M, D), f32), V((M, D), bf),
                        pltpu.SemaphoreType.DMA((2,)), pltpu.SemaphoreType.DMA((6,))] + joiner_scratch(sh),
        compiler_params=pltpu.CompilerParams(vmem_limit_bytes=63 << 20),
        name="encoder_bwd",
    )(dy, dsm, dhw, sv, awin, bwin, *saved)


def sincos_np(width):
    quarter = width // 4
    freq = (1.0 / np.float32(10000.0) ** (np.arange(quarter, dtype=np.float32) / np.float32(quarter))).astype(np.float32)
    pos = np.arange(GRID * GRID)
    cp = (pos % GRID).astype(np.float32)[:, None] * freq[None, :]
    rp = (pos // GRID).astype(np.float32)[:, None] * freq[None, :]
    return np.concatenate([np.sin(cp), np.cos(cp), np.sin(rp), np.cos(rp)], axis=1).astype(np.float32)


def tables():
    dec = np.zeros((DS, DD), np.float32)
    dec[:PATCHES] = sincos_np(DD)
    enc = np.zeros((DS, D), np.float32)
    enc[:PATCHES] = sincos_np(D)
    b = ml_dtypes.bfloat16
    hi = enc.astype(b)
    mid = (enc - hi.astype(np.float32)).astype(b)
    lo = (enc - hi.astype(np.float32) - mid.astype(np.float32)).astype(b)
    return dec, np.concatenate([hi, mid, lo], axis=0)


def adamw(weight, first, second, grad):
    first = 0.9 * first + (1.0 - 0.9) * grad
    second = 0.999 * second + (1.0 - 0.999) * grad * grad
    first_hat = first / (1.0 - 0.9**STEP)
    second_hat = second / (1.0 - 0.999**STEP)
    weight = weight - 0.08 * (first_hat / (jnp.sqrt(second_hat) + 1e-08) + 0.05 * weight)
    return (weight, first, second)


def update_kernel(sh, ga, gb, gc, gd, eall, *refs):
    weights, firsts, seconds = refs[0:6], refs[6:12], refs[12:18]
    new, mo, vo = refs[18:24], refs[24:30], refs[30:36]
    result, e2d = refs[36], refs[37]
    er = sh.erows
    row, col = lax.axis_index("row"), lax.axis_index("col")
    squares = jnp.zeros((1, 128), f32)
    losses = jnp.zeros((1, 128), f32)
    for i in range(sh.nrow * sh.ncol):
        e2d[i * er : (i + 1) * er, :] = eall[i, 0:er, :]
        squares = squares + eall[i, er : er + 1, 0:128]
        losses = losses + eall[i, er : er + 1, 128:256]
    norm = jnp.sqrt(jnp.sum(squares, axis=1, keepdims=True))
    factor = 0.0001 / jnp.maximum(norm, 0.0001)
    result[...] = jnp.where(lax.broadcasted_iota(jnp.int32, (1, 128), 1) == 0, losses, norm)

    def aligned(g, which, index, wide, lanes):
        if wide == lanes:
            return g
        return pltpu.roll(g, lax.rem(lanes - (index * wide - sh.start(which, index)), lanes), 1)[:, 0:wide]

    def apply(i, at, grad):
        out = adamw(weights[i][at], firsts[i][at], seconds[i][at], grad * factor)
        new[i][at], mo[i][at], vo[i][at] = out

    every = (slice(None), slice(None))
    apply(0, every, aligned(ga[...], "A", col, sh.awide, sh.alanes))
    apply(1, every, aligned(gb[...], "B", row, sh.bwide, sh.blanes))
    apply(2, every, gc[...])
    apply(3, every, gd[...])
    for c in range(0, PIX, 256):
        apply(4, (slice(None), slice(c, c + 256)), e2d[2 * c : 2 * c + DD, :])
    for i in range(SMALL // 256):
        for h in (0, 1):
            apply(5, (slice(2 * i + h, 2 * i + h + 1), slice(None)), e2d[3 * DD + i : 3 * DD + i + 1, h * 128 : (h + 1) * 128])


def update(sh, grads, weights, firsts, seconds):
    S = jax.ShapeDtypeStruct
    turn = lambda t: [v.T if i % 6 in (1, 3) else v for i, v in enumerate(t)]
    flat = lambda t: turn([v.reshape(SMALL // 128, 128) if v.ndim == 1 else v for v in t])
    state = flat(weights) + flat(firsts) + flat(seconds)
    outs = pl.pallas_call(
        functools.partial(update_kernel, sh),
        in_specs=vspec(5 + 18), out_specs=vspec(19),
        out_shape=[S(v.shape, f32) for v in state] + [S((1, 128), f32)],
        scratch_shapes=[pltpu.VMEM((sh.nrow * sh.ncol * sh.erows, 256), f32)],
        compiler_params=pltpu.CompilerParams(vmem_limit_bytes=60 << 20),
        name="update",
    )(*grads, *state)
    small = lambda v: v.reshape(SMALL) if v.shape == (SMALL // 128, 128) else v
    return tuple(turn([small(v) for v in outs[:18]])) + (outs[18][0, 0], outs[18][0, 1])


def local(pixels, keep_idx, restore, *state):
    weights, firsts, seconds = state[0:6], state[6:12], state[12:18]
    nrow, ncol = lax.axis_size("row"), lax.axis_size("col")
    sh = Shapes(nrow, ncol)
    n = pixels.shape[0]
    denom = 1.0 * n * nrow * ncol * (PATCHES - KEEP)

    dec_pos, enc_pos = tables()
    fill = lambda count, value: jnp.full((n, count), value, jnp.int32)
    keep = jnp.concatenate([keep_idx, fill(ES - KEEP, NOROW)], axis=1).reshape(n, 1, ES)
    code = jnp.concatenate([jnp.where(restore < KEEP, restore, 64), fill(1, KEEP), fill(DS - PATCHES - 1, NOROW)], axis=1)
    head = weights[4]
    *blocks, sv = prepare(sh, weights[0:4], weights[5])

    y, saved, (aw, bw, c, dt) = encoder_fwd(sh, pixels, keep, jnp.asarray(enc_pos), sv, *blocks)
    dy, dc, ddt, dhead, dsm, loss = decoder(
        y.reshape(n, ES, DD), code.reshape(n, 1, DS), pixels, jnp.asarray(dec_pos), sv, c, dt, head, 1.0 / denom)
    da, dbt, shared = encoder_bwd(sh, dy.reshape(n * ES, DD), dsm, dhead, sv, aw, bw, saved)
    sums = reduce_grads(sh, REDUCED, loss, da, dbt, dc, ddt, shared.reshape(nrow * ncol, sh.erows, 256))
    return update(sh, sums, weights, firsts, seconds)


def solution(mesh):
    both = P(("row", "col"))
    big = [P("row", "col")] * 4 + [P()] * 2
    return jax.shard_map(
        local,
        mesh=mesh,
        in_specs=(both, both, both, *big, *big, *big),
        out_specs=(*big, *big, *big, P(), P()),
        check_vma=False,
    )
```

```python
import functools
import math

import jax
import jax.numpy as jnp
import ml_dtypes
import numpy as np
from jax import lax
from jax.experimental import pallas as pl
from jax.experimental.pallas import tpu as pltpu
from jax.sharding import PartitionSpec as P

D = 768
HEADS = 12
FF = 3072
DD = 512
DHEADS = 16
DFF = 2048
PIX = 768
GRID = 14
PATCHES = 196
KEEP = 49
STEP = 10
SMALL = 21248
ES = 56
DS = 208
SEL = 80
NOROW = 255
f32 = jnp.float32
bf = jnp.bfloat16

LENS = [
    D, D, 2 * D, D, D, D, FF, D, D, D, D, D,
    DD, DD, DD, DD, 2 * DD, DD, DD, DD, DFF, DD, DD, DD, PIX,
]
OFF = [0]
for piece in LENS:
    OFF.append(OFF[-1] + piece)


def part(ref, i):
    return ref[:, OFF[i] : OFF[i + 1]]


def dg(a, b, ca, cb):
    return lax.dot_general(a, b, (((ca,), (cb,)), ((), ())), preferred_element_type=f32)


def nn(a, b):
    return dg(a, b, 1, 0)


def nt(a, b):
    return dg(a, b, 1, 1)


def rows(total, size, fn):
    @pl.loop(0, total // size)
    def _(i):
        fn(pl.ds(pl.multiple_of(i * size, size), size))


def rows_sum(total, size, widths, fn):
    def body(i, carry):
        parts = fn(pl.ds(pl.multiple_of(i * size, size), size))
        return tuple(c + jnp.sum(v.reshape(size // 8, 8, v.shape[1]), axis=0) for c, v in zip(carry, parts))
    carry = lax.fori_loop(0, total // size, body, tuple(jnp.zeros((8, w), f32) for w in widths))
    return [rsum(c) for c in carry]


def pieces(x):
    hi = x.astype(bf)
    rest = x - hi.astype(f32)
    mid = rest.astype(bf)
    low = (rest - mid.astype(f32)).astype(bf)
    return hi, mid, low


def gelu_pair(x):
    ax = jnp.abs(x)
    d = 1.0 + (0.3275911 * 0.7071067811865476) * ax
    r = pl.reciprocal(d, approx=True)
    t = r * (2.0 - d * r)
    e = jnp.exp(-0.5 * (x * x))
    poly = ((((0.5 * 1.061405429 * t - 0.5 * 1.453152027) * t + 0.5 * 1.421413741) * t
             - 0.5 * 0.284496736) * t + 0.5 * 0.254829592) * t
    q = poly * e
    phi = jnp.where(x >= 0.0, 1.0 - q, q)
    return x * phi, phi + x * (e * 0.3989422804014327)


def norm_rows(x, gain, shift):
    c = x - jnp.mean(x, axis=1, keepdims=True)
    rs = lax.rsqrt(jnp.mean(c * c, axis=1, keepdims=True) + 1e-06)
    xh = c * rs
    return xh, rs, xh * gain + shift


def norm_back(da, xh, rs, gain):
    g = da * gain
    m1 = jnp.mean(g, axis=1, keepdims=True)
    m2 = jnp.mean(g * xh, axis=1, keepdims=True)
    return rs * (g - m1 - xh * m2)


def rsum(x):
    return jnp.sum(x, axis=0, keepdims=True)


def lanes_of(x, h, hd):
    lane = lax.broadcasted_iota(jnp.int32, (1, 128), 1)
    return jnp.where((lane >= h * hd) & (lane < (h + 1) * hd), x, jnp.zeros_like(x))


def stack(x, hd):
    return jnp.concatenate([lanes_of(x, h, hd) for h in range(128 // hd)], axis=0)


def unstack(x, hd):
    n = x.shape[0] * hd // 128
    out = None
    for h in range(128 // hd):
        t = lanes_of(x[h * n : (h + 1) * n], h, hd)
        out = t if out is None else out + t
    return out


def att_fwd(qkv, o, p, bias, rsl, width, g, slot, hd):
    c0 = g * 128
    q = qkv[rsl, c0 : c0 + 128]
    k = qkv[rsl, c0 + width : c0 + width + 128]
    v = qkv[rsl, c0 + 2 * width : c0 + 2 * width + 128]
    n = q.shape[0]
    every = nt(stack(k, hd), q)
    probs = []
    for h in range(128 // hd):
        s = every[h * n : (h + 1) * n] * (hd ** -0.5 * 1.4426950408889634) + bias
        e = jnp.exp2(s - jnp.max(s, axis=0, keepdims=True))
        pr = (e * (1.0 / jnp.sum(e, axis=0, keepdims=True))).astype(bf)
        p[slot + h] = pr
        probs.append(pr)
    o[rsl, c0 : c0 + 128] = dg(jnp.concatenate(probs, axis=0), stack(v, hd), 0, 0).astype(bf)


def att_bwd(qkv, do, p, dqkv, rsl, width, g, slot, hd):
    c0 = g * 128
    c1, c2 = c0 + width, c0 + 2 * width
    q = qkv[rsl, c0 : c0 + 128]
    k = qkv[rsl, c1 : c1 + 128]
    v = qkv[rsl, c2 : c2 + 128]
    d = do[rsl, c0 : c0 + 128]
    n = q.shape[0]
    probs = jnp.concatenate([p[slot + h] for h in range(128 // hd)], axis=0)
    every = nt(stack(v, hd), d)
    back = []
    for h in range(128 // hd):
        pf = probs[h * n : (h + 1) * n].astype(f32)
        t = pf * every[h * n : (h + 1) * n].astype(bf).astype(f32)
        back.append(((t - pf * jnp.sum(t, axis=0, keepdims=True)) * (hd ** -0.5)).astype(bf))
    back = jnp.concatenate(back, axis=0)
    dqkv[rsl, c0 : c0 + 128] = dg(back, stack(k, hd), 0, 0).astype(bf)
    dqkv[rsl, c1 : c1 + 128] = unstack(nn(back, q), hd).astype(bf)
    dqkv[rsl, c2 : c2 + 128] = unstack(nn(probs, d), hd).astype(bf)


def dec_kernel(scale, nb, y, coder, pix, pos, sv, win, wout, hw,
               dy, win_out, wout_out, dhw, dsm, loss,
               dwin, dwout, x, t, xh1, xh2, xhf, rs1, rs2, rsf, tm, tr, a1, a2, u, o, qkv, p, hid, gp, dpr, d16, hide, lacc):
    M = nb * DS
    R = M
    W = DD

    @pl.when(pl.program_id(0) == 0)
    def _():
        dsm[...] = jnp.zeros_like(dsm)
        loss[...] = jnp.zeros_like(loss)
        lacc[...] = jnp.zeros_like(lacc)
        dpr[...] = jnp.zeros_like(dpr)
        for ref in (dwin, dwout, dhw):
            rows(ref.shape[0], 16, lambda r: ref.__setitem__((r, slice(None)), jnp.zeros((16, ref.shape[1]), f32)))

    def put(where, sums):
        for (i, lo), v in zip(where, sums):
            dsm[:, OFF[i] + lo : OFF[i] + lo + v.shape[1]] += v

    for b in range(nb):
        pick = (coder[b] == lax.broadcasted_iota(jnp.int32, (SEL, DS), 0)).astype(f32).astype(bf)
        tok = jnp.where(lax.broadcasted_iota(jnp.int32, (8, W), 0) == 0, part(sv, 13), 0.0)
        table = jnp.concatenate([y[b], jnp.zeros((8, W), f32), tok, jnp.zeros((8, W), f32)], axis=0)
        z = pos[...]
        for piece in pieces(table):
            z = z + dg(pick, piece, 0, 0)
        x[b * DS : (b + 1) * DS, :] = z
        mark = (lax.broadcasted_iota(jnp.int32, (SEL, 128), 0) == 64).astype(f32).astype(bf)
        hide[b * DS : (b + 1) * DS, :] = dg(pick, mark, 0, 0)[:, 0:1]

    def ln1(r):
        xh, rs, a = norm_rows(x[r, :], part(sv, 14), part(sv, 15))
        xh1[r, :] = xh
        rs1[r, :] = rs
        a1[r, :] = a.astype(bf)
    rows(M, R, ln1)

    qkv[:, 0:W] = (nn(a1[...], win[:, 0:W]) + sv[:, OFF[16] : OFF[16] + W]).astype(bf)
    qkv[:, W : 2 * W] = nn(a1[...], win[:, W : 2 * W]).astype(bf)
    qkv[:, 2 * W :] = (nn(a1[...], win[:, 2 * W : 3 * W]) + sv[:, OFF[16] + W : OFF[17]]).astype(bf)

    bias = jnp.where(lax.broadcasted_iota(jnp.int32, (DS, 1), 0) <= PATCHES, 0.0, -1e30).astype(f32)

    for i in range(nb):
        rsl = slice(i * DS, (i + 1) * DS)
        for g in range(4):
            att_fwd(qkv, o, p, bias, rsl, W, g, i * 16 + g * 4, 32)

    x[...] += nn(o[...], win[:, 3 * W : 4 * W]) + part(sv, 17)

    def ln2(r):
        xh, rs, a = norm_rows(x[r, :], part(sv, 18), part(sv, 19))
        xh2[r, :] = xh
        rs2[r, :] = rs
        a2[r, :] = a.astype(bf)
    rows(M, R, ln2)

    CW = 512
    for c in range(0, DFF, CW):
        h = nn(a2[...], win[:, 4 * W + c : 4 * W + c + CW])
        g, dg_ = gelu_pair(h + sv[:, OFF[20] + c : OFF[20] + c + CW])
        hid[:, c : c + CW] = g.astype(bf)
        gp[:, c : c + CW] = dg_.astype(bf)

    x[...] += nt(hid[...], wout[...]) + part(sv, 21)

    def lnf(r):
        xh, rs, a = norm_rows(x[r, :], part(sv, 22), part(sv, 23))
        xhf[r, :] = xh
        rsf[r, :] = rs
        u[r, :] = a.astype(bf)
    rows(M, R, lnf)

    for b in range(nb):
        v = pix[b].astype(f32)
        m = jnp.mean(v, axis=1, keepdims=True)
        c = v - m
        tm[b * DS : b * DS + PATCHES, :] = m
        tr[b * DS : b * DS + PATCHES, :] = lax.rsqrt(jnp.mean(c * c, axis=1, keepdims=True) + 1e-06)

    for c in range(0, PIX, 256):
        pr = nn(u[...], hw[:, c : c + 256].astype(bf)) + sv[:, OFF[24] + c : OFF[24] + c + 256]
        for b in range(nb):
            sl = slice(b * DS, b * DS + PATCHES)
            tgt = (pix[b, :, c : c + 256].astype(f32) - tm[sl, :]) * tr[sl, :]
            diff = jnp.where(hide[sl, :] > 0.5, pr[sl] - tgt, 0.0)
            lacc[...] += rsum(diff * diff)
            dp = diff * (2.0 * scale / PIX)
            dsm[:, OFF[24] + c : OFF[24] + c + 256] += rsum(dp)
            dpr[sl, c : c + 256] = dp.astype(bf)

    for c in range(0, PIX, 256):
        dhw[2 * c : 2 * c + DD, :] += dg(u[...], dpr[:, c : c + 256], 0, 0)
    t[...] = nt(dpr[...], hw[...].astype(bf))

    def lnfb(r):
        da = t[r, :]
        xh = xhf[r, :]
        dx = norm_back(da, xh, rsf[r, :], part(sv, 22))
        x[r, :] = dx
        d16[r, :] = dx.astype(bf)
        return da * xh, da, dx
    put([(22, 0), (23, 0), (21, 0)], rows_sum(M, R, [W] * 3, lnfb))

    dwout[...] += dg(d16[...], hid[...], 0, 0)
    for c in range(0, DFF, CW):
        dh = nn(d16[...], wout[:, c : c + CW]) * gp[:, c : c + CW].astype(f32)
        dsm[:, OFF[20] + c : OFF[20] + c + CW] += rsum(dh)
        gp[:, c : c + CW] = dh.astype(bf)
    dwin[:, 4 * W :] += dg(a2[...], gp[...], 0, 0)
    t[...] = nt(gp[...], win[:, 4 * W :])

    def ln2b(r):
        da = t[r, :]
        xh = xh2[r, :]
        dx = x[r, :] + norm_back(da, xh, rs2[r, :], part(sv, 18))
        x[r, :] = dx
        d16[r, :] = dx.astype(bf)
        return da * xh, da, dx
    put([(18, 0), (19, 0), (17, 0)], rows_sum(M, R, [W] * 3, ln2b))

    dwin[:, 3 * W : 4 * W] += dg(o[...], d16[...], 0, 0)
    o[...] = nt(d16[...], win[:, 3 * W : 4 * W]).astype(bf)
    dqkv = gp

    for i in range(nb):
        rsl = slice(i * DS, (i + 1) * DS)
        for g in range(4):
            att_bwd(qkv, o, p, dqkv, rsl, W, g, i * 16 + g * 4, 32)

    dwin[:, 0 : 3 * W] += dg(a1[...], dqkv[:, 0 : 3 * W], 0, 0)
    put([(16, 0), (16, W)], rows_sum(M, R, [W, W], lambda r: [dqkv[r, 0:W].astype(f32), dqkv[r, 2 * W : 3 * W].astype(f32)]))
    t[...] = nt(dqkv[:, 0 : 3 * W], win[:, 0 : 3 * W])

    def ln1b(r):
        da = t[r, :]
        xh = xh1[r, :]
        x[r, :] = x[r, :] + norm_back(da, xh, rs1[r, :], part(sv, 14))
        return da * xh, da
    put([(14, 0), (15, 0)], rows_sum(M, R, [W] * 2, ln1b))

    for b in range(nb):
        pick = (coder[b] == lax.broadcasted_iota(jnp.int32, (SEL, DS), 0)).astype(f32).astype(bf)
        out = None
        for piece in pieces(x[b * DS : (b + 1) * DS, :]):
            v = nn(pick, piece)
            out = v if out is None else out + v
        dy[b] = out[0:ES]
        dsm[:, OFF[13] : OFF[14]] += out[64:65]

    @pl.when(pl.program_id(0) == pl.num_programs(0) - 1)
    def _():
        loss[...] = jnp.broadcast_to(jnp.sum(lacc[...], axis=1, keepdims=True) * (scale / PIX), (1, 128))
        for src, dst in ((dwin, win_out), (dwout, wout_out)):
            rows(DD, 16, lambda r: dst.__setitem__((r, slice(None)), src[r, :].astype(bf)))


def decoder(y, coder, pix, pos, sv, win, wout, hw, scale, nb=2):
    n = y.shape[0]
    M = nb * DS
    whole = lambda a: pl.BlockSpec(a.shape, lambda i: (0,) * a.ndim, pipeline_mode=pl.Buffered(1))
    fixed = lambda s: pl.BlockSpec(s, lambda i: (0,) * len(s), pipeline_mode=pl.Buffered(1))
    blk = lambda s: pl.BlockSpec((nb,) + s, lambda i: (i, 0, 0))
    V = pltpu.VMEM
    return pl.pallas_call(
        functools.partial(dec_kernel, scale, nb),
        grid=(n // nb,),
        in_specs=[blk((ES, DD)), blk((1, DS)), blk((PATCHES, PIX)), whole(pos), whole(sv), whole(win), whole(wout), whole(hw)],
        out_specs=[blk((ES, DD)), fixed(win.shape), fixed(wout.shape), fixed((3 * DD, 256)), fixed((1, SMALL)), fixed((1, 128))],
        out_shape=[
            jax.ShapeDtypeStruct((n, ES, DD), f32), jax.ShapeDtypeStruct(win.shape, bf),
            jax.ShapeDtypeStruct(wout.shape, bf), jax.ShapeDtypeStruct((3 * DD, 256), f32),
            jax.ShapeDtypeStruct((1, SMALL), f32), jax.ShapeDtypeStruct((1, 128), f32)],
        scratch_shapes=[
            V(win.shape, f32), V(wout.shape, f32),
            V((M, DD), f32), V((M, DD), f32), V((M, DD), f32), V((M, DD), f32), V((M, DD), f32),
            V((M, 1), f32), V((M, 1), f32), V((M, 1), f32), V((M, 1), f32), V((M, 1), f32),
            V((M, DD), bf), V((M, DD), bf), V((M, DD), bf), V((M, DD), bf), V((M, 3 * DD), bf),
            V((nb * DHEADS, DS, DS), bf), V((M, DFF), bf), V((M, DFF), bf), V((M, PIX), bf), V((M, DD), bf), V((M, 1), f32),
            V((1, 256), f32)],
        compiler_params=pltpu.CompilerParams(vmem_limit_bytes=60 << 20),
        name="decoder",
    )(y, coder, pix, pos, sv, win, wout, hw)


class Place:
    def __init__(self, nrow, ncol):
        side = math.isqrt(nrow)
        self.nrow, self.ncol = nrow, ncol
        self.n = {"x": side, "y": nrow // side, "z": ncol // 2}
        row, col = lax.axis_index("row"), lax.axis_index("col")
        self.at = {"x": row % side, "y": row // side, "z": col // 2, "core": col % 2}

    def moved(self, **by):
        at = {}
        for k, v in self.at.items():
            step = by.get(k, 0)
            size = 2 if k == "core" else self.n[k]
            at[k] = v if step % size == 0 else lax.rem(v + (step % size), size)
        return at["y"] * self.n["x"] + at["x"], at["z"] * 2 + at["core"]

    def greet(self):
        sem = pltpu.get_barrier_semaphore()
        count = 0
        for axis in ("x", "y", "z", "core"):
            size = 2 if axis == "core" else self.n[axis]
            for step in range(1, size):
                pl.semaphore_signal(sem, inc=1, device_id=self.moved(**{axis: step}), device_id_type=pl.DeviceIdType.MESH)
                count += 1
        pl.semaphore_wait(sem, count)

    def remote(self, src, dst, ssem, rsem, **by):
        return pltpu.make_async_remote_copy(src, dst, ssem, rsem, device_id=self.moved(**by), device_id_type=pl.DeviceIdType.MESH)


ORDER = {
    "A0": ("z", "x", "y"), "A1": ("z", "y", "x"), "A2": ("x", "y", "z"), "B": ("z", "y", "x"),
    "C": ("z", "x", "y"), "D": ("y", "x", "z"), "E": ("z", "y", "x"),
}
DIRECT = ("E",)


class Shapes:
    def __init__(self, nrow, ncol):
        self.nrow, self.ncol = nrow, ncol
        self.half = nrow * ncol // 2
        side = math.isqrt(nrow)
        self.n = {"x": side, "y": nrow // side, "z": ncol // 2}
        self.awide, self.bwide = (5 * D + FF + DD) // ncol, FF // nrow
        self.alanes, self.blanes = self.window(self.awide, ncol), self.window(self.bwide, nrow)
        self.arows, self.brows = D // nrow, D // ncol
        cut = [self.arows * t // 12 // 16 * 16 for t in (5, 4)]
        self.acut = (0, cut[0], cut[0] + cut[1], self.arows)
        self.crows, self.clanes = DD // nrow, (4 * DD + DFF) // ncol
        self.drows, self.dlanes = DD // ncol, DFF // nrow
        self.erows = -(-(DD * PIX + SMALL) // (nrow * ncol * 256 * 8)) * 8
        self.blocks = {
            "A0": (cut[0], self.alanes), "A1": (cut[1], self.alanes), "A2": (self.arows - self.acut[2], self.alanes), "B": (self.brows, self.blanes),
            "C": (self.crows, self.clanes), "D": (self.drows, self.dlanes), "E": (self.erows, 256)}

    @staticmethod
    def window(wide, count):
        return max(-(-((wide * c) % 128 + wide) // 128) * 128 for c in range(count))

    def start(self, which, index):
        wide, lanes, total = (self.awide, self.alanes, 5 * D + FF + DD) if which == "A" else (self.bwide, self.blanes, FF)
        first = (wide * index) // 128
        last = (total - lanes) // 128
        if isinstance(index, int):
            return min(first, last) * 128
        return jnp.minimum(first, last) * 128

    def axes(self, m):
        return ORDER[m], tuple(self.n[a] for a in ORDER[m])

    def steps(self, mats, back, keys=False):
        out = []
        for pos, m in enumerate(mats):
            _, (na, nb, nc) = self.axes(m)
            for i in range(nc):
                for j in range(nb):
                    for k in range(na):
                        key = (na - 1 - k) + (nb - 1 - j) + (nc - 1 - i) if back else i + j + (min(k, 1) if m in DIRECT else k)
                        out.append((key, pos, m, i, j, k))
        return [t if keys else t[2:] for t in sorted(out)]

    def onward(self, m, i, j, k):
        (a, b, c), (na, nb, nc) = self.axes(m)
        slot = (i * nb + j) * na + k
        out = []
        if m in DIRECT and i == j == k == 0:
            out += [(a, t, t) for t in range(1, na)]
        if m not in DIRECT and i == j == 0 and k < na - 1:
            out.append((a, 1, slot + 1))
        if i == 0 and j < nb - 1:
            out.append((b, 1, slot + na))
        if i < nc - 1:
            out.append((c, 1, slot + na * nb))
        return slot, out


class Spread:
    def __init__(self, place, sh, first, spot, send, recv, csend, crecv):
        self.place, self.sh, self.first, self.spot = place, sh, first, spot
        self.send, self.recv, self.csend, self.crecv = send, recv, csend, crecv
        self.sent, self.late = [], []

    def step(self, m, i, j, k):
        place = self.place
        (a, b, c), _ = self.sh.axes(m)
        slot, onward = self.sh.onward(m, i, j, k)
        by = {c: -i, b: -j, a: -k}
        dst = self.spot(m, *place.moved(**by))
        own = i == j == k == 0
        src = self.first(m) if own else dst
        csend, crecv = self.csend[m].at[slot], self.crecv[m].at[slot]
        if not own:
            place.remote(dst, dst, self.send[m].at[slot], self.recv[m].at[slot], core=1).wait_recv()
        for axis, far, there in onward:
            copy = place.remote(src, dst, self.send[m].at[there], self.recv[m].at[there], **{axis: far})
            copy.start()
            self.sent.append(copy)
        copy = place.remote(src, dst, csend, crecv, core=1)
        copy.start()
        self.sent.append(copy)
        other = self.spot(m, *place.moved(core=1, **by))
        self.late.append((m, place.remote(other, other, csend, crecv, core=1)))

    def arrived(self, which):
        for m, copy in self.late:
            if m[0] in which:
                copy.wait_recv()
        self.late = [t for t in self.late if t[0][0] not in which]

    def end(self):
        self.arrived("ABCDE")
        for copy in self.sent:
            copy.wait_send()


def block_at(sh, m, ref, row, col, gathered):
    mul = pl.multiple_of
    if m[0] == "A":
        skip = sh.acut[int(m[1])]
        r = pl.ds(mul(row * sh.arows + skip, 16), sh.blocks[m][0])
        return ref.at[col, r, :] if gathered else ref.at[r, pl.ds(mul(sh.start("A", col), 128), sh.alanes)]
    if m == "B":
        r = pl.ds(mul(col * sh.brows, 16), sh.brows)
        return ref.at[row, r, :] if gathered else ref.at[r, pl.ds(mul(sh.start("B", row), 128), sh.blanes)]
    if m == "C":
        return ref.at[pl.ds(mul(row * sh.crows, 16), sh.crows), pl.ds(mul(col * sh.clanes, 128), sh.clanes)]
    if m == "D":
        return ref.at[pl.ds(mul(col * sh.drows, 16), sh.drows), pl.ds(mul(row * sh.dlanes, 128), sh.dlanes)]
    return ref.at[row * sh.ncol + col]


def start_gather(sh, mats, ins, outs, sems):
    place = Place(sh.nrow, sh.ncol)
    send, recv, csend, crecv = (dict(zip(mats, sems[t * len(mats) :])) for t in range(4))
    lsem = sems[4 * len(mats)]

    def spot(m, row, col):
        return block_at(sh, m, outs[m[0]], row, col, True)

    def first(m):
        if m[0] == "A":
            return ins["A"].at[pl.ds(sh.acut[int(m[1])], sh.blocks[m][0]), :]
        return ins[m]

    place.greet()
    own = [pltpu.make_async_copy(first(m), spot(m, *place.moved()), lsem.at[i]) for i, m in enumerate(mats)]
    for copy in own:
        copy.start()
    return Spread(place, sh, first, spot, send, recv, csend, crecv), dict(zip(mats, own))


def reduce_kernel(sh, mats, *refs):
    refs = list(refs)

    def take(names):
        return {m: refs.pop(0) for m in names}
    whole = sorted({m[0] for m in mats})
    ins = take(whole)
    aux = refs.pop(0)
    outs = take([m for m in whole if m != "E"])
    eall = refs.pop(0)
    acc, sib, rc, rb, ra = (take(mats) for _ in range(5))
    csend, crecv, send, recv = (take(mats) for _ in range(4))
    ge, lsem, erecv, ecr = refs
    place = Place(sh.nrow, sh.ncol)

    def spot(m, row, col):
        return block_at(sh, m, ins[m[0]], row, col, False)

    place.greet()
    steps = sh.steps(mats, True)
    sent = []
    for m, i, j, k in steps:
        (a, b, c), _ = sh.axes(m)
        slot, _ = sh.onward(m, i, j, k)
        by = {c: -i, b: -j, a: -k}
        copy = place.remote(spot(m, *place.moved(core=1, **by)), sib[m].at[slot], csend[m].at[0], crecv[m].at[slot], core=1)
        copy.start()
        pltpu.make_async_copy(spot(m, *place.moved(**by)), acc[m].at[slot], lsem.at[mats.index(m)]).start()
    for m in mats:
        pltpu.make_async_copy(acc[m], acc[m], lsem.at[mats.index(m)]).wait()
    for m, i, j, k in steps:
        (a, b, c), (na, nb, nc) = sh.axes(m)
        slot, onward = sh.onward(m, i, j, k)
        place.remote(sib[m].at[slot], sib[m].at[slot], csend[m].at[0], crecv[m].at[slot], core=1).wait_recv()
        terms = [(sib[m], slot)]
        for axis, far, from_slot in onward:
            buf = {a: ra, b: rb, c: rc}[axis][m]
            here = from_slot - {a: 1, b: na, c: na * nb}[axis]
            place.remote(buf.at[here], buf.at[here], send[m].at[slot], recv[m].at[from_slot], core=1).wait_recv()
            terms.append((buf, here))
        last = i == j == k == 0
        total, lanes = sh.blocks[m]

        def add(r, m=m, terms=terms, last=last, slot=slot):
            v = acc[m][slot, r, :].astype(f32)
            for ref, here in terms:
                v = v + ref[here, r, :].astype(f32)
            if not last:
                acc[m][slot, r, :] = v.astype(acc[m].dtype)
            elif m == "E":
                ge[r, :] = v
            elif m[0] == "A":
                outs["A"][pl.ds(pl.multiple_of(r.start + sh.acut[int(m[1])], 16), r.size), :] = v
            else:
                outs[m[0]][r, :] = v
        rows(total, 8 if m == "E" else (16), add)
        if last:
            continue
        if i > 0:
            axis, buf, there = c, rc, slot - na * nb
        elif j > 0:
            axis, buf, there = b, rb, slot - na
        else:
            axis, buf, there = a, ra, slot - 1
        far = k if m in DIRECT and buf is ra else 1
        copy = place.remote(acc[m].at[slot], buf[m].at[there], send[m].at[slot], recv[m].at[slot], **{axis: -far})
        copy.start()
        sent.append((m, copy))

    row, col = place.moved()
    la = lax.broadcasted_iota(jnp.int32, (1, sh.alanes), 1) + (sh.start("A", col) - col * sh.awide)
    lb = lax.broadcasted_iota(jnp.int32, (1, sh.blanes), 1) + (sh.start("B", row) - row * sh.bwide)
    er = sh.erows
    sq = jnp.zeros((1, 128), f32)
    values = [ge[0:er, :]]
    for m, ref in outs.items():
        v = ref[...]
        if m == "A":
            v = jnp.where((la >= 0) & (la < sh.awide), v, 0.0)
        if m == "B":
            v = jnp.where((lb >= 0) & (lb < sh.bwide), v, 0.0)
        values.append(v)
    for v in values:
        w = rsum(v * v)
        for c0 in range(0, w.shape[1], 128):
            sq = sq + w[:, c0 : c0 + 128]
    ge[er : er + 8, :] = jnp.concatenate([jnp.broadcast_to(sq, (8, 128)), jnp.broadcast_to(aux[...], (8, 128))], axis=1)
    eall[row * sh.ncol + col] = ge[...]
    for m, copy in sent:
        copy.wait_send()
    for m in mats:
        place.remote(sib[m], sib[m], csend[m].at[0], crecv[m].at[0], core=1).wait_send()
    one = lambda v: {"E": v}
    run = Spread(place, sh, lambda m: ge, lambda m, r, c: eall.at[r * sh.ncol + c], one(send["E"]), one(erecv), one(csend["E"]), one(ecr))
    for step in sh.steps(["E"], False):
        run.step(*step)
    run.end()


def reduce_grads(sh, mats, aux, *grads):
    S = jax.ShapeDtypeStruct
    V = pltpu.VMEM
    anyspec = pl.BlockSpec(memory_space=pl.ANY)
    vm = pl.BlockSpec(memory_space=pltpu.VMEM)
    sem = pltpu.SemaphoreType.DMA
    whole = [m for m in sorted({m[0] for m in mats}) if m != "E"]
    outs = {"A": (sh.arows, sh.alanes)} | {m: sh.blocks[m] for m in "BCD"}
    scratch = []
    for count in (
        lambda na, nb, nc: na * nb * nc, lambda na, nb, nc: na * nb * nc, lambda na, nb, nc: (nc - 1) * nb * na,
        lambda na, nb, nc: (nb - 1) * na, lambda na, nb, nc: na - 1,
    ):
        scratch += [V((count(*sh.axes(m)[1]),) + sh.blocks[m], f32 if m == "E" else bf) for m in mats]
    scratch += [sem((sh.half if m == "E" else 1,)) for m in mats] + [sem((sh.half,))] * (3 * len(mats))
    scratch += [V((sh.erows + 8, 256), f32), sem((len(mats),)), sem((sh.half,)), sem((sh.half,))]
    return pl.pallas_call(
        functools.partial(reduce_kernel, sh, mats),
        in_specs=[anyspec] * (len(whole) + 1) + [vm], out_specs=[vm] * (len(whole) + 1),
        out_shape=[S(outs[m], f32) for m in whole] + [S((sh.nrow * sh.ncol, sh.erows + 8, 256), f32)],
        scratch_shapes=scratch,
        compiler_params=pltpu.CompilerParams(collective_id=1, has_side_effects=True, vmem_limit_bytes=44 << 20),
        name="reduce_grads",
    )(*grads, aux)


def prepare_kernel(sh, a, b, c, d, small, aout, bout, cout, dout, sv, awide, bwide):
    row, col = lax.axis_index("row"), lax.axis_index("col")

    def put(ref, out, wide, which, index):
        count, lanes = ref.shape[1], out.shape[1]
        if count == lanes:
            out[...] = ref[...].astype(bf)
            return
        wide[...] = jnp.zeros_like(wide)
        wide[:, 0:count] = ref[...]
        out[...] = pltpu.roll(wide[...], index * count - sh.start(which, index), 1).astype(bf)
    put(a, aout, awide, "A", col)
    put(b, bout, bwide, "B", row)
    cout[...] = c[...].astype(bf)
    dout[...] = d[...].astype(bf)
    for i in range(SMALL // 128):
        sv[:, i * 128 : (i + 1) * 128] = small[i : i + 1, :]


def prepare(sh, weights, small):
    a, b, c, d = weights
    S = jax.ShapeDtypeStruct
    alone = lambda m: (sh.brows, sh.blanes) if m == "B" else sh.blocks[m]
    return pl.pallas_call(
        functools.partial(prepare_kernel, sh),
        in_specs=vspec(5), out_specs=vspec(5),
        out_shape=[S((sh.arows, sh.alanes), bf)] + [S(alone(m), bf) for m in "BCD"] + [S((1, SMALL), f32)],
        scratch_shapes=[pltpu.VMEM((sh.arows, sh.alanes), f32), pltpu.VMEM((sh.brows, sh.blanes), f32)],
        name="prepare",
    )(a, b.T, c, d.T, small.reshape(SMALL // 128, 128))


GATHERED = ["A0", "A1", "A2", "B", "C", "D"]
REDUCED = ["A0", "A1", "A2", "B", "C", "D", "E"]


def tile_plan(sh, which):
    wide, count = (sh.awide, sh.ncol) if which == "A" else (sh.bwide, sh.nrow)
    alone, shared = [], []
    for c in range(count):
        first, end = wide * c // 128, -(-(wide * (c + 1)) // 128)
        base = sh.start(which, c) // 128
        lo = first + 1 if (wide * c) % 128 else first
        hi = end - 1 if (wide * (c + 1)) % 128 else end
        alone.append((c, lo, hi, base))
        if hi < end:
            shared.append((c, hi, base, sh.start(which, c + 1) // 128))
    return alone, shared


MOST = 6


def joiner(sh, which, src, dst, tmp, sem):
    alone, shared = tile_plan(sh, which)
    copies = []
    for c, lo, hi, at in alone:
        copies.append((src.at[c, :, pl.ds((lo - at) * 128, (hi - lo) * 128)], dst.at[:, pl.ds(lo * 128, (hi - lo) * 128)]))
    for u, (c, t, at, nxt) in enumerate(shared):
        copies.append((src.at[c, :, pl.ds((t - at) * 128, 128)], dst.at[:, pl.ds(t * 128, 128)]))
        copies.append((src.at[c + 1, :, pl.ds((t - nxt) * 128, 128)], tmp.at[u % MOST]))
    late = {len(alone) + 2 * u + 1 for u in range(MOST, len(shared))}
    make = lambda i: pltpu.make_async_copy(*copies[i], sem.at[i])
    made = [make(i) for i in range(len(copies)) if i not in late]
    for m in made:
        m.start()

    def end():
        for m in made:
            m.wait()
        for u, (c, t, at, nxt) in enumerate(shared):
            if u >= MOST:
                m = make(len(alone) + 2 * u + 1)
                m.start()
                m.wait()
            dst[:, t * 128 : (t + 1) * 128] += tmp[u % MOST]
    return end


def joiner_scratch(sh):
    V = pltpu.VMEM
    counts = [(len(a), len(s)) for a, s in (tile_plan(sh, "A"), tile_plan(sh, "B"))]
    return [V((D, 5 * D + FF + DD), bf), V((D, FF), bf)] + [V((min(max(s, 1), MOST), D, 128), bf) for _, s in counts] + [
        pltpu.SemaphoreType.DMA((a + 2 * s,)) for a, s in counts]


EG = 4 * ES
O_Q, O_P, O_F, O_E = D, 4 * D, 5 * D, 5 * D + FF


def enc_fwd_kernel(sh, pix, keep, pos3, sv, ain, bin_, cin, din,
                   y, kept, xh1, xh2, xhf, rs1, rs2, rsf, a1, a2, e16, o, qkv, p, hid, gp, awin, bwin, cout, dout,
                   x, bias, win, wout, atmp, btmp, asem, bsem, *sems):
    n = pix.shape[0]
    M = n * ES
    R = M // 2
    W = D
    run, own = start_gather(sh, GATHERED, dict(zip("ABCD", (ain, bin_, cin, din))), dict(zip("ABCD", (awin, bwin, cout, dout))), sems)
    ahead = sh.steps(["A0", "A1", "A2", "B"], False)
    for step in ahead[:4]:
        run.step(*step)

    kind = lax.rem(lax.broadcasted_iota(jnp.int32, (EG, 1), 0), ES)
    for i in range(0, n, 2):
        two = []
        for b in (i, i + 1):
            pick = (keep[b] == lax.broadcasted_iota(jnp.int32, (PATCHES, ES), 0)).astype(f32).astype(bf)
            two.append(dg(pick, pix[b], 0, 0))
            at = pos3[0:PATCHES, :], pos3[DS : DS + PATCHES, :], pos3[2 * DS : 2 * DS + PATCHES, :]
            x[b * ES : (b + 1) * ES, :] = dg(pick, at[0], 0, 0) + dg(pick, at[1], 0, 0) + dg(pick, at[2], 0, 0)
        kept[i * ES : (i + 2) * ES, :] = jnp.concatenate(two, axis=0).astype(bf)
    ki = lax.broadcasted_iota(jnp.int32, (EG, EG), 0)
    qi = lax.broadcasted_iota(jnp.int32, (EG, EG), 1)
    same = jnp.zeros((EG, EG), jnp.bool_)
    for j in range(4):
        same = same | ((ki >= j * ES) & (ki < j * ES + KEEP + 1) & (qi >= j * ES) & (qi < (j + 1) * ES))
    bias[...] = jnp.where(same, 0.0, -1e30).astype(f32)
    for step in ahead[4:]:
        run.step(*step)

    todo = sh.steps(["C", "D"], False)
    each = -(-len(todo) // 32)

    def tick(count=each):
        for _ in range(min(count, len(todo))):
            run.step(*todo.pop(0))
    tick(2)
    run.arrived("A")
    for m in ("A0", "A1", "A2"):
        own[m].wait()
    enda = joiner(sh, "A", awin, win, atmp, asem)
    run.arrived("B")
    own["B"].wait()
    endb = joiner(sh, "B", bwin, wout, btmp, bsem)
    enda()
    for lo in range(0, M, EG):
        sl = slice(lo, lo + EG)
        v = x[sl, :] + nn(kept[sl, :], win[:, 0:W]) + part(sv, 10)
        x[sl, :] = jnp.where(kind < KEEP, v, jnp.where(kind == KEEP, part(sv, 11), 0.0))
        tick()

    def ln1(r):
        xh, rs, a = norm_rows(x[r, :], part(sv, 0), part(sv, 1))
        xh1[r, :] = xh
        rs1[r, :] = rs
        a1[r, :] = a.astype(bf)
    rows(M, R, ln1)
    tick()
    qkv[:, 0:W] = (nn(a1[...], win[:, O_Q : O_Q + W]) + sv[:, OFF[2] : OFF[2] + W]).astype(bf)
    tick()
    qkv[:, W : 2 * W] = nn(a1[...], win[:, O_Q + W : O_Q + 2 * W]).astype(bf)
    tick()
    qkv[:, 2 * W :] = (nn(a1[...], win[:, O_Q + 2 * W : O_P]) + sv[:, OFF[2] + W : OFF[3]]).astype(bf)
    tick()
    for i in range(n // 4):
        for g in range(6):
            att_fwd(qkv, o, p, bias[...], slice(i * EG, (i + 1) * EG), W, g, i * 12 + g * 2, 64)
            if g % GROUPS == GROUPS - 1:
                tick(GROUPS * each)

    x[...] += nn(o[...], win[:, O_P : O_P + W]) + part(sv, 3)
    tick()

    def ln2(r):
        xh, rs, a = norm_rows(x[r, :], part(sv, 4), part(sv, 5))
        xh2[r, :] = xh
        rs2[r, :] = rs
        a2[r, :] = a.astype(bf)
    rows(M, R, ln2)
    tick()

    for c in range(0, FF, 512):
        h = nn(a2[...], win[:, O_F + c : O_F + c + 512])
        g, dg_ = gelu_pair(h + sv[:, OFF[6] + c : OFF[6] + c + 512])
        hid[:, c : c + 512] = g.astype(bf)
        gp[:, c : c + 512] = dg_.astype(bf)
        tick()
    endb()
    x[...] += nt(hid[...], wout[...]) + part(sv, 7)
    tick()

    def lnf(r):
        xh, rs, a = norm_rows(x[r, :], part(sv, 8), part(sv, 9))
        xhf[r, :] = xh
        rsf[r, :] = rs
        e16[r, :] = a.astype(bf)
    rows(M, R, lnf)
    tick()
    y[...] = nn(e16[...], win[:, O_E:]) + part(sv, 12)
    tick(len(todo))
    run.end()
    own["C"].wait()
    own["D"].wait()


GROUPS = 3


def vspec(k):
    return [pl.BlockSpec(memory_space=pltpu.VMEM)] * k


def encoder_fwd(sh, pix, keep, pos3, sv, *blocks):
    n = pix.shape[0]
    M = n * ES
    S = jax.ShapeDtypeStruct
    V = pltpu.VMEM
    sem = pltpu.SemaphoreType.DMA
    anyspec = pl.BlockSpec(memory_space=pl.ANY)
    outs = [S((M, DD), f32), S((M, D), bf), S((M, D), f32), S((M, D), f32), S((M, D), f32),
            S((M, 1), f32), S((M, 1), f32), S((M, 1), f32), S((M, D), bf), S((M, D), bf), S((M, D), bf), S((M, D), bf),
            S((M, 3 * D), bf), S((n // 4 * HEADS, EG, EG), bf), S((M, FF), bf), S((M, FF), bf)]
    weights = [S((sh.ncol, D, sh.alanes), bf), S((sh.nrow, D, sh.blanes), bf), S((DD, 4 * DD + DFF), bf), S((DD, DFF), bf)]
    out = pl.pallas_call(
        functools.partial(enc_fwd_kernel, sh),
        in_specs=vspec(4) + [anyspec] * 4, out_specs=vspec(len(outs)) + [anyspec] * 4, out_shape=outs + weights,
        scratch_shapes=[V((M, D), f32), V((EG, EG), f32)] + joiner_scratch(sh) + [sem((sh.half,))] * (4 * len(GATHERED)) + [sem((len(GATHERED),))],
        compiler_params=pltpu.CompilerParams(vmem_limit_bytes=60 << 20, collective_id=0, has_side_effects=True),
        name="encoder_fwd",
    )(pix, keep, pos3, sv, *blocks)
    return out[0], out[1 : len(outs)], out[len(outs) :]


def enc_bwd_kernel(sh, dy, dsm_in, dhw, sv, awin, bwin, kept, xh1_in, xh2, xhf_in, rs1, rs2, rsf, a1_in, a2, e16_in, o, qkv, p, hid, gp,
                   dwin, dwout, eout, dsm, etail, x, t, d16, dh16, stage, xb, ab, sem, lsem, win, wout, atmp, btmp, asem, bsem):
    def fetch(i, src, dst):
        copy = pltpu.make_async_copy(src, dst, lsem.at[i])
        copy.start()
        return copy

    at_e, at_xhf = fetch(0, e16_in, ab), fetch(1, xhf_in, xb)
    enda = joiner(sh, "A", awin, win, atmp, asem)
    endb = joiner(sh, "B", bwin, wout, btmp, bsem)
    M = dy.shape[0]
    R = M // 2
    W = D
    dsm[...] = dsm_in[...]
    head = fetch(4, dhw, eout.at[pl.ds(0, 3 * DD), :])

    def save(where, sums):
        for (i, lo), v in zip(where, sums):
            dsm[:, OFF[i] + lo : OFF[i] + lo + v.shape[1]] += v

    shots = []

    def put(out, base, value):
        width = value.shape[1]
        slot = len(shots) % 2
        if len(shots) >= 2:
            shots[-2].wait()
        stage[slot, :, 0:width] = value.astype(bf)
        copy = pltpu.make_async_copy(stage.at[slot, :, pl.ds(0, width)], out.at[:, pl.ds(base, width)], sem.at[slot])
        copy.start()
        shots.append(copy)

    def emb(r):
        v = dy[r, :]
        d16[r, 0:DD] = v.astype(bf)
        return [v]
    save([(12, 0)], rows_sum(M, R, [DD], emb))
    at_e.wait()
    put(dwin, O_E, dg(ab[...], d16[:, 0:DD], 0, 0))
    at_a = fetch(2, a1_in, ab)
    enda()
    endb()
    t[...] = nt(d16[:, 0:DD], win[:, O_E:])

    at_xhf.wait()

    def lnfb(r):
        da = t[r, :]
        xh = xb[r, :]
        dx = norm_back(da, xh, rsf[r, :], part(sv, 8))
        x[r, :] = dx
        d16[r, :] = dx.astype(bf)
        return da * xh, da, dx
    save([(8, 0), (9, 0), (7, 0)], rows_sum(M, R, [W] * 3, lnfb))
    at_xh1 = fetch(3, xh1_in, xb)
    for c in range(0, FF, W):
        put(dwout, c, dg(d16[...], hid[:, c : c + W], 0, 0))
        dh = nn(d16[...], wout[:, c : c + W]) * gp[:, c : c + W].astype(f32)
        dsm[:, OFF[6] + c : OFF[6] + c + W] += rsum(dh)
        dh16[:, c : c + W] = dh.astype(bf)
        put(dwin, O_F + c, dg(a2[...], dh16[:, c : c + W], 0, 0))
    t[...] = nt(dh16[...], win[:, O_F:O_E])
    dqkv = dh16

    def ln2b(r):
        da = t[r, :]
        xh = xh2[r, :]
        dx = x[r, :] + norm_back(da, xh, rs2[r, :], part(sv, 4))
        x[r, :] = dx
        d16[r, :] = dx.astype(bf)
        return da * xh, da, dx
    save([(4, 0), (5, 0), (3, 0)], rows_sum(M, R, [W] * 3, ln2b))
    put(dwin, O_P, dg(o[...], d16[...], 0, 0))
    d16[...] = nt(d16[...], win[:, O_P:O_F]).astype(bf)

    for i in range(M // EG):
        rsl = slice(i * EG, (i + 1) * EG)
        for g in range(6):
            att_bwd(qkv, d16, p, dqkv, rsl, W, g, i * 12 + g * 2, 64)

    at_a.wait()
    for c in range(0, 3 * D, W):
        put(dwin, O_Q + c, dg(ab[...], dqkv[:, c : c + W], 0, 0))
    save([(2, 0), (2, W)], rows_sum(M, R, [W, W], lambda r: [dqkv[r, 0:W].astype(f32), dqkv[r, 2 * W : 3 * W].astype(f32)]))
    t[...] = nt(dqkv[:, 0 : 3 * W], win[:, O_Q:O_P])
    at_xh1.wait()

    def ln1b(r):
        da = t[r, :]
        xh = xb[r, :]
        dx = x[r, :] + norm_back(da, xh, rs1[r, :], part(sv, 0))
        kind = lax.rem(lax.broadcasted_iota(jnp.int32, (r.size, 1), 0), ES)
        only = jnp.where(kind < KEEP, dx, 0.0)
        d16[r, :] = only.astype(bf)
        return da * xh, da, jnp.where(kind == KEEP, dx, 0.0), only
    save([(0, 0), (1, 0), (11, 0), (10, 0)], rows_sum(M, R, [W] * 4, ln1b))
    put(dwin, 0, dg(kept[...], d16[...], 0, 0))
    etail[...] = jnp.zeros_like(etail)
    for i in range(SMALL // 256):
        etail[i : i + 1, :] = dsm[:, i * 256 : (i + 1) * 256]
    tail = fetch(5, etail, eout.at[pl.ds(3 * DD, etail.shape[0]), :])
    for c in shots[-2:] + [head, tail]:
        c.wait()


def encoder_bwd(sh, dy, dsm, dhw, sv, awin, bwin, saved):
    M = dy.shape[0]
    count = sh.nrow * sh.ncol * sh.erows
    S = jax.ShapeDtypeStruct
    V = pltpu.VMEM
    anyspec = pl.BlockSpec(memory_space=pl.ANY)
    return pl.pallas_call(
        functools.partial(enc_bwd_kernel, sh),
        in_specs=[anyspec if i in (2, 4, 5, 7, 9, 13, 15) else spec for i, spec in enumerate(vspec(6 + len(saved)))],
        out_specs=[anyspec] * 3,
        out_shape=[S((D, 5 * D + FF + DD), bf), S((D, FF), bf), S((count, 256), f32)],
        scratch_shapes=[V((1, SMALL), f32), V((count - 3 * DD, 256), f32), V((M, D), f32), V((M, D), f32), V((M, D), bf), V((M, FF), bf), V((2, D, D), bf), V((M, D), f32), V((M, D), bf),
                        pltpu.SemaphoreType.DMA((2,)), pltpu.SemaphoreType.DMA((6,))] + joiner_scratch(sh),
        compiler_params=pltpu.CompilerParams(vmem_limit_bytes=63 << 20),
        name="encoder_bwd",
    )(dy, dsm, dhw, sv, awin, bwin, *saved)


def sincos_np(width):
    quarter = width // 4
    freq = (1.0 / np.float32(10000.0) ** (np.arange(quarter, dtype=np.float32) / np.float32(quarter))).astype(np.float32)
    pos = np.arange(GRID * GRID)
    cp = (pos % GRID).astype(np.float32)[:, None] * freq[None, :]
    rp = (pos // GRID).astype(np.float32)[:, None] * freq[None, :]
    return np.concatenate([np.sin(cp), np.cos(cp), np.sin(rp), np.cos(rp)], axis=1).astype(np.float32)


def tables():
    dec = np.zeros((DS, DD), np.float32)
    dec[:PATCHES] = sincos_np(DD)
    enc = np.zeros((DS, D), np.float32)
    enc[:PATCHES] = sincos_np(D)
    b = ml_dtypes.bfloat16
    hi = enc.astype(b)
    mid = (enc - hi.astype(np.float32)).astype(b)
    lo = (enc - hi.astype(np.float32) - mid.astype(np.float32)).astype(b)
    return dec, np.concatenate([hi, mid, lo], axis=0)


def adamw(weight, first, second, grad):
    first = 0.9 * first + (1.0 - 0.9) * grad
    second = 0.999 * second + (1.0 - 0.999) * grad * grad
    first_hat = first / (1.0 - 0.9**STEP)
    second_hat = second / (1.0 - 0.999**STEP)
    weight = weight - 0.08 * (first_hat / (jnp.sqrt(second_hat) + 1e-08) + 0.05 * weight)
    return (weight, first, second)


def update_kernel(sh, ga, gb, gc, gd, eall, *refs):
    weights, firsts, seconds = refs[0:6], refs[6:12], refs[12:18]
    new, mo, vo = refs[18:24], refs[24:30], refs[30:36]
    result, e2d = refs[36], refs[37]
    er = sh.erows
    row, col = lax.axis_index("row"), lax.axis_index("col")
    squares = jnp.zeros((1, 128), f32)
    losses = jnp.zeros((1, 128), f32)
    for i in range(sh.nrow * sh.ncol):
        e2d[i * er : (i + 1) * er, :] = eall[i, 0:er, :]
        squares = squares + eall[i, er : er + 1, 0:128]
        losses = losses + eall[i, er : er + 1, 128:256]
    norm = jnp.sqrt(jnp.sum(squares, axis=1, keepdims=True))
    factor = 0.0001 / jnp.maximum(norm, 0.0001)
    result[...] = jnp.where(lax.broadcasted_iota(jnp.int32, (1, 128), 1) == 0, losses, norm)

    def aligned(g, which, index, wide, lanes):
        if wide == lanes:
            return g
        return pltpu.roll(g, lax.rem(lanes - (index * wide - sh.start(which, index)), lanes), 1)[:, 0:wide]

    def apply(i, at, grad):
        out = adamw(weights[i][at], firsts[i][at], seconds[i][at], grad * factor)
        new[i][at], mo[i][at], vo[i][at] = out

    every = (slice(None), slice(None))
    apply(0, every, aligned(ga[...], "A", col, sh.awide, sh.alanes))
    apply(1, every, aligned(gb[...], "B", row, sh.bwide, sh.blanes))
    apply(2, every, gc[...])
    apply(3, every, gd[...])
    for c in range(0, PIX, 256):
        apply(4, (slice(None), slice(c, c + 256)), e2d[2 * c : 2 * c + DD, :])
    for i in range(SMALL // 256):
        for h in (0, 1):
            apply(5, (slice(2 * i + h, 2 * i + h + 1), slice(None)), e2d[3 * DD + i : 3 * DD + i + 1, h * 128 : (h + 1) * 128])


def update(sh, grads, weights, firsts, seconds):
    S = jax.ShapeDtypeStruct
    turn = lambda t: [v.T if i % 6 in (1, 3) else v for i, v in enumerate(t)]
    flat = lambda t: turn([v.reshape(SMALL // 128, 128) if v.ndim == 1 else v for v in t])
    state = flat(weights) + flat(firsts) + flat(seconds)
    outs = pl.pallas_call(
        functools.partial(update_kernel, sh),
        in_specs=vspec(5 + 18), out_specs=vspec(19),
        out_shape=[S(v.shape, f32) for v in state] + [S((1, 128), f32)],
        scratch_shapes=[pltpu.VMEM((sh.nrow * sh.ncol * sh.erows, 256), f32)],
        compiler_params=pltpu.CompilerParams(vmem_limit_bytes=34 << 20),
        name="update",
    )(*grads, *state)
    small = lambda v: v.reshape(SMALL) if v.shape == (SMALL // 128, 128) else v
    return tuple(turn([small(v) for v in outs[:18]])) + (outs[18][0, 0], outs[18][0, 1])


def local(pixels, keep_idx, restore, *state):
    weights, firsts, seconds = state[0:6], state[6:12], state[12:18]
    nrow, ncol = lax.axis_size("row"), lax.axis_size("col")
    sh = Shapes(nrow, ncol)
    n = pixels.shape[0]
    denom = 1.0 * n * nrow * ncol * (PATCHES - KEEP)

    dec_pos, enc_pos = tables()
    fill = lambda count, value: jnp.full((n, count), value, jnp.int32)
    keep = jnp.concatenate([keep_idx, fill(ES - KEEP, NOROW)], axis=1).reshape(n, 1, ES)
    code = jnp.concatenate([jnp.where(restore < KEEP, restore, 64), fill(1, KEEP), fill(DS - PATCHES - 1, NOROW)], axis=1)
    head = weights[4]
    *blocks, sv = prepare(sh, weights[0:4], weights[5])

    y, saved, (aw, bw, c, dt) = encoder_fwd(sh, pixels, keep, jnp.asarray(enc_pos), sv, *blocks)
    dy, dc, ddt, dhead, dsm, loss = decoder(
        y.reshape(n, ES, DD), code.reshape(n, 1, DS), pixels, jnp.asarray(dec_pos), sv, c, dt, head, 1.0 / denom)
    da, dbt, shared = encoder_bwd(sh, dy.reshape(n * ES, DD), dsm, dhead, sv, aw, bw, saved)
    sums = reduce_grads(sh, REDUCED, loss, da, dbt, dc, ddt, shared.reshape(nrow * ncol, sh.erows, 256))
    return update(sh, sums, weights, firsts, seconds)


def solution(mesh):
    both = P(("row", "col"))
    big = [P("row", "col")] * 4 + [P()] * 2
    return jax.shard_map(
        local,
        mesh=mesh,
        in_specs=(both, both, both, *big, *big, *big),
        out_specs=(*big, *big, *big, P(), P()),
        check_vma=False,
    )
```
